32 devices in a mesh: dp: 8 (over z, y), row: 2 (over x), col: 2 (over core).
Axes of the slice: x: 2, y: 2, z: 4, core: 2. Of those that a mesh axis runs over, the one named last changes fastest.
Arguments:
- tokens: bfloat16 [8192, 2048], P(('dp', 'col'), 'row'), may hold values from -6 to 6
- segments: int32 [8, 1024], P('dp'), may hold values from 0 to 3, never falling along the last dimension, each value on 1 to 512 neighbouring positions
- ln1_gain: float32 [2048], P('row'), may hold values from 0.5 to 1.5
- ln1_bias: float32 [2048], P('row'), may hold values from -2 to 2
- qkv_weight: bfloat16 [2048, 3, 2048], P('row', None, 'col'), may hold values from -0.125 to 0.125
- qkv_bias: float32 [3, 2048], P(None, 'col'), may hold values from -2 to 2
- out_weight: bfloat16 [2048, 2048], P('col', 'row'), may hold values from -1.5 to 1.5
- ln2_gain: float32 [2048], P('row'), may hold values from 0.5 to 1.5
- ln2_bias: float32 [2048], P('row'), may hold values from -2 to 2
- gate_up_weight: bfloat16 [2048, 2, 5632], P('row', None, 'col'), may hold values from -0.125 to 0.125
- down_weight: bfloat16 [5632, 2048], P('col', 'row'), may hold values from -0.078125 to 0.078125
- cotangent: bfloat16 [8192, 2048], P(('dp', 'col'), 'row'), may hold values from -6 to 6
Outputs:
- result: bfloat16 [8192, 2048], P(('dp', 'col'), 'row')
- input_grad: float32 [8192, 2048], P(('dp', 'col'), 'row')
- ln1_gain_grad: float32 [2048], P('row')
- ln1_bias_grad: float32 [2048], P('row')
- qkv_weight_grad: float32 [2048, 3, 2048], P('row', None, 'col')
- qkv_bias_grad: float32 [3, 2048], P(None, 'col')
- out_weight_grad: float32 [2048, 2048], P('col', 'row')
- ln2_gain_grad: float32 [2048], P('row')
- ln2_bias_grad: float32 [2048], P('row')
- gate_up_weight_grad: float32 [2048, 2, 5632], P('row', None, 'col')
- down_weight_grad: float32 [5632, 2048], P('col', 'row')
The draws below stay inside these ranges and needn't reach their ends.
All inputs are finite; a program needn't handle non-finite values.
Results may differ from the reference program's by a relative error of at most 0.025.
Values may be sent and summed in bfloat16 or wider, within the bound.
A program may use at most 256 MiB of HBM per device.

```python
import math
import jax
import jax.numpy as jnp
import numpy as np
from jax import lax

D = 2048
HEADS = 32
HEAD = 64
ROT = 16
FF = 5632
SEQ = 1024
DOCS = 4
BATCH = 8
TOKENS = 8192


def levels(own_key, dims, split, low, largest):
    gain = 1.0
    for position, parts in split:
        draws = jax.random.uniform(jax.random.fold_in(jax.random.fold_in(own_key, 6), position), (parts,), jnp.float32, low / len(split), largest / len(split))
        gain = gain * jnp.repeat(jnp.exp(draws), dims[position] // parts).reshape((-1,) + (1,) * (len(dims) - 1 - position))
    return gain


def length_profile(number_of, total, reach, slope):
    weights = [(1 << 20) // math.isqrt(grade ** slope) + 1 for grade in range(2, number_of + 1)]
    spare, holding = total - reach - (number_of - 1), [1] * (number_of - 1)
    while spare > 0:
        free = [i for i in range(number_of - 1) if holding[i] < reach]
        mass, remaining = sum([weights[i] for i in free]), spare
        for i in free:
            more = min(reach - holding[i], max(1, remaining * weights[i] // mass), spare)
            holding[i] = holding[i] + more
            spare = spare - more
    return np.array([reach] + holding)


def ragged(key, amount, total, reach, slope):
    if amount == 2:
        one = jax.random.randint(key, (), max(1, total - reach), min(reach, total - 1) + 1)
        return jnp.stack([one, total - one])
    sizes = jnp.asarray(length_profile(amount, total, reach, slope), jnp.int32)
    twos = (amount - 1) // 2
    donor, sink = sizes[1:1 + 2 * twos:2], sizes[2:2 + 2 * twos:2]
    room = jnp.minimum(donor - 1, reach - sink)
    passed = jax.random.randint(jax.random.fold_in(key, 1), (twos,), 0, 1 << 20) % (room + 1)
    sizes = sizes.at[1:1 + 2 * twos:2].set(donor - passed).at[2:2 + 2 * twos:2].set(sink + passed)
    return sizes[jax.random.permutation(jax.random.fold_in(key, 2), amount)]


def centred(own_key, shape, deviation, most, split=(), held_as=jnp.bfloat16):
    result = jax.random.normal(own_key, shape, jnp.float32) * deviation
    if len(split) > 0:
        result = levels(own_key, shape, split, -0.22, 0.18) * result
    return jnp.clip(result, min=-most, max=most).astype(held_as)


def setup_inputs(seed: int = 0) -> dict:
    key_of = jax.random.split(jax.random.key(seed), 13)
    return {
        "tokens": centred(key_of[0], (TOKENS, D), 1.0, 6.0, ((0, 16), (1, 2))),
        "segments": jax.vmap(lambda own: jnp.searchsorted(jnp.cumsum(ragged(own, DOCS, SEQ, SEQ // 2, 0)), jnp.arange(SEQ), side="right"))(jax.random.split(key_of[1], BATCH)).reshape((BATCH, SEQ)).astype(jnp.int32),
        "ln1_gain": jnp.clip(1.0 + 0.1 * jax.random.normal(key_of[2], (D,), jnp.float32), 0.5, 1.5),
        "ln1_bias": centred(key_of[3], (D,), 0.3, 2.0, ((0, 2),), jnp.float32),
        "qkv_weight": centred(key_of[4], (D, 3, D), D ** -0.5, 0.125, ((0, 2), (2, 2))),
        "qkv_bias": centred(key_of[5], (3, D), 0.3, 2.0, ((1, 2),), jnp.float32),
        "out_weight": centred(key_of[6], (D, D), (max(D // 128, 4)) ** -0.5, 1.5, ((0, 2), (1, 2))),
        "ln2_gain": jnp.clip(1.0 + 0.1 * jax.random.normal(key_of[7], (D,), jnp.float32), 0.5, 1.5),
        "ln2_bias": centred(key_of[8], (D,), 0.3, 2.0, ((0, 2),), jnp.float32),
        "gate_up_weight": centred(key_of[9], (D, 2, FF), D ** -0.5, 0.125, ((0, 2), (2, 2))),
        "down_weight": centred(key_of[10], (FF, D), FF ** -0.5, 0.078125, ((0, 2), (1, 2))),
        "cotangent": centred(key_of[11], (TOKENS, D), 1.0, 6.0, ((0, 16), (1, 2))),
    }


EPSILON = 1e-05
ROPE_BASE = 10000.0
NEGATIVE = -1e+30
HIGHEST = lax.Precision.HIGHEST

@jax.custom_vjp
def low(v):
    return lax.optimization_barrier(v.astype(jnp.bfloat16)).astype(jnp.float32)

@jax.custom_vjp
def low_back(v):
    return v

def low_keep(v):
    return (low(v), None)

def low_pass(kept, grad):
    return (grad,)

def back_keep(v):
    return (v, None)

def back_low(kept, grad):
    return (low(grad),)
low.defvjp(low_keep, low_pass)
low_back.defvjp(back_keep, back_low)

def layer_norm(values, norm_gain, norm_shift):
    center_mean = lax.optimization_barrier(jnp.mean(values, axis=-1, keepdims=True))
    spread = lax.optimization_barrier(jnp.mean(values * values, axis=-1, keepdims=True)) - center_mean * center_mean
    return (values - center_mean) * lax.rsqrt(spread + EPSILON) * norm_gain + norm_shift

def doc_positions(segment_ids):
    places = jnp.arange(segment_ids.shape[0], dtype=jnp.int32)
    starts = jnp.concatenate([jnp.ones((1,), dtype=bool), segment_ids[1:] != segment_ids[:-1]])
    first_place = lax.cummax(jnp.where(starts, places, jnp.zeros_like(places)), axis=0)
    return places - first_place

def rotary_tables(segment_ids):
    places = doc_positions(segment_ids).astype(jnp.float32)
    freq_index = jnp.arange(ROT // 2, dtype=jnp.float32)
    inverse = jnp.exp(freq_index * (-2.0 / ROT) * math.log(ROPE_BASE))
    angles = places[:, None] * inverse[None, :]
    return (jnp.cos(angles)[:, None, :], jnp.sin(angles)[:, None, :])

def rotary(head_rows, cosines, sines):
    half_rot = ROT // 2
    first_half = head_rows[..., :half_rot]
    second_half = head_rows[..., half_rot:ROT]
    return jnp.concatenate([first_half * cosines - second_half * sines, second_half * cosines + first_half * sines, head_rows[..., ROT:]], axis=-1)

def head_attention(allowed, factor):

    def attend(pieces):
        queries, key_rows, value_rows = pieces
        scores = jnp.dot(queries, key_rows.T, precision=HIGHEST) * factor
        scores = low_back(scores)
        scores = jnp.where(allowed, scores, NEGATIVE)
        shifted = jnp.exp(scores - lax.optimization_barrier(jnp.max(scores, axis=-1, keepdims=True)))
        weights = low(shifted / lax.optimization_barrier(jnp.sum(shifted, axis=-1, keepdims=True)))
        return jnp.dot(weights, value_rows, precision=HIGHEST)
    return jax.checkpoint(attend)

def block_layer(inputs, segment_ids, norm1_gain, norm1_shift, qkv_matrix, qkv_offset, out_matrix, norm2_gain, norm2_shift, gate_matrix, down_matrix):
    length = inputs.shape[0]
    cosines, sines = rotary_tables(segment_ids)
    places = jnp.arange(length, dtype=jnp.int32)
    allowed = (segment_ids[:, None] == segment_ids[None, :]) & (places[None, :] <= places[:, None])
    act_one = low(layer_norm(inputs, norm1_gain, norm1_shift))
    joined_qkv = jnp.einsum('sd,dkh->skh', act_one, qkv_matrix, precision=HIGHEST) + qkv_offset
    joined_qkv = low_back(joined_qkv).reshape(length, 3, HEADS, HEAD)
    queries = low(rotary(joined_qkv[:, 0], cosines, sines))
    key_heads = low(rotary(joined_qkv[:, 1], cosines, sines))
    value_heads = low(joined_qkv[:, 2])
    attend = head_attention(allowed, HEAD ** (-0.5))
    mixed_heads = lax.map(attend, (queries.transpose(1, 0, 2), key_heads.transpose(1, 0, 2), value_heads.transpose(1, 0, 2)))
    attended = low_back(low(mixed_heads.transpose(1, 0, 2).reshape(length, D)))
    hidden_state = inputs + low_back(jnp.dot(attended, out_matrix, precision=HIGHEST))
    act_two = low(layer_norm(hidden_state, norm2_gain, norm2_shift))
    gate_up = low_back(jnp.einsum('sd,dkf->skf', act_two, gate_matrix, precision=HIGHEST))
    inner_act = low(jax.nn.silu(gate_up[:, 0]) * gate_up[:, 1])
    return hidden_state + low_back(jnp.dot(inner_act, down_matrix, precision=HIGHEST))

def reference(tokens, segments, ln1_gain, ln1_bias, qkv_weight, qkv_bias, out_weight, ln2_gain, ln2_bias, gate_up_weight, down_weight, cotangent):
    params = (ln1_gain.astype(jnp.float32), ln1_bias.astype(jnp.float32), qkv_weight.astype(jnp.float32), qkv_bias.astype(jnp.float32), out_weight.astype(jnp.float32), ln2_gain.astype(jnp.float32), ln2_bias.astype(jnp.float32), gate_up_weight.astype(jnp.float32), down_weight.astype(jnp.float32))
    sequences = tokens.astype(jnp.float32).reshape(BATCH, SEQ, D)
    grad_rows = cotangent.astype(jnp.float32).reshape(BATCH, SEQ, D)

    def seq_step(grad_totals, seq_item):
        inputs, segment_ids, incoming = seq_item

        def forward(values, *weight_list):
            return block_layer(values, segment_ids, *weight_list)
        output, pullback = jax.vjp(forward, inputs, *params)
        grads_back = pullback(incoming)
        grad_totals = tuple((left + right for left, right in zip(grad_totals, grads_back[1:])))
        return (grad_totals, (output.astype(jnp.bfloat16), grads_back[0]))
    zero_grads = tuple((jnp.zeros_like(item_param) for item_param in params))
    grad_totals, (outputs, input_grads) = lax.scan(seq_step, zero_grads, (sequences, segments, grad_rows))
    return (outputs.reshape(TOKENS, D), input_grads.reshape(TOKENS, D), grad_totals[0], grad_totals[1], grad_totals[2], grad_totals[3], grad_totals[4], grad_totals[5], grad_totals[6], grad_totals[7], grad_totals[8])
```

```python
import math

import jax
import jax.numpy as jnp
from jax import lax
from jax.sharding import PartitionSpec as P

HEAD = 64
ROT = 16
EPSILON = 1e-05
ROPE_BASE = 10000.0
NEGATIVE = -1e30
BF = jnp.bfloat16
F32 = jnp.float32
SWAP = [(0, 1), (1, 0)]


def swap(v, axis):
    return lax.ppermute(v, axis, SWAP)


def ordered(flag, mine, other, axis=0):
    first = jnp.where(flag == 0, mine, other)
    second = jnp.where(flag == 0, other, mine)
    return jnp.concatenate([first, second], axis=axis)


def piece(v, index, count, axis=0):
    size = v.shape[axis] // count
    return lax.dynamic_slice_in_dim(v, index * size, size, axis)


def add(a, b):
    return (a.astype(F32) + b.astype(F32)).astype(BF)


def dot(a, b):
    return jnp.dot(a, b, preferred_element_type=F32)


def dot_t(a, b):
    return lax.dot_general(a, b, (((1,), (1,)), ((), ())), preferred_element_type=F32)


def t_dot(a, b):
    return lax.dot_general(a, b, (((0,), (0,)), ((), ())), preferred_element_type=F32)


class Place:
    def __init__(self):
        self.r = lax.axis_index("row")
        self.c = lax.axis_index("col")
        self.d = lax.axis_index("dp")
        self.count = lax.axis_size("dp")
        self.y = lax.rem(self.d, 2)
        self.zp = lax.rem(self.d // 2, 2)
        self.z = self.d // 2
        self.mid = (self.z == 1) | (self.z == 2)
        self.upper = (self.z >= 2).astype(jnp.int32)


def dp_perm(bit, count):
    return [(i, i ^ bit) for i in range(count)]


def fetch(send, place, y_first):
    count = place.count
    if count % 4:
        return swap(send, "row")
    if y_first:
        index = place.zp * 2 + place.y
        steps = ((1, place.y), (2, place.zp))
    else:
        index = place.y * 2 + place.zp
        steps = ((2, place.zp), (1, place.y))
    held = swap(piece(send, index, 4), "row")
    for bit, flag in steps:
        other = lax.ppermute(held, "dp", dp_perm(bit, count))
        held = ordered(flag, held, other)
    return held


def cross(v):
    half = v.shape[-1] // 2
    return jnp.concatenate([v[..., half:], v[..., :half]], axis=-1)


def gather_blocks(block, place):
    other = cross(swap(block, "row"))
    pair = ordered(place.r, block, other)
    rest = swap(pair, "col")
    return ordered(place.c, pair, rest)


def reduce_blocks(partial, place):
    kept = piece(partial, place.c, 2)
    got = swap(piece(partial, 1 - place.c, 2), "col")
    held = add(kept, got)
    kept = piece(held, place.r, 2)
    got = cross(swap(piece(held, 1 - place.r, 2), "row"))
    return kept.astype(F32) + got.astype(F32)


def norm_forward(values, gain, shift):
    count = values.shape[-1]
    mean = jnp.sum(values, axis=-1, keepdims=True) / count
    spread = jnp.sum(values * values, axis=-1, keepdims=True) / count - mean * mean
    inverse = lax.rsqrt(spread + EPSILON)
    normal = (values - mean) * inverse
    return normal * gain + shift, normal, inverse


def norm_backward(grad, normal, inverse, gain):
    count = grad.shape[-1]
    scaled = grad * gain
    first = jnp.sum(scaled, axis=-1, keepdims=True) / count
    second = jnp.sum(scaled * normal, axis=-1, keepdims=True) / count
    grad_input = inverse * (scaled - first - normal * second)
    return grad_input, jnp.sum(grad * normal, axis=0), jnp.sum(grad, axis=0)


def doc_positions(segment_ids):
    places = jnp.arange(segment_ids.shape[0], dtype=jnp.int32)
    starts = jnp.concatenate([jnp.ones((1,), dtype=bool), segment_ids[1:] != segment_ids[:-1]])
    first_place = lax.cummax(jnp.where(starts, places, jnp.zeros_like(places)), axis=0)
    return places - first_place


def rotary_tables(segment_ids):
    places = doc_positions(segment_ids).astype(F32)
    freq_index = jnp.arange(ROT // 2, dtype=F32)
    inverse = jnp.exp(freq_index * (-2.0 / ROT) * math.log(ROPE_BASE))
    angles = places[:, None] * inverse[None, :]
    return (jnp.cos(angles)[:, None, :], jnp.sin(angles)[:, None, :])


def rotary(head_rows, cosines, sines):
    half_rot = ROT // 2
    first_half = head_rows[..., :half_rot]
    second_half = head_rows[..., half_rot:ROT]
    return jnp.concatenate(
        [
            first_half * cosines - second_half * sines,
            second_half * cosines + first_half * sines,
            head_rows[..., ROT:],
        ],
        axis=-1,
    )


def score_block(query_rows, key_rows, query_ids, key_ids, begin_row, factor):
    scores = (
        jnp.einsum("qhd,khd->hqk", query_rows, key_rows, preferred_element_type=F32) * factor
    )
    query_places = begin_row + jnp.arange(query_rows.shape[0], dtype=jnp.int32)
    key_places = jnp.arange(key_rows.shape[0], dtype=jnp.int32)
    allowed = (query_ids[:, None] == key_ids[None, :]) & (
        key_places[None, :] <= query_places[:, None]
    )
    return jnp.where(allowed[None], scores, NEGATIVE)


def attention_forward(queries, keys, values, ids, factor):
    length = ids.shape[0]
    rows = min(512, length)
    outs, logs = [], []
    for begin in range(0, length, rows):
        end = begin + rows
        scores = score_block(queries[begin:end], keys[:end], ids[begin:end], ids[:end], begin, factor)
        maxima = jnp.max(scores, axis=-1, keepdims=True)
        shifted = jnp.exp(scores - maxima)
        totals = jnp.sum(shifted, axis=-1, keepdims=True)
        weights = (shifted / totals).astype(BF)
        outs.append(
            jnp.einsum("hqk,khd->qhd", weights, values[:end], preferred_element_type=F32)
        )
        logs.append(maxima + jnp.log(totals))
    return jnp.concatenate(outs, axis=0).astype(BF), logs


def attention_backward(queries, keys, values, grads, logs, ids, factor):
    length = ids.shape[0]
    rows = min(512, length)
    grad_queries = []
    grad_keys = jnp.zeros(keys.shape, F32)
    grad_values = jnp.zeros(values.shape, F32)
    for index, begin in enumerate(range(0, length, rows)):
        end = begin + rows
        scores = score_block(queries[begin:end], keys[:end], ids[begin:end], ids[:end], begin, factor)
        weights = jnp.exp(scores - logs[index])
        block = grads[begin:end]
        grad_values = grad_values.at[:end].add(
            jnp.einsum("hqk,qhd->khd", weights.astype(BF), block, preferred_element_type=F32)
        )
        grad_weights = jnp.einsum("qhd,khd->hqk", block, values[:end], preferred_element_type=F32)
        grad_scores = (
            weights * (grad_weights - jnp.sum(weights * grad_weights, axis=-1, keepdims=True))
        ).astype(BF)
        grad_queries.append(
            jnp.einsum("hqk,khd->qhd", grad_scores, keys[:end], preferred_element_type=F32) * factor
        )
        grad_keys = grad_keys.at[:end].add(
            jnp.einsum("hqk,qhd->khd", grad_scores, queries[begin:end], preferred_element_type=F32)
            * factor
        )
    return jnp.concatenate(grad_queries, axis=0), grad_keys, grad_values


class Reducer:
    def __init__(self, place):
        self.place = place
        both = [(2 * i, 2 * i + 1) for i in range(8)]
        middle = [(2, 4), (4, 2), (3, 5), (5, 3)]
        outer = [pair for i in (0, 1, 6, 7) for pair in (both[i], both[i][::-1])]
        self.middle = outer + [(2 * i + k, 2 * j + k) for i, j in middle for k in (0, 1)]
        self.middle_y = outer + [
            (2 * i + k, 2 * (i ^ 1) + k) for i in (2, 3, 4, 5) for k in (0, 1)
        ]
        self.inward = [(0, 2), (1, 3), (6, 4), (7, 5)]
        self.outward = [(j, i) for i, j in self.inward]

    def along_y(self, v):
        return lax.ppermute(v, "dp", dp_perm(1, 8))

    def centre(self, v):
        return lax.ppermute(v, ("dp", "col"), self.middle)

    def centre_y(self, v):
        return lax.ppermute(v, ("dp", "col"), self.middle_y)

    def edge(self, inward, outward):
        mid = self.place.mid
        if outward is None:
            return lax.ppermute(inward, "dp", self.inward)
        if inward is None:
            return lax.ppermute(outward, "dp", self.outward)
        return lax.ppermute(jnp.where(mid, outward, inward), "dp", dp_perm(2, 8))

    def line(self, raws, centre):
        count = len(raws)
        totals, outs = [None] * count, [None] * count
        for step in range(count + 2):
            raw = raws[step] if step < count else None
            done = totals[step - 2] if step >= 2 else None
            got = self.edge(raw, done)
            if raw is not None:
                totals[step] = centre(add(raw, got))
            if done is not None:
                outs[step - 2] = jnp.where(self.place.mid, done, got)
        return outs

    def wide(self, chunks):
        y = self.place.y

        def centre(v):
            return add(v, self.centre(v))

        raws = [add(piece(v, y, 2), self.along_y(piece(v, 1 - y, 2))) for v in chunks]
        outs = self.line(raws, centre)
        return [ordered(y, v, self.along_y(v)) for v in outs]

    def deep(self, chunks):
        upper = self.place.upper

        def centre(v):
            held = add(piece(v, upper, 2), self.centre(piece(v, 1 - upper, 2)))
            held = add(held, self.centre_y(held))
            return ordered(upper, held, self.centre(held))

        return self.line(list(chunks), centre)


def reduce_dp(place, arrays, kind, parts):
    if place.count != 8:
        return [lax.psum(v, "dp") for v in arrays]
    reducer = Reducer(place)
    chunks = [v for a in arrays for v in jnp.split(a, parts)]
    outs = getattr(reducer, kind)(chunks)
    return [jnp.concatenate(outs[i * parts : (i + 1) * parts]) for i in range(len(arrays))]


def local(
    tokens,
    segments,
    ln1_gain,
    ln1_bias,
    qkv_weight,
    qkv_bias,
    out_weight,
    ln2_gain,
    ln2_bias,
    gate_up_weight,
    down_weight,
    cotangent,
):
    place = Place()
    r, c = place.r, place.c
    ids = segments[0]
    length = ids.shape[0]
    factor = HEAD ** (-0.5)
    half = qkv_weight.shape[0]
    units = qkv_weight.shape[2] // 2
    heads = units // HEAD
    hidden = gate_up_weight.shape[2] // 2

    qkv_flat = [qkv_weight[:, k] for k in range(3)]
    qkv_own = jnp.concatenate([piece(w, r, 2, 1) for w in qkv_flat], axis=1)
    qkv_send = jnp.concatenate([piece(w, 1 - r, 2, 1) for w in qkv_flat], axis=1)
    w_qkv = jnp.concatenate([qkv_own, fetch(qkv_send, place, False)], axis=0)

    other = swap(tokens, "row")
    mine = jnp.concatenate([tokens, other], axis=1)
    tokens_all = ordered(c, mine, swap(mine, "col"))
    params = jnp.stack([ln1_gain, ln1_bias, ln2_gain, ln2_bias])
    params = jnp.concatenate([params, swap(params, "row")], axis=1)

    w_out = jnp.concatenate(
        [piece(out_weight, r, 2), fetch(piece(out_weight, 1 - r, 2), place, True)], axis=1
    )
    gate_flat = [gate_up_weight[:, k] for k in range(2)]
    gate_own = jnp.concatenate([piece(w, r, 2, 1) for w in gate_flat], axis=1)
    gate_send = jnp.concatenate([piece(w, 1 - r, 2, 1) for w in gate_flat], axis=1)
    w_gate = jnp.concatenate([gate_own, fetch(gate_send, place, True)], axis=0)
    cot_other = swap(cotangent, "row")
    cot_mine = jnp.concatenate([cotangent, cot_other], axis=1)
    cot_all = ordered(c, cot_mine, swap(cot_mine, "col"))
    w_down = jnp.concatenate(
        [piece(down_weight, r, 2), fetch(piece(down_weight, 1 - r, 2), place, False)], axis=1
    )

    cosines, sines = rotary_tables(ids)
    inputs = tokens_all.astype(F32)
    normed, _, _ = norm_forward(inputs, params[0], params[1])
    act_one = normed.astype(BF)
    joined = dot(act_one, w_qkv).reshape(length, 3, heads, HEAD)
    joined = joined + piece(qkv_bias, r, 2, 1).reshape(3, heads, HEAD)
    queries = rotary(joined[:, 0], cosines, sines).astype(BF)
    keys = rotary(joined[:, 1], cosines, sines).astype(BF)
    values = joined[:, 2].astype(BF)
    attended, logs = attention_forward(queries, keys, values, ids, factor)
    attended = attended.reshape(length, units)
    block = c * 2 + r
    own_inputs = piece(tokens_all, block, 4).astype(F32)
    branch = reduce_blocks(dot(attended, w_out).astype(BF), place)
    hidden_state = own_inputs + branch
    normed, normal_two, inverse_two = norm_forward(hidden_state, params[2], params[3])
    act_two = gather_blocks(normed.astype(BF), place)
    gate_up = dot(act_two, w_gate)
    gate, up = gate_up[:, :hidden], gate_up[:, hidden:]
    inner = (jax.nn.silu(gate) * up).astype(BF)

    def exchanged(own, other):
        return own, swap(other, "row")

    down_grads = exchanged(
        t_dot(inner, cot_all[:, :half]).astype(BF), t_dot(inner, cot_all[:, half:]).astype(BF)
    )
    feed = reduce_blocks(dot(inner, w_down).astype(BF), place)
    result = (hidden_state + feed).astype(BF)
    result = ordered(r, result[:, :half], swap(result[:, half:], "row"))

    grad_inner = dot_t(cot_all, w_down)
    rate = 1.0 / (1.0 + jnp.exp(-gate))
    silu = gate * rate
    grad_gate = (grad_inner * up * (rate * (1.0 + gate * (1.0 - rate)))).astype(BF)
    grad_up = (grad_inner * silu).astype(BF)
    grad_pair = jnp.concatenate([grad_gate, grad_up], axis=1)
    grad_act_two = reduce_blocks(dot_t(grad_pair, w_gate).astype(BF), place)
    gate_grads = [
        exchanged(t_dot(act_two[:, :half], g).astype(BF), t_dot(act_two[:, half:], g).astype(BF))
        for g in (grad_gate, grad_up)
    ]
    grad_norm, ln2_gain_grad, ln2_bias_grad = norm_backward(
        grad_act_two, normal_two, inverse_two, params[2]
    )
    own_cot = piece(cot_all, block, 4).astype(F32)
    grad_hidden = own_cot + grad_norm
    grad_branch = gather_blocks(grad_hidden.astype(BF), place)
    grad_attended = dot_t(grad_branch, w_out).astype(BF).reshape(length, heads, HEAD)
    out_grads = exchanged(
        t_dot(attended, grad_branch[:, :half]).astype(BF),
        t_dot(attended, grad_branch[:, half:]).astype(BF),
    )
    grad_queries, grad_keys, grad_values = attention_backward(
        queries, keys, values, grad_attended, logs, ids, factor
    )
    grad_joined = jnp.stack(
        [rotary(grad_queries, cosines, -sines), rotary(grad_keys, cosines, -sines), grad_values],
        axis=1,
    )
    grad_joined = grad_joined.reshape(length, 3 * units).astype(BF)
    qkv_grads = exchanged(
        t_dot(act_one[:, :half], grad_joined).astype(BF),
        t_dot(act_one[:, half:], grad_joined).astype(BF),
    )
    bias_grad = jnp.sum(grad_joined, axis=0, dtype=F32)
    grad_act_one = reduce_blocks(dot_t(grad_joined, w_qkv).astype(BF), place)
    _, normal_one, inverse_one = norm_forward(own_inputs, params[0], params[1])
    grad_norm, ln1_gain_grad, ln1_bias_grad = norm_backward(
        grad_act_one, normal_one, inverse_one, params[0]
    )
    input_grad = grad_hidden + grad_norm
    input_grad = ordered(r, input_grad[:, :half], swap(input_grad[:, half:], "row"))

    small = jnp.stack([ln1_gain_grad, ln1_bias_grad, ln2_gain_grad, ln2_bias_grad])
    small = small[:, :half] + swap(small[:, half:], "row")
    small = small + swap(small, "col")
    bias_grad = bias_grad.reshape(3, units)
    small = jnp.concatenate([small.reshape(-1), bias_grad.reshape(-1)])
    if place.count == 8:
        for bit in (1, 2, 4):
            small = small + lax.ppermute(small, "dp", dp_perm(bit, 8))
    else:
        small = lax.psum(small, "dp")
    norms = small[: 4 * half].reshape(4, half)
    bias_grad = small[4 * half :].reshape(3, units)
    bias_grad = ordered(r, bias_grad, swap(bias_grad, "row"), 1)

    down_own, down_got = reduce_dp(place, down_grads, "deep", 4)
    gate_own, gate_got, up_own, up_got = reduce_dp(
        place, gate_grads[0] + gate_grads[1], "wide", 2
    )
    out_own, out_got = reduce_dp(place, out_grads, "deep", 2)
    qkv_own, qkv_got = reduce_dp(place, qkv_grads, "deep", 4)

    down_grad = ordered(r, down_own, down_got).astype(F32)
    out_grad = ordered(r, out_own, out_got).astype(F32)
    gate_up_grad = jnp.stack(
        [ordered(r, gate_own, gate_got, 1), ordered(r, up_own, up_got, 1)], axis=1
    ).astype(F32)
    qkv_grad = jnp.concatenate(
        [
            ordered(r, qkv_own.reshape(half, 3, units), qkv_got.reshape(half, 3, units), 2),
        ],
        axis=2,
    ).astype(F32)
    return (
        result,
        input_grad,
        norms[0],
        norms[1],
        qkv_grad,
        bias_grad,
        out_grad,
        norms[2],
        norms[3],
        gate_up_grad,
        down_grad,
    )


def solution(mesh):
    in_specs = (
        P(("dp", "col"), "row"),
        P("dp", None),
        P("row"),
        P("row"),
        P("row", None, "col"),
        P(None, "col"),
        P("col", "row"),
        P("row"),
        P("row"),
        P("row", None, "col"),
        P("col", "row"),
        P(("dp", "col"), "row"),
    )
    out_specs = (
        P(("dp", "col"), "row"),
        P(("dp", "col"), "row"),
        P("row"),
        P("row"),
        P("row", None, "col"),
        P(None, "col"),
        P("col", "row"),
        P("row"),
        P("row"),
        P("row", None, "col"),
        P("col", "row"),
    )
    return jax.shard_map(local, mesh=mesh, in_specs=in_specs, out_specs=out_specs, check_vma=False)
```

```python
import functools
import math

import jax
import jax.numpy as jnp
from jax import lax
from jax.experimental import pallas as pl
from jax.experimental.pallas import tpu as pltpu
from jax.sharding import PartitionSpec as P

HEAD = 64
ROT = 16
EPSILON = 1e-05
ROPE_BASE = 10000.0
NEGATIVE = -1e30
BF = jnp.bfloat16
F32 = jnp.float32
SWAP = [(0, 1), (1, 0)]


def swap(v, axis):
    return lax.ppermute(v, axis, SWAP)


def ordered(flag, mine, other, axis=0):
    first = jnp.where(flag == 0, mine, other)
    second = jnp.where(flag == 0, other, mine)
    return jnp.concatenate([first, second], axis=axis)


def piece(v, index, count, axis=0):
    size = v.shape[axis] // count
    return lax.dynamic_slice_in_dim(v, index * size, size, axis)


def add(a, b):
    return (a.astype(F32) + b.astype(F32)).astype(BF)


def dot(a, b):
    return jnp.dot(a, b, preferred_element_type=F32)


def dot_t(a, b):
    return lax.dot_general(a, b, (((1,), (1,)), ((), ())), preferred_element_type=F32)


def t_dot(a, b):
    return lax.dot_general(a, b, (((0,), (0,)), ((), ())), preferred_element_type=F32)


class Place:
    def __init__(self):
        self.r = lax.axis_index("row")
        self.c = lax.axis_index("col")
        self.d = lax.axis_index("dp")
        self.count = lax.axis_size("dp")
        self.y = lax.rem(self.d, 2)
        self.zp = lax.rem(self.d // 2, 2)
        self.z = self.d // 2
        self.mid = (self.z == 1) | (self.z == 2)
        self.upper = (self.z >= 2).astype(jnp.int32)


def dp_perm(bit, count):
    return [(i, i ^ bit) for i in range(count)]


def fetch(send, place, y_first):
    count = place.count
    if count % 4:
        return swap(send, "row")
    if y_first:
        index = place.zp * 2 + place.y
        steps = ((1, place.y), (2, place.zp))
    else:
        index = place.y * 2 + place.zp
        steps = ((2, place.zp), (1, place.y))
    held = swap(piece(send, index, 4), "row")
    for bit, flag in steps:
        other = lax.ppermute(held, "dp", dp_perm(bit, count))
        held = ordered(flag, held, other)
    return held


def cross(v):
    half = v.shape[-1] // 2
    return jnp.concatenate([v[..., half:], v[..., :half]], axis=-1)


def gather_blocks(block, place):
    other = cross(swap(block, "row"))
    pair = ordered(place.r, block, other)
    rest = swap(pair, "col")
    return ordered(place.c, pair, rest)


def reduce_blocks(partial, place):
    kept = piece(partial, place.c, 2)
    got = swap(piece(partial, 1 - place.c, 2), "col")
    held = add(kept, got)
    kept = piece(held, place.r, 2)
    got = cross(swap(piece(held, 1 - place.r, 2), "row"))
    return kept.astype(F32) + got.astype(F32)


def norm_forward(values, gain, shift):
    count = values.shape[-1]
    mean = jnp.sum(values, axis=-1, keepdims=True) / count
    spread = jnp.sum(values * values, axis=-1, keepdims=True) / count - mean * mean
    inverse = lax.rsqrt(spread + EPSILON)
    normal = (values - mean) * inverse
    return normal * gain + shift, normal, inverse


def norm_backward(grad, normal, inverse, gain):
    count = grad.shape[-1]
    scaled = grad * gain
    first = jnp.sum(scaled, axis=-1, keepdims=True) / count
    second = jnp.sum(scaled * normal, axis=-1, keepdims=True) / count
    grad_input = inverse * (scaled - first - normal * second)
    return grad_input, jnp.sum(grad * normal, axis=0), jnp.sum(grad, axis=0)


def doc_positions(segment_ids):
    places = jnp.arange(segment_ids.shape[0], dtype=jnp.int32)
    starts = jnp.concatenate([jnp.ones((1,), dtype=bool), segment_ids[1:] != segment_ids[:-1]])
    first_place = lax.cummax(jnp.where(starts, places, jnp.zeros_like(places)), axis=0)
    return places - first_place


def rotary_tables(segment_ids):
    places = doc_positions(segment_ids).astype(F32)
    freq_index = jnp.arange(ROT // 2, dtype=F32)
    inverse = jnp.exp(freq_index * (-2.0 / ROT) * math.log(ROPE_BASE))
    angles = places[:, None] * inverse[None, :]
    return (jnp.cos(angles), jnp.sin(angles))


LONGEST = 512
QB = 256

def windows(length):
    for begin in range(0, length, QB):
        low = max(0, (begin - LONGEST + 1) // QB * QB)
        yield begin, low, begin + QB


def barred(starts, begin, low, end):
    shape = (end - begin, end - low)
    query = begin + lax.broadcasted_iota(jnp.int32, shape, 0)
    key = low + lax.broadcasted_iota(jnp.int32, shape, 1)
    return jnp.where((key <= query) & (key >= starts), 0.0, NEGATIVE)


def turned(v, table):
    width = v.shape[-1]
    return v * table[0] + pltpu.roll(v, width - 8, 1) * table[1] + pltpu.roll(v, 8, 1) * table[2]


def nt(a, b):
    return lax.dot_general(a, b, (((1,), (1,)), ((), ())), preferred_element_type=F32)


def tn(a, b):
    return lax.dot_general(a, b, (((0,), (0,)), ((), ())), preferred_element_type=F32)


def forward_kernel(q_in, k_in, v_in, bias_ref, starts_ref, table_ref, q_ref, k_ref, v_ref, out_ref, raw_ref, log_ref):
    length = q_in.shape[0]
    table = (table_ref[0], table_ref[1], table_ref[2])
    q_ref[...] = (turned(q_in[...] + bias_ref[0, 0:1], table).astype(BF).astype(F32) * HEAD ** (-0.5)).astype(BF)
    k_ref[...] = turned(k_in[...] + bias_ref[0, 1:2], table).astype(BF)
    v_ref[...] = (v_in[...] + bias_ref[0, 2:3]).astype(BF)
    for begin, low, end in windows(length):
        bar = barred(starts_ref[begin:end], begin, low, end)
        outs = []
        for h in range(2):
            lanes = slice(h * HEAD, (h + 1) * HEAD)
            scores = nt(q_ref[begin:end, lanes], k_ref[low:end, lanes]) + bar
            maxima = jnp.max(scores, axis=1, keepdims=True)
            shifted = jnp.exp(scores - maxima).astype(BF)
            wide = jnp.concatenate([v_ref[low:end, lanes], jnp.ones((end - low, HEAD), BF)], axis=1)
            got = jnp.dot(shifted, wide, preferred_element_type=F32)
            totals = got[:, HEAD : HEAD + 1]
            outs.append(got[:, :HEAD] / totals)
            log_ref[0, begin:end, h : h + 1] = maxima + jnp.log(totals)
        out = jnp.concatenate(outs, axis=1)
        raw_ref[begin:end] = out
        out_ref[begin:end] = out.astype(BF)


def backward_kernel(q_ref, k_ref, v_ref, g_ref, raw_ref, log_ref, starts_ref, table_ref, dq_ref, dk_ref, dv_ref, dk_acc, dv_acc):
    length = q_ref.shape[0]
    dk_acc[...] = jnp.zeros_like(dk_acc)
    dv_acc[...] = jnp.zeros_like(dv_acc)
    for begin, low, end in windows(length):
        bar = barred(starts_ref[begin:end], begin, low, end)
        outs, dks, dvs = [], [], []
        for h in range(2):
            lanes = slice(h * HEAD, (h + 1) * HEAD)
            q, k, v, g = q_ref[begin:end, lanes], k_ref[low:end, lanes], v_ref[low:end, lanes], g_ref[begin:end, lanes]
            weights = jnp.exp(nt(q, k) + bar - log_ref[0, begin:end, h : h + 1])
            dvs.append(tn(weights.astype(BF), g))
            inner = jnp.sum(g.astype(F32) * raw_ref[begin:end, lanes], axis=1, keepdims=True)
            grads = (weights * (nt(g, v) - inner)).astype(BF)
            outs.append(jnp.dot(grads, k, preferred_element_type=F32))
            dks.append(tn(grads, q))
        table = (table_ref[0, begin:end], -table_ref[1, begin:end], -table_ref[2, begin:end])
        dq_ref[begin:end] = turned(jnp.concatenate(outs, axis=1) * HEAD ** (-0.5), table).astype(BF)
        dk_acc[low:end] += jnp.concatenate(dks, axis=1)
        dv_acc[low:end] += jnp.concatenate(dvs, axis=1)
    table = (table_ref[0], -table_ref[1], -table_ref[2])
    dk_ref[...] = turned(dk_acc[...], table).astype(BF)
    dv_ref[...] = dv_acc[...].astype(BF)


def tables(cosines, sines):
    length = cosines.shape[0]
    ones = jnp.ones((length, HEAD - 16), F32)
    none = jnp.zeros((length, HEAD - 8), F32)
    one = jnp.concatenate([cosines, cosines, ones], axis=1)
    ahead = jnp.concatenate([-sines, none], axis=1)
    behind = jnp.concatenate([none[:, :8], sines, none[:, 8:]], axis=1)
    return jnp.stack([jnp.concatenate([v, v], axis=1) for v in (one, ahead, behind)])


def attention_forward(joined, bias, starts, table):
    length, pairs = joined.shape[0], bias.shape[0]
    units = pairs * 128
    part = lambda n: pl.BlockSpec((length, 128), lambda p, n=n: (0, n * pairs + p))
    same = pl.BlockSpec((length, 128), lambda p: (0, p))
    half = jax.ShapeDtypeStruct((length, units), BF)
    return pl.pallas_call(
        forward_kernel,
        grid=(pairs,),
        in_specs=[
            part(0), part(1), part(2),
            pl.BlockSpec((1, 3, 128), lambda p: (p, 0, 0)),
            pl.BlockSpec((length, 1), lambda p: (0, 0)),
            pl.BlockSpec((3, length, 128), lambda p: (0, 0, 0)),
        ],
        out_specs=[same] * 5 + [pl.BlockSpec((1, length, 2), lambda p: (p, 0, 0))],
        out_shape=[half] * 4 + [jax.ShapeDtypeStruct((length, units), F32), jax.ShapeDtypeStruct((pairs, length, 2), F32)],
        compiler_params=pltpu.CompilerParams(vmem_limit_bytes=48 * 2**20),
        cost_estimate=pl.CostEstimate(flops=pairs * 2 * length * 640 * 256, bytes_accessed=12 * 2**20, transcendentals=pairs * 2 * length * 640),
    )(joined, joined, joined, bias, starts, table)


def attention_backward(queries, keys, values, grads, raw, logs, starts, table):
    length, units = queries.shape
    pairs = units // 128
    same = pl.BlockSpec((length, 128), lambda p: (0, p))
    half = jax.ShapeDtypeStruct((length, units), BF)
    return pl.pallas_call(
        backward_kernel,
        grid=(pairs,),
        in_specs=[same] * 5
        + [
            pl.BlockSpec((1, length, 2), lambda p: (p, 0, 0)),
            pl.BlockSpec((length, 1), lambda p: (0, 0)),
            pl.BlockSpec((3, length, 128), lambda p: (0, 0, 0)),
        ],
        out_specs=[same] * 3,
        out_shape=[half] * 3,
        scratch_shapes=[pltpu.VMEM((length, 128), F32)] * 2,
        compiler_params=pltpu.CompilerParams(vmem_limit_bytes=48 * 2**20),
        cost_estimate=pl.CostEstimate(flops=pairs * 2 * length * 640 * 640, bytes_accessed=8 * 2**20, transcendentals=pairs * 2 * length * 640),
    )(queries, keys, values, grads, raw, logs, starts, table)


MESH = pl.DeviceIdType.MESH

BR = 512
BC = 256
SLOTS = 6


def gradient_kernel(segments, half, *refs):
    count = len(segments)
    total = sum(s[1] for s in segments)
    sources = refs[: 2 * count]
    out_ref = refs[2 * count]
    out_own, out_got = out_ref.at[0], out_ref.at[1]
    rest = refs[2 * count + 1 :]
    held = rest[: 2 * count]
    (
        load_sem,
        turn,
        part,
        x_src,
        x_dst,
        y_dst,
        acc,
        e_dst,
        low,
        m_dst,
        full,
        f_dst,
        deep,
        n_dst,
        key,
        k_dst,
        whole,
    ) = rest[2 * count : 2 * count + 17]
    sems = rest[2 * count + 17 :]
    names = ("x", "y", "ei", "eo", "m", "g", "fi", "fo", "n", "k", "w")
    send = {k: sems[i] for i, k in enumerate(names)}
    recv = {k: sems[len(names) + i] for i, k in enumerate(names)}
    store_own, store_got = sems[2 * len(names)], sems[2 * len(names) + 1]

    d, r = lax.axis_index("dp"), lax.axis_index("row")
    y, z = lax.rem(d, 2), d // 2
    upper = d // 4
    mid = (z == 1) | (z == 2)
    outer = (z == 0) | (z == 3)
    x_peer = {"row": 1 - r}
    y_peer = {"dp": d + 1 - 2 * y}
    e_peer = {"dp": d + 2 - 4 * lax.rem(z, 2)}
    m_peer = {"dp": d + 2 - 4 * upper}

    loads = []
    for i in range(2 * count):
        loads.append(pltpu.make_async_copy(sources[i], held[i], load_sem.at[i]))
        loads[-1].start()

    barrier = pltpu.get_barrier_semaphore()
    for peer in (x_peer, y_peer, e_peer):
        pl.semaphore_signal(barrier, inc=1, device_id=peer, device_id_type=MESH)

    @pl.when(mid)
    def _():
        pl.semaphore_signal(barrier, inc=1, device_id=m_peer, device_id_type=MESH)
        pl.semaphore_wait(barrier, 4)

    @pl.when(outer)
    def _():
        pl.semaphore_wait(barrier, 3)

    rows = BR // 2

    def halves(index):
        return pl.ds(pl.multiple_of(index * rows, rows), rows)

    def copy(name, u, src, dst, peer):
        s = lax.rem(u, SLOTS)
        return pltpu.make_async_remote_copy(
            src_ref=src, dst_ref=dst, send_sem=send[name].at[s], recv_sem=recv[name].at[s], device_id=peer, device_id_type=MESH
        )

    def slot(u):
        return lax.rem(u, SLOTS)

    def out_half(ref, u, index):
        return ref.at[u, halves(index)]

    def x_copy(u):
        return copy("x", u, x_src.at[slot(u)], x_dst.at[slot(u)], x_peer)

    def y_copy(u):
        return copy("y", u, part.at[slot(u), halves(1 - y)], y_dst.at[slot(u)], y_peer)

    def e_in(u):
        return copy("ei", u, acc.at[slot(u)], e_dst.at[slot(u)], e_peer)

    def e_out(u):
        return copy("eo", u, full.at[slot(u)], e_dst.at[slot(u)], e_peer)

    def m_copy(u):
        return copy("m", u, low.at[slot(u)], m_dst.at[slot(u)], m_peer)

    def g_mid(u):
        return copy("g", u, full.at[slot(u)], out_half(out_own, u, y), y_peer)

    def g_out(u):
        return copy("g", u, e_dst.at[slot(u)], out_half(out_own, u, y), y_peer)

    def f_in(u):
        return copy("fi", u, x_dst.at[slot(u)], f_dst.at[slot(u)], e_peer)

    def f_out(u):
        return copy("fo", u, whole.at[slot(u)], out_got.at[u], e_peer)

    def n_copy(u):
        return copy("n", u, deep.at[slot(u), halves(1 - upper)], n_dst.at[slot(u)], m_peer)

    def k_copy(u):
        return copy("k", u, key.at[slot(u)], k_dst.at[slot(u)], y_peer)

    def w_copy(u):
        place = whole.at[slot(u), halves(upper)]
        return copy("w", u, place, place, m_peer)

    def keep_own(u, src):
        return pltpu.make_async_copy(src, out_half(out_own, u, y), store_own.at[slot(u)])

    def keep_got(u):
        return pltpu.make_async_copy(whole.at[slot(u)], out_got.at[u], store_got.at[slot(u)])

    def stage(u, fn, role=None):
        ok = (u >= 0) & (u < total)
        if role is not None:
            ok = ok & role

        @pl.when(ok)
        def _():
            fn(u)

    def produce(u):
        s = slot(u)
        first = 0
        for i, (kind, blocks) in enumerate(segments):
            lhs, rhs = held[2 * i], held[2 * i + 1]

            @pl.when(u == first)
            def _(i=i):
                loads[2 * i].wait()
                loads[2 * i + 1].wait()

            @pl.when((u >= first) & (u < first + blocks))
            def _(kind=kind, first=first, lhs=lhs, rhs=rhs):
                k = u - first
                if kind == "D":
                    columns = rhs.shape[1] // BC

                    @pl.when(lax.rem(k, columns) == 0)
                    def _():
                        for side in range(2):
                            at = pl.multiple_of(side * half + k // columns * BR, BR)
                            turn[side] = lhs[:, pl.ds(at, BR)].T

                    right = rhs[:, pl.ds(pl.multiple_of(lax.rem(k, columns) * BC, BC), BC)]
                    for side, ref in ((1, x_src), (0, part)):
                        ref[s] = jnp.dot(turn[side], right, preferred_element_type=F32).astype(BF)
                else:
                    size = BR * BC // half
                    left = lhs[:, pl.ds(pl.multiple_of(k * size, size), size)].T
                    for side, ref in ((1, x_src), (0, part)):
                        for q in range(half // BC):
                            right = rhs[:, side * half + q * BC : side * half + (q + 1) * BC]
                            ref[s, q * size : (q + 1) * size] = jnp.dot(
                                left, right, preferred_element_type=F32
                            ).astype(BF)

            first += blocks
        x_copy(u).start()
        y_copy(u).start()

    def t1_a(u):
        s = slot(u)
        y_copy(u).wait_recv()
        acc[s] = part[s, halves(y)] + y_dst[s]
        pl.when(outer)(lambda: e_in(u).start())

    def t1_b(u):
        s = slot(u)
        e_in(u).wait_recv()
        low[s] = acc[s] + e_dst[s]
        m_copy(u).start()

    def t1_c(u):
        s = slot(u)
        m_copy(u).wait_recv()
        full[s] = low[s] + m_dst[s]
        e_out(u).start()
        g_mid(u).start()
        keep_own(u, full.at[s]).start()

    def t1_d(u):
        e_out(u).wait_recv()
        g_out(u).start()
        keep_own(u, e_dst.at[slot(u)]).start()

    def t2_a(u):
        x_copy(u).wait_recv()
        pl.when(outer)(lambda: f_in(u).start())

    def t2_b(u):
        s = slot(u)
        f_in(u).wait_recv()
        deep[s] = x_dst[s] + f_dst[s]
        n_copy(u).start()

    def t2_c(u):
        s = slot(u)
        n_copy(u).wait_recv()
        key[s] = deep[s, halves(upper)] + n_dst[s]
        k_copy(u).start()

    def t2_d(u):
        s = slot(u)
        k_copy(u).wait_recv()
        whole[s, halves(upper)] = key[s] + k_dst[s]
        w_copy(u).start()

    def t2_e(u):
        w_copy(u).wait_recv()
        f_out(u).start()
        keep_got(u).start()

    def body(t, carry):
        stage(t - 2, lambda u: (x_copy(u).wait_send(), y_copy(u).wait_send()))
        stage(t - 3, lambda u: e_in(u).wait_send(), outer)
        stage(t - 3, lambda u: f_in(u).wait_send(), outer)
        stage(t - 4, lambda u: (m_copy(u).wait_send(), n_copy(u).wait_send()), mid)
        stage(t - 5, lambda u: k_copy(u).wait_send(), mid)
        stage(t - 6, lambda u: w_copy(u).wait_send(), mid)
        stage(t - 5, lambda u: (e_out(u).wait_send(), g_mid(u).wait_send(), keep_own(u, full.at[slot(u)]).wait()), mid)
        stage(t - 5, lambda u: (g_out(u).wait_send(), keep_own(u, e_dst.at[slot(u)]).wait()), outer)
        stage(t - 7, lambda u: (f_out(u).wait_send(), keep_got(u).wait()), mid)
        stage(t - 5, lambda u: g_mid(u).wait_recv(), mid)
        stage(t - 6, lambda u: g_out(u).wait_recv(), outer)
        stage(t - 7, lambda u: f_out(u).wait_recv(), outer)
        stage(t - 5, t2_e, mid)
        stage(t - 4, t2_d, mid)
        stage(t - 3, t2_c, mid)
        stage(t - 2, t2_b, mid)
        stage(t - 1, t2_a)
        stage(t - 4, t1_d, outer)
        stage(t - 3, t1_c, mid)
        stage(t - 2, t1_b, mid)
        stage(t - 1, t1_a)
        stage(t, produce)
        return carry

    lax.fori_loop(0, total + 8, body, 0)


def gradient_sums(pairs, half):
    segments, operands = [], []
    for kind, left, right in pairs:
        area = half * right.shape[1] if kind == "D" else left.shape[1] * half
        segments.append((kind, area // (BR * BC)))
        operands += [left, right]
    total = sum(s[1] for s in segments)
    tokens = operands[0].shape[0]
    wide, thin = pltpu.VMEM((SLOTS, BR, BC), BF), pltpu.VMEM((SLOTS, BR // 2, BC), BF)
    dma = pltpu.SemaphoreType.DMA((SLOTS,))
    return pl.pallas_call(
        functools.partial(gradient_kernel, segments, half),
        out_shape=jax.ShapeDtypeStruct((2, total, BR, BC), BF),
        in_specs=[pl.BlockSpec(memory_space=pl.ANY)] * len(operands),
        out_specs=pl.BlockSpec(memory_space=pl.ANY),
        scratch_shapes=[pltpu.VMEM(v.shape, v.dtype) for v in operands]
        + [pltpu.SemaphoreType.DMA((len(operands),)), pltpu.VMEM((2, BR, tokens), BF)]
        + [wide, wide, wide, thin, thin, thin, thin, thin, thin, wide, wide, thin, thin, thin, wide]
        + [dma] * 24,
        compiler_params=pltpu.CompilerParams(
            collective_id=1, has_side_effects=True, vmem_limit_bytes=60 * 2**20
        ),
        cost_estimate=pl.CostEstimate(
            flops=4 * total * BR * BC * tokens, bytes_accessed=4 * total * BR * BC, transcendentals=0
        ),
    )(*operands)


def spread_kernel(side_ref, block_ref, out_ref):
    for i in range(block_ref.shape[1]):
        out_ref[0, i * BR : (i + 1) * BR] = block_ref[0, i].astype(F32)


def spread_pair_kernel(side_ref, gate_ref, up_ref, out_ref):
    for i in range(gate_ref.shape[1]):
        out_ref[i * BR : (i + 1) * BR, 0, :] = gate_ref[0, i].astype(F32)
        out_ref[i * BR : (i + 1) * BR, 1, :] = up_ref[0, i].astype(F32)


def spread_rows_kernel(side_ref, block_ref, out_ref):
    size = out_ref.shape[0]
    for q in range(BR // size):
        out_ref[:, q * BC : (q + 1) * BC] = block_ref[0, 0, q * size : (q + 1) * size].astype(F32)


def spread(body, side, blocks, grid, in_specs, out_spec, out_shape):
    return pl.pallas_call(
        body,
        grid_spec=pltpu.PrefetchScalarGridSpec(
            num_scalar_prefetch=1, grid=grid, in_specs=in_specs, out_specs=out_spec
        ),
        out_shape=jax.ShapeDtypeStruct(out_shape, F32),
        compiler_params=pltpu.CompilerParams(vmem_limit_bytes=48 * 2**20),
    )(side, *([blocks] * len(in_specs)))


def place_of(which, side_ref):
    return which + side_ref[0] - 2 * which * side_ref[0]


def spread_qkv(side, blocks, base, half, units):
    per, kind_blocks = half // BR, units // BC
    return spread(
        spread_kernel,
        side,
        blocks,
        (2, 3 * kind_blocks, per),
        [pl.BlockSpec((1, 1, BR, BC), lambda w, j, i, s: (w, base + i * 3 * kind_blocks + j, 0, 0))],
        pl.BlockSpec(
            (1, BR, BC),
            lambda w, j, i, s: (j // kind_blocks, i, place_of(w, s) * kind_blocks + j % kind_blocks),
        ),
        (3, half, 2 * units),
    ).transpose(1, 0, 2)


def spread_gate_up(side, blocks, base, half, units):
    tiles, columns = units // 128, 2 * units // BC

    def block_of(w, i, f):
        return (w, base + i * columns + f // (BC // 128), 0, f % (BC // 128))

    return spread(
        spread_pair_kernel,
        side,
        blocks,
        (2, half // BR, tiles),
        [
            pl.BlockSpec((1, 1, BR, 128), lambda w, i, f, s: block_of(w, i, f)),
            pl.BlockSpec((1, 1, BR, 128), lambda w, i, f, s: block_of(w, i, tiles + f)),
        ],
        pl.BlockSpec((BR, 2, 128), lambda w, i, f, s: (i, 0, place_of(w, s) * tiles + f)),
        (half, 2, 2 * units),
    )


def spread_rows(side, blocks, base, half, units):
    size = BR * BC // half
    count = units // size
    return spread(
        spread_rows_kernel,
        side,
        blocks,
        (2, count),
        [pl.BlockSpec((1, 1, BR, BC), lambda w, k, s: (w, base + k, 0, 0))],
        pl.BlockSpec((size, half), lambda w, k, s: (place_of(w, s) * count + k, 0)),
        (2 * units, half),
    )


def local(
    tokens,
    segments,
    ln1_gain,
    ln1_bias,
    qkv_weight,
    qkv_bias,
    out_weight,
    ln2_gain,
    ln2_bias,
    gate_up_weight,
    down_weight,
    cotangent,
):
    place = Place()
    r, c = place.r, place.c
    ids = segments[0]
    length = ids.shape[0]
    factor = HEAD ** (-0.5)
    half = qkv_weight.shape[0]
    units = qkv_weight.shape[2] // 2
    heads = units // HEAD
    hidden = gate_up_weight.shape[2] // 2

    other = swap(tokens, "row")
    mine = jnp.concatenate([tokens, other], axis=1)
    tokens_all = ordered(c, mine, swap(mine, "col"))
    params = jnp.stack([ln1_gain, ln1_bias, ln2_gain, ln2_bias])
    params = jnp.concatenate([params, swap(params, "row")], axis=1)

    qkv_flat = [qkv_weight[:, k] for k in range(3)]
    qkv_own = jnp.concatenate([piece(w, r, 2, 1) for w in qkv_flat], axis=1)
    qkv_send = jnp.concatenate([piece(w, 1 - r, 2, 1) for w in qkv_flat], axis=1)
    w_qkv = jnp.concatenate([qkv_own, fetch(qkv_send, place, False)], axis=0)
    w_out = jnp.concatenate(
        [piece(out_weight, r, 2), fetch(piece(out_weight, 1 - r, 2), place, True)], axis=1
    )
    w_gate = jnp.concatenate(
        [
            piece(gate_up_weight, r, 2, 2),
            fetch(piece(gate_up_weight, 1 - r, 2, 2), place, True),
        ],
        axis=0,
    )
    cot_other = swap(cotangent, "row")
    cot_mine = jnp.concatenate([cotangent, cot_other], axis=1)
    cot_all = ordered(c, cot_mine, swap(cot_mine, "col"))
    w_down = jnp.concatenate(
        [piece(down_weight, r, 2), fetch(piece(down_weight, 1 - r, 2), place, False)], axis=1
    )

    cosines, sines = rotary_tables(ids)
    table = tables(cosines, sines)
    inputs = tokens_all.astype(F32)
    normed, _, _ = norm_forward(inputs, params[0], params[1])
    act_one = normed.astype(BF)
    joined = dot(act_one, w_qkv)
    starts = (jnp.arange(length, dtype=jnp.int32) - doc_positions(ids))[:, None]
    bias = piece(qkv_bias, r, 2, 1).reshape(3, units // 128, 128).transpose(1, 0, 2)
    queries, keys, values, attended, raw, logs = attention_forward(joined, bias, starts, table)
    block = c * 2 + r
    own_inputs = piece(tokens_all, block, 4).astype(F32)
    branch = reduce_blocks(dot(attended, w_out).astype(BF), place)
    hidden_state = own_inputs + branch
    normed, normal_two, inverse_two = norm_forward(hidden_state, params[2], params[3])
    act_two = gather_blocks(normed.astype(BF), place)
    gate_up = jnp.einsum("sd,dkf->ksf", act_two, w_gate, preferred_element_type=F32)
    gate, up = gate_up[0], gate_up[1]
    inner = (jax.nn.silu(gate) * up).astype(BF)

    feed = reduce_blocks(dot(inner, w_down).astype(BF), place)
    result = (hidden_state + feed).astype(BF)
    result = ordered(r, result[:, :half], swap(result[:, half:], "row"))

    grad_inner = dot_t(cot_all, w_down)
    rate = 1.0 / (1.0 + jnp.exp(-gate))
    silu = gate * rate
    grad_gate = (grad_inner * up * (rate * (1.0 + gate * (1.0 - rate)))).astype(BF)
    grad_up = (grad_inner * silu).astype(BF)
    grad_two = jnp.stack([grad_gate, grad_up])
    grad_pair = jnp.concatenate([grad_gate, grad_up], axis=1)
    grad_act_two = reduce_blocks(
        jnp.einsum("ksf,dkf->sd", grad_two, w_gate, preferred_element_type=F32).astype(BF), place
    )
    grad_norm, ln2_gain_grad, ln2_bias_grad = norm_backward(
        grad_act_two, normal_two, inverse_two, params[2]
    )
    own_cot = piece(cot_all, block, 4).astype(F32)
    grad_hidden = own_cot + grad_norm
    grad_branch = gather_blocks(grad_hidden.astype(BF), place)
    grad_attended = dot_t(grad_branch, w_out).astype(BF)
    grad_joined = attention_backward(
        queries, keys, values, grad_attended, raw, logs, starts, table
    )
    grad_joined = jnp.concatenate(grad_joined, axis=1)
    bias_grad = jnp.sum(grad_joined, axis=0, dtype=F32)
    grad_act_one = reduce_blocks(dot_t(grad_joined, w_qkv).astype(BF), place)
    _, normal_one, inverse_one = norm_forward(own_inputs, params[0], params[1])
    grad_norm, ln1_gain_grad, ln1_bias_grad = norm_backward(
        grad_act_one, normal_one, inverse_one, params[0]
    )
    input_grad = grad_hidden + grad_norm
    input_grad = ordered(r, input_grad[:, :half], swap(input_grad[:, half:], "row"))

    small = jnp.stack([ln1_gain_grad, ln1_bias_grad, ln2_gain_grad, ln2_bias_grad])
    small = small[:, :half] + swap(small[:, half:], "row")
    small = small + swap(small, "col")
    bias_grad = bias_grad.reshape(3, units)
    small = jnp.concatenate([small.reshape(-1), bias_grad.reshape(-1)])
    if place.count == 8:
        for bit in (1, 2, 4):
            small = small + lax.ppermute(small, "dp", dp_perm(bit, 8))
    else:
        small = lax.psum(small, "dp")
    norms = small[: 4 * half].reshape(4, half)
    bias_grad = small[4 * half :].reshape(3, units)
    bias_grad = ordered(r, bias_grad, swap(bias_grad, "row"), 1)

    pairs = (
        ("D", act_two, grad_pair),
        ("D", act_one, grad_joined),
        ("U", attended, grad_branch),
        ("U", inner, cot_all),
    )
    if place.count == 8:
        sums = gradient_sums(pairs, half)
        side = r.reshape(1)
        qkv_base = half * 2 * hidden // (BR * BC)
        out_base = qkv_base + half * 3 * units // (BR * BC)
        down_base = out_base + half * units // (BR * BC)
        gate_up_grad = spread_gate_up(side, sums, 0, half, hidden)
        qkv_grad = spread_qkv(side, sums, qkv_base, half, units)
        out_grad = spread_rows(side, sums, out_base, half, units)
        down_grad = spread_rows(side, sums, down_base, half, hidden)
    else:
        sums = []
        for kind, left, right in pairs:
            both = t_dot(left, right).astype(BF)
            axis = 0 if kind == "D" else 1
            own, sent = jnp.split(both, 2, axis)
            sums.append([lax.psum(v, "dp").astype(F32) for v in (own, swap(sent, "row"))])
        gate_up_grad = ordered(r, *[v.reshape(half, 2, hidden) for v in sums[0]], 2)
        qkv_grad = ordered(r, *[v.reshape(half, 3, units) for v in sums[1]], 2)
        out_grad = ordered(r, *sums[2])
        down_grad = ordered(r, *sums[3])
    return (
        result,
        input_grad,
        norms[0],
        norms[1],
        qkv_grad,
        bias_grad,
        out_grad,
        norms[2],
        norms[3],
        gate_up_grad,
        down_grad,
    )


def solution(mesh):
    in_specs = (
        P(("dp", "col"), "row"),
        P("dp", None),
        P("row"),
        P("row"),
        P("row", None, "col"),
        P(None, "col"),
        P("col", "row"),
        P("row"),
        P("row"),
        P("row", None, "col"),
        P("col", "row"),
        P(("dp", "col"), "row"),
    )
    out_specs = (
        P(("dp", "col"), "row"),
        P(("dp", "col"), "row"),
        P("row"),
        P("row"),
        P("row", None, "col"),
        P(None, "col"),
        P("col", "row"),
        P("row"),
        P("row"),
        P("row", None, "col"),
        P("col", "row"),
    )
    return jax.shard_map(local, mesh=mesh, in_specs=in_specs, out_specs=out_specs, check_vma=False)
```

```python
import functools
import math

import jax
import jax.numpy as jnp
from jax import lax
from jax.experimental import pallas as pl
from jax.experimental.pallas import tpu as pltpu
from jax.sharding import PartitionSpec as P

HEAD = 64
ROT = 16
EPSILON = 1e-05
ROPE_BASE = 10000.0
NEGATIVE = -1e30
BF = jnp.bfloat16
F32 = jnp.float32
SWAP = [(0, 1), (1, 0)]
MESH = pl.DeviceIdType.MESH


def swap(v, axis):
    return lax.ppermute(v, axis, SWAP)


def ordered(flag, mine, other, axis=0):
    first = jnp.where(flag == 0, mine, other)
    second = jnp.where(flag == 0, other, mine)
    return jnp.concatenate([first, second], axis=axis)


def piece(v, index, count, axis=0):
    size = v.shape[axis] // count
    return lax.dynamic_slice_in_dim(v, index * size, size, axis)


def add(a, b):
    return (a.astype(F32) + b.astype(F32)).astype(BF)


def dot(a, b):
    return jnp.dot(a, b, preferred_element_type=F32)


def dot_t(a, b):
    return lax.dot_general(a, b, (((1,), (1,)), ((), ())), preferred_element_type=F32)


def t_dot(a, b):
    return lax.dot_general(a, b, (((0,), (0,)), ((), ())), preferred_element_type=F32)


class Place:
    def __init__(self):
        self.r = lax.axis_index("row")
        self.c = lax.axis_index("col")
        self.d = lax.axis_index("dp")
        self.count = lax.axis_size("dp")
        self.y = lax.rem(self.d, 2)
        self.zp = lax.rem(self.d // 2, 2)
        self.z = self.d // 2
        self.mid = (self.z == 1) | (self.z == 2)
        self.upper = (self.z >= 2).astype(jnp.int32)


def dp_perm(bit, count):
    return [(i, i ^ bit) for i in range(count)]


def cross(v):
    half = v.shape[-1] // 2
    return jnp.concatenate([v[..., half:], v[..., :half]], axis=-1)


def gather_blocks(block, place):
    other = cross(swap(block, "row"))
    pair = ordered(place.r, block, other)
    rest = swap(pair, "col")
    return ordered(place.c, pair, rest)


def reduce_blocks(partial, place):
    kept = piece(partial, place.c, 2)
    got = swap(piece(partial, 1 - place.c, 2), "col")
    held = add(kept, got)
    kept = piece(held, place.r, 2)
    got = cross(swap(piece(held, 1 - place.r, 2), "row"))
    return kept.astype(F32) + got.astype(F32)


def norm_forward(values, gain, shift):
    count = values.shape[-1]
    mean = jnp.sum(values, axis=-1, keepdims=True) / count
    spread = jnp.sum(values * values, axis=-1, keepdims=True) / count - mean * mean
    inverse = lax.rsqrt(spread + EPSILON)
    normal = (values - mean) * inverse
    return normal * gain + shift, normal, inverse


def norm_backward(grad, normal, inverse, gain):
    count = grad.shape[-1]
    scaled = grad * gain
    first = jnp.sum(scaled, axis=-1, keepdims=True) / count
    second = jnp.sum(scaled * normal, axis=-1, keepdims=True) / count
    grad_input = inverse * (scaled - first - normal * second)
    return grad_input, jnp.sum(grad * normal, axis=0), jnp.sum(grad, axis=0)


def doc_positions(segment_ids):
    places = jnp.arange(segment_ids.shape[0], dtype=jnp.int32)
    starts = jnp.concatenate([jnp.ones((1,), dtype=bool), segment_ids[1:] != segment_ids[:-1]])
    first_place = lax.cummax(jnp.where(starts, places, jnp.zeros_like(places)), axis=0)
    return places - first_place


def rotary_tables(segment_ids):
    places = doc_positions(segment_ids).astype(F32)
    freq_index = jnp.arange(ROT // 2, dtype=F32)
    inverse = jnp.exp(freq_index * (-2.0 / ROT) * math.log(ROPE_BASE))
    angles = places[:, None] * inverse[None, :]
    return (jnp.cos(angles), jnp.sin(angles))


LONGEST = 512
QB = 256

def windows(length):
    for begin in range(0, length, QB):
        low = max(0, (begin - LONGEST + 1) // QB * QB)
        yield begin, low, begin + QB


def barred(starts, begin, low, end):
    shape = (end - begin, end - low)
    query = begin + lax.broadcasted_iota(jnp.int32, shape, 0)
    key = low + lax.broadcasted_iota(jnp.int32, shape, 1)
    return jnp.where((key <= query) & (key >= starts), 0.0, NEGATIVE)


def turned(v, table):
    width = v.shape[-1]
    return v * table[0] + pltpu.roll(v, width - 8, 1) * table[1] + pltpu.roll(v, 8, 1) * table[2]


def nt(a, b):
    return lax.dot_general(a, b, (((1,), (1,)), ((), ())), preferred_element_type=F32)


def tn(a, b):
    return lax.dot_general(a, b, (((0,), (0,)), ((), ())), preferred_element_type=F32)


def backward_kernel(q_ref, k_ref, v_ref, g_ref, raw_ref, log_ref, starts_ref, table_ref, dq_ref, dk_ref, dv_ref, dk_acc, dv_acc):
    length = q_ref.shape[0]
    dk_acc[...] = jnp.zeros_like(dk_acc)
    dv_acc[...] = jnp.zeros_like(dv_acc)
    for begin, low, end in windows(length):
        bar = barred(starts_ref[begin:end], begin, low, end)
        outs, dks, dvs = [], [], []
        for h in range(2):
            lanes = slice(h * HEAD, (h + 1) * HEAD)
            q, k, v, g = q_ref[begin:end, lanes], k_ref[low:end, lanes], v_ref[low:end, lanes], g_ref[begin:end, lanes]
            weights = jnp.exp(nt(q, k) + bar - log_ref[0, begin:end, h : h + 1])
            dvs.append(tn(weights.astype(BF), g))
            inner = jnp.sum(g.astype(F32) * raw_ref[begin:end, lanes], axis=1, keepdims=True)
            grads = (weights * (nt(g, v) - inner)).astype(BF)
            outs.append(jnp.dot(grads, k, preferred_element_type=F32))
            dks.append(tn(grads, q))
        table = (table_ref[0, begin:end], -table_ref[1, begin:end], -table_ref[2, begin:end])
        dq_ref[begin:end] = turned(jnp.concatenate(outs, axis=1) * HEAD ** (-0.5), table).astype(BF)
        dk_acc[low:end] += jnp.concatenate(dks, axis=1)
        dv_acc[low:end] += jnp.concatenate(dvs, axis=1)
    table = (table_ref[0], -table_ref[1], -table_ref[2])
    dk_ref[...] = turned(dk_acc[...], table).astype(BF)
    dv_ref[...] = dv_acc[...].astype(BF)


def tables(cosines, sines):
    length = cosines.shape[0]
    ones = jnp.ones((length, HEAD - 16), F32)
    none = jnp.zeros((length, HEAD - 8), F32)
    one = jnp.concatenate([cosines, cosines, ones], axis=1)
    ahead = jnp.concatenate([-sines, none], axis=1)
    behind = jnp.concatenate([none[:, :8], sines, none[:, 8:]], axis=1)
    return jnp.stack([jnp.concatenate([v, v], axis=1) for v in (one, ahead, behind)])


def attention_backward(queries, keys, values, grads, raw, logs, starts, table):
    length, units = queries.shape
    pairs = units // 128
    same = pl.BlockSpec((length, 128), lambda p: (0, p))
    half = jax.ShapeDtypeStruct((length, units), BF)
    return pl.pallas_call(
        backward_kernel,
        grid=(pairs,),
        in_specs=[same] * 5
        + [
            pl.BlockSpec((1, length, 2), lambda p: (p, 0, 0)),
            pl.BlockSpec((length, 1), lambda p: (0, 0)),
            pl.BlockSpec((3, length, 128), lambda p: (0, 0, 0)),
        ],
        out_specs=[same] * 3,
        out_shape=[half] * 3,
        scratch_shapes=[pltpu.VMEM((length, 128), F32)] * 2,
        compiler_params=pltpu.CompilerParams(vmem_limit_bytes=48 * 2**20),
        cost_estimate=pl.CostEstimate(flops=pairs * 2 * length * 640 * 640, bytes_accessed=8 * 2**20, transcendentals=pairs * 2 * length * 640),
    )(queries, keys, values, grads, raw, logs, starts, table)


BR = 512
BC = 256
SLOTS = 6


def gradient_kernel(segments, bases, half, *refs):
    count = len(segments)
    total = sum(s[1] for s in segments)
    sources = refs[: 2 * count]
    out_ref = refs[2 * count]
    out_own, out_got = out_ref.at[0], out_ref.at[1]
    rest = refs[2 * count + 1 :]
    held = rest[: 2 * count]
    (
        load_sem,
        turn,
        part,
        x_src,
        x_dst,
        y_dst,
        acc,
        e_dst,
        low,
        m_dst,
        full,
        f_dst,
        deep,
        n_dst,
        key,
        k_dst,
        whole,
    ) = rest[2 * count : 2 * count + 17]
    sems = rest[2 * count + 17 :]
    names = ("x", "y", "ei", "eo", "m", "g", "fi", "fo", "n", "k", "w")
    send = {k: sems[i] for i, k in enumerate(names)}
    recv = {k: sems[len(names) + i] for i, k in enumerate(names)}
    store_own, store_got = sems[2 * len(names)], sems[2 * len(names) + 1]

    d, r = lax.axis_index("dp"), lax.axis_index("row")
    y, z = lax.rem(d, 2), d // 2
    upper = d // 4
    mid = (z == 1) | (z == 2)
    outer = (z == 0) | (z == 3)
    x_peer = {"row": 1 - r}
    y_peer = {"dp": d + 1 - 2 * y}
    e_peer = {"dp": d + 2 - 4 * lax.rem(z, 2)}
    m_peer = {"dp": d + 2 - 4 * upper}

    loads = []
    for i in range(2 * count):
        loads.append(pltpu.make_async_copy(sources[i], held[i], load_sem.at[i]))
        loads[-1].start()

    barrier = pltpu.get_barrier_semaphore()
    for peer in (x_peer, y_peer, e_peer):
        pl.semaphore_signal(barrier, inc=1, device_id=peer, device_id_type=MESH)

    @pl.when(mid)
    def _():
        pl.semaphore_signal(barrier, inc=1, device_id=m_peer, device_id_type=MESH)
        pl.semaphore_wait(barrier, 4)

    @pl.when(outer)
    def _():
        pl.semaphore_wait(barrier, 3)

    rows = BR // 2

    def halves(index):
        return pl.ds(pl.multiple_of(index * rows, rows), rows)

    def copy(name, u, src, dst, peer):
        s = lax.rem(u, SLOTS)
        return pltpu.make_async_remote_copy(
            src_ref=src, dst_ref=dst, send_sem=send[name].at[s], recv_sem=recv[name].at[s], device_id=peer, device_id_type=MESH
        )

    def slot(u):
        return lax.rem(u, SLOTS)

    def spot(u):
        place, first = u, 0
        for (_, blocks), base in zip(segments, bases):
            place = jnp.where(u >= first, u + (base - first), place)
            first += blocks
        return place

    def out_half(ref, u, index):
        return ref.at[spot(u), halves(index)]

    def x_copy(u):
        return copy("x", u, x_src.at[slot(u)], x_dst.at[slot(u)], x_peer)

    def y_copy(u):
        return copy("y", u, part.at[slot(u), halves(1 - y)], y_dst.at[slot(u)], y_peer)

    def e_in(u):
        return copy("ei", u, acc.at[slot(u)], e_dst.at[slot(u)], e_peer)

    def e_out(u):
        return copy("eo", u, full.at[slot(u)], e_dst.at[slot(u)], e_peer)

    def m_copy(u):
        return copy("m", u, low.at[slot(u)], m_dst.at[slot(u)], m_peer)

    def g_mid(u):
        return copy("g", u, full.at[slot(u)], out_half(out_own, u, y), y_peer)

    def g_out(u):
        return copy("g", u, e_dst.at[slot(u)], out_half(out_own, u, y), y_peer)

    def f_in(u):
        return copy("fi", u, x_dst.at[slot(u)], f_dst.at[slot(u)], e_peer)

    def f_out(u):
        return copy("fo", u, whole.at[slot(u)], out_got.at[spot(u)], e_peer)

    def n_copy(u):
        return copy("n", u, deep.at[slot(u), halves(1 - upper)], n_dst.at[slot(u)], m_peer)

    def k_copy(u):
        return copy("k", u, key.at[slot(u)], k_dst.at[slot(u)], y_peer)

    def w_copy(u):
        place = whole.at[slot(u), halves(upper)]
        return copy("w", u, place, place, m_peer)

    def keep_own(u, src):
        return pltpu.make_async_copy(src, out_half(out_own, u, y), store_own.at[slot(u)])

    def keep_got(u):
        return pltpu.make_async_copy(whole.at[slot(u)], out_got.at[spot(u)], store_got.at[slot(u)])

    def stage(u, fn, role=None):
        ok = (u >= 0) & (u < total)
        if role is not None:
            ok = ok & role

        @pl.when(ok)
        def _():
            fn(u)

    def produce(u):
        s = slot(u)
        first = 0
        for i, (kind, blocks) in enumerate(segments):
            lhs, rhs = held[2 * i], held[2 * i + 1]

            @pl.when(u == first)
            def _(i=i):
                loads[2 * i].wait()
                loads[2 * i + 1].wait()

            @pl.when((u >= first) & (u < first + blocks))
            def _(kind=kind, first=first, lhs=lhs, rhs=rhs):
                k = u - first
                if kind == "D":
                    columns = rhs.shape[1] // BC

                    @pl.when(lax.rem(k, columns) == 0)
                    def _():
                        for side in range(2):
                            at = pl.multiple_of(side * half + k // columns * BR, BR)
                            turn[side] = lhs[:, pl.ds(at, BR)].T

                    right = rhs[:, pl.ds(pl.multiple_of(lax.rem(k, columns) * BC, BC), BC)]
                    for side, ref in ((1, x_src), (0, part)):
                        ref[s] = jnp.dot(turn[side], right, preferred_element_type=F32).astype(BF)
                else:
                    size = BR * BC // half
                    left = lhs[:, pl.ds(pl.multiple_of(k * size, size), size)].T
                    for side, ref in ((1, x_src), (0, part)):
                        for q in range(half // BC):
                            right = rhs[:, side * half + q * BC : side * half + (q + 1) * BC]
                            ref[s, q * size : (q + 1) * size] = jnp.dot(
                                left, right, preferred_element_type=F32
                            ).astype(BF)

            first += blocks
        x_copy(u).start()
        y_copy(u).start()

    def t1_a(u):
        s = slot(u)
        y_copy(u).wait_recv()
        acc[s] = part[s, halves(y)] + y_dst[s]
        pl.when(outer)(lambda: e_in(u).start())

    def t1_b(u):
        s = slot(u)
        e_in(u).wait_recv()
        low[s] = acc[s] + e_dst[s]
        m_copy(u).start()

    def t1_c(u):
        s = slot(u)
        m_copy(u).wait_recv()
        full[s] = low[s] + m_dst[s]
        e_out(u).start()
        g_mid(u).start()
        keep_own(u, full.at[s]).start()

    def t1_d(u):
        e_out(u).wait_recv()
        g_out(u).start()
        keep_own(u, e_dst.at[slot(u)]).start()

    def t2_a(u):
        x_copy(u).wait_recv()
        pl.when(outer)(lambda: f_in(u).start())

    def t2_b(u):
        s = slot(u)
        f_in(u).wait_recv()
        deep[s] = x_dst[s] + f_dst[s]
        n_copy(u).start()

    def t2_c(u):
        s = slot(u)
        n_copy(u).wait_recv()
        key[s] = deep[s, halves(upper)] + n_dst[s]
        k_copy(u).start()

    def t2_d(u):
        s = slot(u)
        k_copy(u).wait_recv()
        whole[s, halves(upper)] = key[s] + k_dst[s]
        w_copy(u).start()

    def t2_e(u):
        w_copy(u).wait_recv()
        f_out(u).start()
        keep_got(u).start()

    def body(t, carry):
        stage(t - 2, lambda u: (x_copy(u).wait_send(), y_copy(u).wait_send()))
        stage(t - 3, lambda u: e_in(u).wait_send(), outer)
        stage(t - 3, lambda u: f_in(u).wait_send(), outer)
        stage(t - 4, lambda u: (m_copy(u).wait_send(), n_copy(u).wait_send()), mid)
        stage(t - 5, lambda u: k_copy(u).wait_send(), mid)
        stage(t - 6, lambda u: w_copy(u).wait_send(), mid)
        stage(t - 5, lambda u: (e_out(u).wait_send(), g_mid(u).wait_send(), keep_own(u, full.at[slot(u)]).wait()), mid)
        stage(t - 5, lambda u: (g_out(u).wait_send(), keep_own(u, e_dst.at[slot(u)]).wait()), outer)
        stage(t - 7, lambda u: (f_out(u).wait_send(), keep_got(u).wait()), mid)
        stage(t - 5, lambda u: g_mid(u).wait_recv(), mid)
        stage(t - 6, lambda u: g_out(u).wait_recv(), outer)
        stage(t - 7, lambda u: f_out(u).wait_recv(), outer)
        stage(t - 5, t2_e, mid)
        stage(t - 4, t2_d, mid)
        stage(t - 3, t2_c, mid)
        stage(t - 2, t2_b, mid)
        stage(t - 1, t2_a)
        stage(t - 4, t1_d, outer)
        stage(t - 3, t1_c, mid)
        stage(t - 2, t1_b, mid)
        stage(t - 1, t1_a)
        stage(t, produce)
        return carry

    lax.fori_loop(0, total + 8, body, 0)


def gradient_sums(pairs, half):
    segments, operands = [], []
    for kind, left, right in pairs:
        area = half * right.shape[1] if kind == "D" else left.shape[1] * half
        segments.append((kind, area // (BR * BC)))
        operands += [left, right]
    total = sum(s[1] for s in segments)
    tokens = operands[0].shape[0]
    bases, end = [], 0
    for _, blocks in segments:
        bases.append(-(-end // blocks) * blocks)
        end = bases[-1] + blocks
    wide, thin = pltpu.VMEM((SLOTS, BR, BC), BF), pltpu.VMEM((SLOTS, BR // 2, BC), BF)
    dma = pltpu.SemaphoreType.DMA((SLOTS,))
    sums = pl.pallas_call(
        functools.partial(gradient_kernel, segments, bases, half),
        out_shape=jax.ShapeDtypeStruct((2, end, BR, BC), BF),
        in_specs=[pl.BlockSpec(memory_space=pl.ANY)] * len(operands),
        out_specs=pl.BlockSpec(memory_space=pl.ANY),
        scratch_shapes=[pltpu.VMEM(v.shape, v.dtype) for v in operands]
        + [pltpu.SemaphoreType.DMA((len(operands),)), pltpu.VMEM((2, BR, tokens), BF)]
        + [wide, wide, wide, thin, thin, thin, thin, thin, thin, wide, wide, thin, thin, thin, wide]
        + [dma] * 24,
        compiler_params=pltpu.CompilerParams(
            collective_id=1, has_side_effects=True, vmem_limit_bytes=60 * 2**20
        ),
        cost_estimate=pl.CostEstimate(
            flops=4 * total * BR * BC * tokens, bytes_accessed=4 * total * BR * BC, transcendentals=0
        ),
    )(*operands)
    return sums, bases


def spread_qkv_kernel(side_ref, block_ref, out_ref):
    per = out_ref.shape[2] // BC
    for j in range(block_ref.shape[1]):
        at = j % per * BC
        out_ref[j // per, :, at : at + BC] = block_ref[0, j].astype(F32)


def spread_pair_kernel(side_ref, block_ref, out_ref):
    units = out_ref.shape[2]
    for j in range(block_ref.shape[1]):
        for at in range(0, BC, 128):
            unit = j * BC + at
            out_ref[:, unit // units, unit % units : unit % units + 128] = block_ref[
                0, j, :, at : at + 128
            ].astype(F32)


def spread_rows_kernel(side_ref, block_ref, out_ref):
    size = block_ref.shape[2]
    for k in range(block_ref.shape[1]):
        out_ref[k * size : (k + 1) * size] = block_ref[0, k].astype(F32)


def spread(body, side, blocks, steps, in_spec, out_spec, out_shape):
    return pl.pallas_call(
        body,
        grid_spec=pltpu.PrefetchScalarGridSpec(
            num_scalar_prefetch=1, grid=(2, steps), in_specs=[in_spec], out_specs=out_spec
        ),
        out_shape=jax.ShapeDtypeStruct(out_shape, F32),
        compiler_params=pltpu.CompilerParams(vmem_limit_bytes=48 * 2**20),
    )(side, blocks)


def place_of(which, side_ref):
    return which + side_ref[0] - 2 * which * side_ref[0]


def spread_columns(side, blocks, base, half, units, kinds, rows):
    columns, per = kinds * units // BC, BR // rows
    first = base // columns
    in_spec = pl.BlockSpec(
        (1, columns, rows, BC), lambda w, i, s: (w, first + i // per, i % per, 0)
    )
    if kinds == 3:
        return spread(
            spread_qkv_kernel,
            side,
            blocks,
            half // rows,
            in_spec,
            pl.BlockSpec((3, rows, units), lambda w, i, s: (0, i, place_of(w, s))),
            (3, half, 2 * units),
        ).transpose(1, 0, 2)
    return spread(
        spread_pair_kernel,
        side,
        blocks,
        half // rows,
        in_spec,
        pl.BlockSpec((rows, 2, units), lambda w, i, s: (i, 0, place_of(w, s))),
        (half, 2, 2 * units),
    )


def spread_rows(side, blocks, base, half, units):
    size = BR * BC // half
    count = units // size
    return spread(
        spread_rows_kernel,
        side,
        blocks,
        half // BC,
        pl.BlockSpec((1, count, size, BC), lambda w, q, s: (w, base // count, q, 0)),
        pl.BlockSpec((units, BC), lambda w, q, s: (place_of(w, s), q)),
        (2 * units, half),
    )


def front_kernel(
    tokens,
    starts_ref,
    table_ref,
    params_ref,
    bias_ref,
    qkv_w,
    out_w,
    gate_w,
    down_w,
    cotangent,
    act_one,
    q_out,
    k_out,
    v_out,
    att_out,
    raw_out,
    log_out,
    hid_out,
    act_two,
    gate_out,
    up_out,
    inner_out,
    wq_out,
    wo_out,
    wg_out,
    wd_out,
    cot_out,
    own_out,
    tok,
    act,
    wq,
    wo,
    wg,
    gate_far,
    gate_own,
    qs,
    ks,
    vs,
    att,
    raw,
    logs,
    core_in,
    row_src,
    row_in,
    own_in,
    hid,
    tile,
    send_sem,
    recv_sem,
    load_sem,
    store_sem,
):
    r, c, d = lax.axis_index("row"), lax.axis_index("col"), lax.axis_index("dp")
    y, zp = lax.rem(d, 2), lax.rem(d // 2, 2)
    length, width = tok.shape
    half = width // 2
    part, block = length // 2, length // 4
    units, hidden = qs.shape[1], wg.shape[2]
    sub = zp * 2 + y
    dy, dz = 1 - 2 * y, 2 - 4 * zp
    row_peer, col_peer = {"row": 1 - r}, {"col": 1 - c}
    near = ({"dp": d + dy}, {"dp": d + dz}, {"dp": d + dy + dz})

    barrier = pltpu.get_barrier_semaphore()
    for peer in (row_peer, col_peer) + near:
        pl.semaphore_signal(barrier, inc=1, device_id=peer, device_id_type=MESH)

    stores = []

    def span(start, size):
        return pl.ds(pl.multiple_of(start, size), size)

    def load(n, src, dst):
        copy = pltpu.make_async_copy(src, dst, load_sem.at[n])
        copy.start()
        return copy

    def store(src, dst):
        copy = pltpu.make_async_copy(src, dst, store_sem.at[len(stores)])
        copy.start()
        stores.append(copy)
        return copy

    def remote(n, src, dst, peer):
        return pltpu.make_async_remote_copy(
            src_ref=src,
            dst_ref=dst,
            send_sem=send_sem.at[n],
            recv_sem=recv_sem.at[n],
            device_id=peer,
            device_id_type=MESH,
        )

    mine, theirs = span(r * units, units), span((1 - r) * units, units)
    own_rows, far_rows = span(c * part, part), span((1 - c) * part, part)
    lo, hi = pl.ds(0, half), pl.ds(half, half)
    quarter = half // 4
    down_quarter = hidden // 4

    load_tok = load(0, tokens, tok.at[own_rows, lo])
    load_q = load(1, qkv_w.at[:, :, mine], wq.at[:, lo])
    load_o = load(2, out_w.at[mine], wo.at[:, lo])
    gate_cols = span(r * hidden, hidden)

    def load_gate(i):
        return load(3 + i % 2, gate_w.at[pl.ds(i * quarter, quarter), :, gate_cols], gate_own.at[i % 2])

    load_d = load(5, down_w.at[span(r * hidden, hidden)], wd_out.at[:, lo])
    load_c = load(6, cotangent, cot_out.at[own_rows, lo])
    gates = [load_gate(0), load_gate(1)]

    rows_sub = span(sub * quarter, quarter)
    rows_far = span(half + sub * quarter, quarter)
    q_x = remote(0, qkv_w.at[:, rows_sub, theirs], wq.at[:, rows_far], row_peer)
    q_n = [remote(1 + k, wq.at[:, rows_far], wq.at[:, rows_far], p) for k, p in enumerate(near)]
    tok_x = remote(4, tokens, tok.at[own_rows, hi], row_peer)
    tok_c = remote(5, tokens, tok.at[own_rows, lo], col_peer)
    tok_f = remote(6, tok.at[own_rows, hi], tok.at[own_rows, hi], col_peer)
    out_rows = units // 4
    out_sub = span(sub * out_rows, out_rows)
    o_x = remote(
        7, out_w.at[span((1 - r) * units + sub * out_rows, out_rows)], wo.at[out_sub, hi], row_peer
    )
    o_n = [remote(8 + k, wo.at[out_sub, hi], wo.at[out_sub, hi], p) for k, p in enumerate(near)]
    g_x = remote(
        11, gate_w.at[rows_sub, :, span((1 - r) * hidden, hidden)], gate_far.at[sub], row_peer
    )
    g_n = [remote(12 + k, gate_far.at[sub], gate_far.at[sub], p) for k, p in enumerate(near)]
    down_sub = span(sub * down_quarter, down_quarter)
    d_x = remote(
        15,
        down_w.at[span((1 - r) * hidden + sub * down_quarter, down_quarter)],
        wd_out.at[down_sub, hi],
        row_peer,
    )
    d_n = [
        remote(16 + k, wd_out.at[down_sub, hi], wd_out.at[down_sub, hi], p)
        for k, p in enumerate(near)
    ]
    c_x = remote(19, cotangent, cot_out.at[own_rows, hi], row_peer)
    c_c = remote(20, cotangent, cot_out.at[own_rows, lo], col_peer)
    c_f = remote(21, cot_out.at[own_rows, hi], cot_out.at[own_rows, hi], col_peer)
    rs_c = remote(22, act.at[far_rows], core_in, col_peer)
    rs_x = remote(23, row_src, row_in, row_peer)
    own_block = span(c * part + r * block, block)
    x_block = span(c * part + (1 - r) * block, block)
    ag_x = [
        remote(24, tok.at[own_block, lo], tok.at[own_block, hi], row_peer),
        remote(25, tok.at[own_block, hi], tok.at[own_block, lo], row_peer),
    ]
    ag_c = remote(26, tok.at[own_block], tok.at[own_block], col_peer)
    ag_f = remote(27, tok.at[x_block], tok.at[x_block], col_peer)

    def start(copies):
        for copy in copies:
            copy.start()

    def arrived(copies):
        for copy in copies:
            copy.wait_recv()

    def part_gate(ref, at):
        wg[0, at] = ref[:, 0, :]
        wg[1, at] = ref[:, 1, :]

    pl.semaphore_wait(barrier, 5)
    q_x.start()
    tok_c.start()
    c_c.start()
    for i in range(4):
        if i == 2:
            q_x.wait_recv()
            start(q_n)
            tok_x.start()
        gates[i].wait()
        part_gate(gate_own.at[i % 2], pl.ds(i * quarter, quarter))
        if i + 2 < 4:
            gates.append(load_gate(i + 2))
    tok_x.wait_recv()
    tok_f.start()
    o_x.start()
    g_x.start()

    load_tok.wait()
    tok_c.wait_recv()

    def normed(v, at):
        mean = jnp.sum(v, axis=1, keepdims=True) / width
        spread_of = jnp.sum(v * v, axis=1, keepdims=True) / width - mean * mean
        v = (v - mean) * lax.rsqrt(spread_of + EPSILON)
        return (v * params_ref[at : at + 1] + params_ref[at + 1 : at + 2]).astype(BF)

    norm_rows = 64

    def norm_one(base):
        def body(i, carry):
            at = span(base + i * norm_rows, norm_rows)
            act[at] = normed(tok[at].astype(F32), 0)
            return carry

        lax.fori_loop(0, part // norm_rows, body, 0)

    norm_one(c * part)
    own_in[...] = tok[own_block]
    tok_f.wait_recv()
    norm_one((1 - c) * part)
    store(act, act_one)
    store(own_in, own_out)

    load_q.wait()
    arrived(q_n)
    o_x.wait_recv()
    start(o_n)
    store(wq, wq_out)
    chunk = 256

    def project(i, carry):
        at = span(i * chunk, chunk)
        rows = act[at]
        for kind, ref in enumerate((qs, ks, vs)):
            out = jnp.dot(rows, wq[kind], preferred_element_type=F32) + bias_ref[kind : kind + 1]
            if kind == 2:
                ref[at] = out.astype(BF)
                continue
            table = (table_ref[0, at], table_ref[1, at], table_ref[2, at])
            for g in range(units // 128):
                lanes = slice(g * 128, (g + 1) * 128)
                v = turned(out[:, lanes], table).astype(BF)
                if kind == 0:
                    v = (v.astype(F32) * HEAD ** (-0.5)).astype(BF)
                ref[at, lanes] = v
        return carry

    lax.fori_loop(0, length // chunk, project, 0)
    for ref, out in ((qs, q_out), (ks, k_out), (vs, v_out)):
        store(ref, out)

    pairs = units // 128

    def attend(p, carry):
        @pl.when(p == pairs // 2)
        def _():
            g_x.wait_recv()
            start(g_n)
            d_x.start()

        lane0 = p * 128
        q2 = qs[:, span(lane0, 128)]
        k2 = ks[:, span(lane0, 128)]
        v2 = vs[:, span(lane0, 128)]
        for begin, low, end in windows(length):
            bar = barred(starts_ref[begin:end], begin, low, end)
            outs = []
            for h in range(2):
                lanes = slice(h * HEAD, (h + 1) * HEAD)
                scores = nt(q2[begin:end, lanes], k2[low:end, lanes]) + bar
                maxima = jnp.max(scores, axis=1, keepdims=True)
                shifted = jnp.exp(scores - maxima).astype(BF)
                wide = jnp.concatenate([v2[low:end, lanes], jnp.ones((end - low, HEAD), BF)], axis=1)
                got = jnp.dot(shifted, wide, preferred_element_type=F32)
                totals = got[:, HEAD : HEAD + 1]
                outs.append(got[:, :HEAD] / totals)
                logs[p, begin:end, h : h + 1] = maxima + jnp.log(totals)
            out = jnp.concatenate(outs, axis=1)
            raw[begin:end, span(lane0, 128)] = out
            att[begin:end, span(lane0, 128)] = out.astype(BF)
        return carry

    lax.fori_loop(0, pairs, attend, 0)
    store(att, att_out)
    store(raw, raw_out)
    store(logs, log_out)

    load_o.wait()
    arrived(o_n)
    store(wo, wo_out)
    stores[0].wait()
    tok_f.wait_send()

    def branch(base):
        def body(i, carry):
            at = span(base + i * chunk, chunk)
            act[at] = jnp.dot(att[at], wo[...], preferred_element_type=F32).astype(BF)
            return carry

        lax.fori_loop(0, part // chunk, body, 0)

    branch((1 - c) * part)
    rs_c.start()
    branch(c * part)
    rs_c.wait_recv()
    row_src[...] = act[x_block] + core_in[span((1 - r) * block, block)]
    rs_x.start()
    part_gate(gate_far.at[sub], span(half + sub * quarter, quarter))
    subs = (zp * 2 + 1 - y, (1 - zp) * 2 + y, (1 - zp) * 2 + 1 - y)
    rs_x.wait_recv()
    hid_rows = 64

    def norm_two(i, carry):
        at = span(i * hid_rows, hid_rows)
        kept = act[span(c * part + r * block + i * hid_rows, hid_rows)].astype(F32)
        kept = kept + core_in[span(r * block + i * hid_rows, hid_rows)].astype(F32)
        got = row_in[at].astype(F32)
        kept = kept + jnp.concatenate([got[:, half:], got[:, :half]], axis=1)
        kept = own_in[at].astype(F32) + kept
        hid[at] = kept
        tok[span(c * part + r * block + i * hid_rows, hid_rows)] = normed(kept, 2)
        return carry

    lax.fori_loop(0, block // hid_rows, norm_two, 0)
    start(ag_x)
    ag_c.start()
    store(hid, hid_out)
    d_x.wait_recv()
    start(d_n)
    c_x.start()
    for k in range(3):
        g_n[k].wait_recv()
        part_gate(gate_far.at[subs[k]], span(half + subs[k] * quarter, quarter))
    store(wg, wg_out)

    stores_of = []
    columns = [(at, min(512, hidden - at)) for at in range(0, hidden, 512)]
    for b in range(4):
        cc = c if b % 2 == 0 else 1 - c
        rr = r if b < 2 else 1 - r
        at = span(cc * part + rr * block, block)
        if b == 1:
            ag_c.wait_recv()
        elif b == 2:
            arrived(ag_x)
            ag_f.start()
        elif b == 3:
            ag_f.wait_recv()
        s = b % 2
        for copy in stores_of[3 * (b - 2) : 3 * (b - 1)] if b >= 2 else ():
            copy.wait()
        rows = tok[at]
        for first, size in columns:
            cols = slice(first, first + size)
            gate = jnp.dot(rows, wg[0, :, cols], preferred_element_type=F32)
            up = jnp.dot(rows, wg[1, :, cols], preferred_element_type=F32)
            tile[s, 0, :, cols] = gate.astype(BF)
            tile[s, 1, :, cols] = up.astype(BF)
            tile[s, 2, :, cols] = (gate / (1.0 + jnp.exp(-gate)) * up).astype(BF)
        for k, out in enumerate((gate_out, up_out, inner_out)):
            copy = pltpu.make_async_copy(tile.at[s, k], out.at[at], load_sem.at[7 + 3 * s + k])
            copy.start()
            stores_of.append(copy)
    store(tok, act_two)
    c_x.wait_recv()
    load_c.wait()
    c_f.start()
    for copy in stores_of[6:] + stores[1:] + [load_d]:
        copy.wait()
    arrived(d_n)
    c_c.wait_recv()
    c_f.wait_recv()
    for copy in [q_x, tok_x, tok_c, o_x, g_x, d_x, c_x, c_c, c_f, rs_c, rs_x, ag_c, ag_f] + (
        q_n + o_n + g_n + d_n + ag_x
    ):
        copy.wait_send()


def front(tokens, starts, table, params, bias, qkv_w, out_w, gate_w, down_w, cotangent):
    part, half = tokens.shape
    length, width, block = 2 * part, 2 * half, part // 2
    units, hidden = out_w.shape[0] // 2, down_w.shape[0] // 2
    any_spec, vmem_spec = pl.BlockSpec(memory_space=pl.ANY), pl.BlockSpec(memory_space=pltpu.VMEM)
    pairs = units // 128

    def bf(*shape):
        return jax.ShapeDtypeStruct(shape, BF)

    def f32(*shape):
        return jax.ShapeDtypeStruct(shape, F32)

    outs = [
        bf(length, width),
        bf(length, units),
        bf(length, units),
        bf(length, units),
        bf(length, units),
        f32(length, units),
        f32(pairs, length, 2),
        f32(block, width),
        bf(length, width),
        bf(length, hidden),
        bf(length, hidden),
        bf(length, hidden),
        bf(3, width, units),
        bf(units, width),
        bf(2, width, hidden),
        bf(hidden, width),
        bf(length, width),
        bf(block, width),
    ]
    scratch = [
        bf(length, width),
        bf(length, width),
        bf(3, width, units),
        bf(units, width),
        bf(2, width, hidden),
        bf(4, half // 4, 2, hidden),
        bf(2, half // 4, 2, hidden),
        bf(length, units),
        bf(length, units),
        bf(length, units),
        bf(length, units),
        f32(length, units),
        f32(pairs, length, 2),
        bf(part, width),
        bf(block, width),
        bf(block, width),
        bf(block, width),
        f32(block, width),
        bf(2, 3, block, hidden),
    ]
    dma = pltpu.SemaphoreType.DMA
    return pl.pallas_call(
        front_kernel,
        out_shape=outs,
        in_specs=[any_spec] + [vmem_spec] * 4 + [any_spec] * 5,
        out_specs=[any_spec] * len(outs),
        scratch_shapes=[pltpu.VMEM(v.shape, v.dtype) for v in scratch]
        + [dma((28,)), dma((28,)), dma((13,)), dma((16,))],
        compiler_params=pltpu.CompilerParams(
            collective_id=2, has_side_effects=True, vmem_limit_bytes=62 * 2**20
        ),
        cost_estimate=pl.CostEstimate(
            flops=2 * length * width * (4 * units + 2 * hidden),
            bytes_accessed=100 * 2**20,
            transcendentals=length * 2048,
        ),
    )(tokens, starts, table, params, bias, qkv_w, out_w, gate_w, down_w, cotangent)


def local(
    tokens,
    segments,
    ln1_gain,
    ln1_bias,
    qkv_weight,
    qkv_bias,
    out_weight,
    ln2_gain,
    ln2_bias,
    gate_up_weight,
    down_weight,
    cotangent,
):
    place = Place()
    r, c = place.r, place.c
    ids = segments[0]
    length = ids.shape[0]
    factor = HEAD ** (-0.5)
    half = qkv_weight.shape[0]
    units = qkv_weight.shape[2] // 2
    heads = units // HEAD
    hidden = gate_up_weight.shape[2] // 2

    params = jnp.stack([ln1_gain, ln1_bias, ln2_gain, ln2_bias])
    params = jnp.concatenate([params, swap(params, "row")], axis=1)
    cosines, sines = rotary_tables(ids)
    table = tables(cosines, sines)
    starts = (jnp.arange(length, dtype=jnp.int32) - doc_positions(ids))[:, None]
    bias = piece(qkv_bias, r, 2, 1)
    (
        act_one,
        queries,
        keys,
        values,
        attended,
        raw,
        logs,
        hidden_state,
        act_two,
        gate,
        up,
        inner,
        w_qkv,
        w_out,
        w_gate,
        w_down,
        cot_all,
        own_inputs,
    ) = front(
        tokens,
        starts,
        table,
        params,
        bias,
        qkv_weight.transpose(1, 0, 2),
        out_weight,
        gate_up_weight,
        down_weight,
        cotangent,
    )
    block = c * 2 + r
    own_inputs = own_inputs.astype(F32)
    _, normal_two, inverse_two = norm_forward(hidden_state, params[2], params[3])
    gate, up = gate.astype(F32), up.astype(F32)

    feed = reduce_blocks(dot(inner, w_down).astype(BF), place)
    result = (hidden_state + feed).astype(BF)
    result = ordered(r, result[:, :half], swap(result[:, half:], "row"))

    grad_inner = dot_t(cot_all, w_down)
    rate = 1.0 / (1.0 + jnp.exp(-gate))
    silu = gate * rate
    grad_gate = (grad_inner * up * (rate * (1.0 + gate * (1.0 - rate)))).astype(BF)
    grad_up = (grad_inner * silu).astype(BF)
    grad_two = jnp.stack([grad_gate, grad_up])
    grad_pair = jnp.concatenate([grad_gate, grad_up], axis=1)
    grad_act_two = reduce_blocks(
        jnp.einsum("ksf,kdf->sd", grad_two, w_gate, preferred_element_type=F32).astype(BF), place
    )
    grad_norm, ln2_gain_grad, ln2_bias_grad = norm_backward(
        grad_act_two, normal_two, inverse_two, params[2]
    )
    own_cot = piece(cot_all, block, 4).astype(F32)
    grad_hidden = own_cot + grad_norm
    grad_branch = gather_blocks(grad_hidden.astype(BF), place)
    grad_attended = dot_t(grad_branch, w_out).astype(BF)
    grad_joined = attention_backward(
        queries, keys, values, grad_attended, raw, logs, starts, table
    )
    grad_joined = jnp.concatenate(grad_joined, axis=1)
    bias_grad = jnp.sum(grad_joined, axis=0, dtype=F32)
    grad_kinds = grad_joined.reshape(length, 3, units)
    grad_act_one = reduce_blocks(
        jnp.einsum("sku,kdu->sd", grad_kinds, w_qkv, preferred_element_type=F32).astype(BF), place
    )
    _, normal_one, inverse_one = norm_forward(own_inputs, params[0], params[1])
    grad_norm, ln1_gain_grad, ln1_bias_grad = norm_backward(
        grad_act_one, normal_one, inverse_one, params[0]
    )
    input_grad = grad_hidden + grad_norm
    input_grad = ordered(r, input_grad[:, :half], swap(input_grad[:, half:], "row"))

    small = jnp.stack([ln1_gain_grad, ln1_bias_grad, ln2_gain_grad, ln2_bias_grad])
    small = small[:, :half] + swap(small[:, half:], "row")
    small = small + swap(small, "col")
    bias_grad = bias_grad.reshape(3, units)
    small = jnp.concatenate([small.reshape(-1), bias_grad.reshape(-1)])
    if place.count == 8:
        for bit in (1, 2, 4):
            small = small + lax.ppermute(small, "dp", dp_perm(bit, 8))
    else:
        small = lax.psum(small, "dp")
    norms = small[: 4 * half].reshape(4, half)
    bias_grad = small[4 * half :].reshape(3, units)
    bias_grad = ordered(r, bias_grad, swap(bias_grad, "row"), 1)

    pairs = (
        ("D", act_two, grad_pair),
        ("D", act_one, grad_joined),
        ("U", attended, grad_branch),
        ("U", inner, cot_all),
    )
    if place.count == 8:
        sums, bases = gradient_sums(pairs, half)
        side = r.reshape(1)
        gate_up_grad = spread_columns(side, sums, bases[0], half, hidden, 2, 256)
        qkv_grad = spread_columns(side, sums, bases[1], half, units, 3, 256)
        out_grad = spread_rows(side, sums, bases[2], half, units)
        down_grad = spread_rows(side, sums, bases[3], half, hidden)
    else:
        sums = []
        for kind, left, right in pairs:
            both = t_dot(left, right).astype(BF)
            axis = 0 if kind == "D" else 1
            own, sent = jnp.split(both, 2, axis)
            sums.append([lax.psum(v, "dp").astype(F32) for v in (own, swap(sent, "row"))])
        gate_up_grad = ordered(r, *[v.reshape(half, 2, hidden) for v in sums[0]], 2)
        qkv_grad = ordered(r, *[v.reshape(half, 3, units) for v in sums[1]], 2)
        out_grad = ordered(r, *sums[2])
        down_grad = ordered(r, *sums[3])
    return (
        result,
        input_grad,
        norms[0],
        norms[1],
        qkv_grad,
        bias_grad,
        out_grad,
        norms[2],
        norms[3],
        gate_up_grad,
        down_grad,
    )


def solution(mesh):
    in_specs = (
        P(("dp", "col"), "row"),
        P("dp", None),
        P("row"),
        P("row"),
        P("row", None, "col"),
        P(None, "col"),
        P("col", "row"),
        P("row"),
        P("row"),
        P("row", None, "col"),
        P("col", "row"),
        P(("dp", "col"), "row"),
    )
    out_specs = (
        P(("dp", "col"), "row"),
        P(("dp", "col"), "row"),
        P("row"),
        P("row"),
        P("row", None, "col"),
        P(None, "col"),
        P("col", "row"),
        P("row"),
        P("row"),
        P("row", None, "col"),
        P("col", "row"),
    )
    return jax.shard_map(local, mesh=mesh, in_specs=in_specs, out_specs=out_specs, check_vma=False)
```

```python
import functools
import math

import jax
import jax.numpy as jnp
from jax import lax
from jax.experimental import pallas as pl
from jax.experimental.pallas import tpu as pltpu
from jax.sharding import PartitionSpec as P

HEAD = 64
ROT = 16
EPSILON = 1e-05
ROPE_BASE = 10000.0
NEGATIVE = -1e30
BF = jnp.bfloat16
F32 = jnp.float32
SWAP = [(0, 1), (1, 0)]
MESH = pl.DeviceIdType.MESH


def swap(v, axis):
    return lax.ppermute(v, axis, SWAP)


def ordered(flag, mine, other, axis=0):
    first = jnp.where(flag == 0, mine, other)
    second = jnp.where(flag == 0, other, mine)
    return jnp.concatenate([first, second], axis=axis)


def piece(v, index, count, axis=0):
    size = v.shape[axis] // count
    return lax.dynamic_slice_in_dim(v, index * size, size, axis)


def add(a, b):
    return (a.astype(F32) + b.astype(F32)).astype(BF)


def dot(a, b):
    return jnp.dot(a, b, preferred_element_type=F32)


def dot_t(a, b):
    return lax.dot_general(a, b, (((1,), (1,)), ((), ())), preferred_element_type=F32)


def t_dot(a, b):
    return lax.dot_general(a, b, (((0,), (0,)), ((), ())), preferred_element_type=F32)


class Place:
    def __init__(self):
        self.r = lax.axis_index("row")
        self.c = lax.axis_index("col")
        self.d = lax.axis_index("dp")
        self.count = lax.axis_size("dp")
        self.y = lax.rem(self.d, 2)
        self.zp = lax.rem(self.d // 2, 2)
        self.z = self.d // 2
        self.mid = (self.z == 1) | (self.z == 2)
        self.upper = (self.z >= 2).astype(jnp.int32)


def dp_perm(bit, count):
    return [(i, i ^ bit) for i in range(count)]


def cross(v):
    half = v.shape[-1] // 2
    return jnp.concatenate([v[..., half:], v[..., :half]], axis=-1)


def gather_blocks(block, place):
    other = cross(swap(block, "row"))
    pair = ordered(place.r, block, other)
    rest = swap(pair, "col")
    return ordered(place.c, pair, rest)


def reduce_blocks(partial, place):
    kept = piece(partial, place.c, 2)
    got = swap(piece(partial, 1 - place.c, 2), "col")
    held = add(kept, got)
    kept = piece(held, place.r, 2)
    got = cross(swap(piece(held, 1 - place.r, 2), "row"))
    return kept.astype(F32) + got.astype(F32)


def norm_forward(values, gain, shift):
    count = values.shape[-1]
    mean = jnp.sum(values, axis=-1, keepdims=True) / count
    spread = jnp.sum(values * values, axis=-1, keepdims=True) / count - mean * mean
    inverse = lax.rsqrt(spread + EPSILON)
    normal = (values - mean) * inverse
    return normal * gain + shift, normal, inverse


def norm_backward(grad, normal, inverse, gain):
    count = grad.shape[-1]
    scaled = grad * gain
    first = jnp.sum(scaled, axis=-1, keepdims=True) / count
    second = jnp.sum(scaled * normal, axis=-1, keepdims=True) / count
    grad_input = inverse * (scaled - first - normal * second)
    return grad_input, jnp.sum(grad * normal, axis=0), jnp.sum(grad, axis=0)


def doc_positions(segment_ids):
    places = jnp.arange(segment_ids.shape[0], dtype=jnp.int32)
    starts = jnp.concatenate([jnp.ones((1,), dtype=bool), segment_ids[1:] != segment_ids[:-1]])
    first_place = lax.cummax(jnp.where(starts, places, jnp.zeros_like(places)), axis=0)
    return places - first_place


def rotary_tables(segment_ids):
    places = doc_positions(segment_ids).astype(F32)
    freq_index = jnp.arange(ROT // 2, dtype=F32)
    inverse = jnp.exp(freq_index * (-2.0 / ROT) * math.log(ROPE_BASE))
    angles = places[:, None] * inverse[None, :]
    return (jnp.cos(angles), jnp.sin(angles))


LONGEST = 512
QB = 256

def windows(length):
    for begin in range(0, length, QB):
        low = max(0, (begin - LONGEST + 1) // QB * QB)
        yield begin, low, begin + QB


def barred(starts, begin, low, end):
    shape = (end - begin, end - low)
    query = begin + lax.broadcasted_iota(jnp.int32, shape, 0)
    key = low + lax.broadcasted_iota(jnp.int32, shape, 1)
    return jnp.where((key <= query) & (key >= starts), 0.0, NEGATIVE)


def turned(v, table):
    width = v.shape[-1]
    return v * table[0] + pltpu.roll(v, width - 8, 1) * table[1] + pltpu.roll(v, 8, 1) * table[2]


def nt(a, b):
    return lax.dot_general(a, b, (((1,), (1,)), ((), ())), preferred_element_type=F32)


def tn(a, b):
    return lax.dot_general(a, b, (((0,), (0,)), ((), ())), preferred_element_type=F32)


def backward_kernel(q_ref, k_ref, v_ref, g_ref, att_ref, log_ref, starts_ref, table_ref, dq_ref, dk_ref, dv_ref, dk_acc, dv_acc):
    length = q_ref.shape[0]
    dk_acc[...] = jnp.zeros_like(dk_acc)
    dv_acc[...] = jnp.zeros_like(dv_acc)
    for begin, low, end in windows(length):
        bar = barred(starts_ref[begin:end], begin, low, end)
        outs, dks, dvs = [], [], []
        for h in range(2):
            lanes = slice(h * HEAD, (h + 1) * HEAD)
            q, k, v, g = q_ref[begin:end, lanes], k_ref[low:end, lanes], v_ref[low:end, lanes], g_ref[begin:end, lanes]
            weights = jnp.exp(nt(q, k) + bar - log_ref[0, begin:end, h : h + 1])
            dvs.append(tn(weights.astype(BF), g))
            inner = jnp.sum(g.astype(F32) * att_ref[begin:end, lanes].astype(F32), axis=1, keepdims=True)
            grads = (weights * (nt(g, v) - inner)).astype(BF)
            outs.append(jnp.dot(grads, k, preferred_element_type=F32))
            dks.append(tn(grads, q))
        table = (table_ref[0, begin:end], -table_ref[1, begin:end], -table_ref[2, begin:end])
        dq_ref[begin:end] = turned(jnp.concatenate(outs, axis=1) * HEAD ** (-0.5), table).astype(BF)
        dk_acc[low:end] += jnp.concatenate(dks, axis=1)
        dv_acc[low:end] += jnp.concatenate(dvs, axis=1)
    table = (table_ref[0], -table_ref[1], -table_ref[2])
    dk_ref[...] = turned(dk_acc[...], table).astype(BF)
    dv_ref[...] = dv_acc[...].astype(BF)


def tables(cosines, sines):
    length = cosines.shape[0]
    ones = jnp.ones((length, HEAD - 16), F32)
    none = jnp.zeros((length, HEAD - 8), F32)
    one = jnp.concatenate([cosines, cosines, ones], axis=1)
    ahead = jnp.concatenate([-sines, none], axis=1)
    behind = jnp.concatenate([none[:, :8], sines, none[:, 8:]], axis=1)
    return jnp.stack([jnp.concatenate([v, v], axis=1) for v in (one, ahead, behind)])


def attention_backward(queries, keys, values, grads, attended, logs, starts, table):
    length, units = queries.shape
    pairs = units // 128
    same = pl.BlockSpec((length, 128), lambda p: (0, p))
    half = jax.ShapeDtypeStruct((length, units), BF)
    return pl.pallas_call(
        backward_kernel,
        grid=(pairs,),
        in_specs=[same] * 5
        + [
            pl.BlockSpec((1, length, 2), lambda p: (p, 0, 0)),
            pl.BlockSpec((length, 1), lambda p: (0, 0)),
            pl.BlockSpec((3, length, 128), lambda p: (0, 0, 0)),
        ],
        out_specs=[same] * 3,
        out_shape=[half] * 3,
        scratch_shapes=[pltpu.VMEM((length, 128), F32)] * 2,
        compiler_params=pltpu.CompilerParams(vmem_limit_bytes=48 * 2**20),
        cost_estimate=pl.CostEstimate(flops=pairs * 2 * length * 640 * 640, bytes_accessed=8 * 2**20, transcendentals=pairs * 2 * length * 640),
    )(queries, keys, values, grads, attended, logs, starts, table)


BR = 512
BC = 256
SLOTS = 5
SEMAPHORES = 8


def back_kernel(
    bases,
    inner,
    cotangent,
    gate,
    up,
    act_two,
    attended,
    queries,
    keys,
    values,
    logs,
    starts_ref,
    table_ref,
    act_one,
    hidden_state,
    own_inputs,
    params_ref,
    w_down,
    w_gate,
    w_out,
    w_qkv,
    out_ref,
    res_own,
    res_got,
    grad_own,
    grad_got,
    norm_sums,
    bias_sums,
    turn,
    turn_in,
    joint,
    branch,
    pair,
    att,
    att_grad,
    heads,
    head_logs,
    key_sums,
    value_sums,
    down_rows,
    gate_in,
    down_columns,
    wide_w,
    w_o,
    sent,
    kept,
    core_in,
    row_src,
    row_in,
    acc_rows,
    grad_rows,
    hid,
    own,
    result,
    part,
    x_src,
    x_dst,
    y_dst,
    acc,
    e_dst,
    low,
    m_dst,
    full,
    f_dst,
    deep,
    n_dst,
    key,
    k_dst,
    whole,
    load_sem,
    once_sem,
    piece_sem,
    gather_sem,
    *sems,
):
    out_own, out_got = out_ref.at[0], out_ref.at[1]
    names = ("x", "y", "ei", "eo", "m", "g", "fi", "fo", "n", "k", "w")
    send = {k: sems[i] for i, k in enumerate(names)}
    recv = {k: sems[len(names) + i] for i, k in enumerate(names)}
    store_own, store_got = sems[2 * len(names)], sems[2 * len(names) + 1]

    length, width = branch.shape
    half, part_rows, block = width // 2, length // 2, length // 4
    hidden, units = pair.shape[1] // 2, att.shape[1]
    pairs = units // 128
    size = BR * BC // half
    segments = (hidden // size, half * 2 * hidden // (BR * BC), units // size, half * 3 * units // (BR * BC))
    total = sum(segments)
    firsts = [sum(segments[:i]) for i in range(4)]

    d, r, c = lax.axis_index("dp"), lax.axis_index("row"), lax.axis_index("col")
    y, z = lax.rem(d, 2), d // 2
    upper = d // 4
    mid = (z == 1) | (z == 2)
    outer = (z == 0) | (z == 3)
    x_peer, c_peer = {"row": 1 - r}, {"col": 1 - c}
    y_peer = {"dp": d + 1 - 2 * y}
    e_peer = {"dp": d + 2 - 4 * lax.rem(z, 2)}
    m_peer = {"dp": d + 2 - 4 * upper}

    def span(start, count):
        return pl.ds(pl.multiple_of(start, count), count)

    def local_copy(n, src, dst):
        return pltpu.make_async_copy(src, dst, load_sem.at[n])

    barrier = pltpu.get_barrier_semaphore()
    for peer in (x_peer, y_peer, e_peer, c_peer):
        pl.semaphore_signal(barrier, inc=1, device_id=peer, device_id_type=MESH)

    @pl.when(mid)
    def _():
        pl.semaphore_signal(barrier, inc=1, device_id=m_peer, device_id_type=MESH)

    own_block = span(c * part_rows + r * block, block)
    x_block = span(c * part_rows + (1 - r) * block, block)
    lo, hi = pl.ds(0, half), pl.ds(half, half)
    load_inner = local_copy(0, inner, joint.at[:, pl.ds(0, hidden)])
    load_cot = local_copy(1, cotangent, branch)
    load_hid = local_copy(2, hidden_state, hid)
    load_own = local_copy(3, cotangent.at[own_block], own)
    load_att = local_copy(4, attended, att)
    load_wo = local_copy(5, w_out, w_o)
    load_inputs = local_copy(6, own_inputs, own)

    def down_rows_load(i):
        s = lax.rem(i, 2)
        at = span(i * 128, 128)
        return (
            pltpu.make_async_copy(w_down.at[at], down_rows.at[s], once_sem.at[s]),
            pltpu.make_async_copy(gate.at[:, at], gate_in.at[s, 0], once_sem.at[2 + s]),
            pltpu.make_async_copy(up.at[:, at], gate_in.at[s, 1], once_sem.at[4 + s]),
        )

    def order(i):
        return lax.rem(i, 2) * (half // BC) + i // 2

    def down_columns_load(i):
        s = lax.rem(i, 2)
        return (pltpu.make_async_copy(w_down.at[:, span(order(i) * BC, BC)], down_columns.at[s], once_sem.at[6 + s]),)

    def gate_load(i):
        s = lax.rem(i, 2)
        return (pltpu.make_async_copy(w_gate.at[:, span(order(i) * BC, BC)], wide_w.at[s], once_sem.at[8 + s]),)

    def qkv_load(i):
        s = lax.rem(i, 2)
        rows = span(order(i) * BC, BC)
        return tuple(
            pltpu.make_async_copy(
                w_qkv.at[k, rows], wide_w.at[s, k // 2, :, pl.ds(k % 2 * units, units)], once_sem.at[10 + 2 * k + s]
            )
            for k in range(3)
        )

    def heads_load(p):
        s = lax.rem(p, 2)
        lanes = span(p * 128, 128)
        return tuple(
            pltpu.make_async_copy(ref.at[:, lanes], heads.at[s, k], once_sem.at[16 + 2 * k + s])
            for k, ref in enumerate((queries, keys, values))
        ) + (pltpu.make_async_copy(logs.at[p], head_logs.at[s], once_sem.at[22 + s]),)

    def turn_load(source, i):
        return tuple(
            local_copy(7 + side, source.at[:, span(side * half + i * BR, BR)], turn_in.at[side]) for side in range(2)
        )

    def start(copies):
        for copy in copies:
            copy.start()

    def wait(copies):
        for copy in copies:
            copy.wait()

    start((load_inner, load_cot, load_hid, load_own, load_att, load_wo))
    start(down_rows_load(0))
    start(down_columns_load(0))
    start(turn_load(act_two, 0))

    @pl.when(mid)
    def _():
        pl.semaphore_wait(barrier, 5)

    @pl.when(outer)
    def _():
        pl.semaphore_wait(barrier, 4)

    rows = BR // 2

    def halves(index):
        return span(index * rows, rows)

    def slot(u):
        return lax.rem(u, SLOTS)

    def copy(name, u, src, dst, peer):
        s = lax.rem(u, SEMAPHORES)
        return pltpu.make_async_remote_copy(
            src_ref=src,
            dst_ref=dst,
            send_sem=send[name].at[s],
            recv_sem=recv[name].at[s],
            device_id=peer,
            device_id_type=MESH,
        )

    def spot(u):
        place = u
        for first, base in zip(firsts, bases):
            place = jnp.where(u >= first, u + (base - first), place)
        return place

    def out_half(ref, u, index):
        return ref.at[spot(u), halves(index)]

    def x_copy(u):
        return copy("x", u, x_src.at[slot(u)], x_dst.at[slot(u)], x_peer)

    def y_copy(u):
        return copy("y", u, part.at[slot(u), halves(1 - y)], y_dst.at[slot(u)], y_peer)

    def e_in(u):
        return copy("ei", u, acc.at[slot(u)], e_dst.at[slot(u)], e_peer)

    def e_out(u):
        return copy("eo", u, full.at[slot(u)], e_dst.at[slot(u)], e_peer)

    def m_copy(u):
        return copy("m", u, low.at[slot(u)], m_dst.at[slot(u)], m_peer)

    def g_mid(u):
        return copy("g", u, full.at[slot(u)], out_half(out_own, u, y), y_peer)

    def g_out(u):
        return copy("g", u, e_dst.at[slot(u)], out_half(out_own, u, y), y_peer)

    def f_in(u):
        return copy("fi", u, x_dst.at[slot(u)], f_dst.at[slot(u)], e_peer)

    def f_out(u):
        return copy("fo", u, whole.at[slot(u)], out_got.at[spot(u)], e_peer)

    def n_copy(u):
        return copy("n", u, deep.at[slot(u), halves(1 - upper)], n_dst.at[slot(u)], m_peer)

    def k_copy(u):
        return copy("k", u, key.at[slot(u)], k_dst.at[slot(u)], y_peer)

    def w_copy(u):
        place = whole.at[slot(u), halves(upper)]
        return copy("w", u, place, place, m_peer)

    def keep_own(u, src):
        return pltpu.make_async_copy(src, out_half(out_own, u, y), store_own.at[slot(u)])

    def keep_got(u):
        return pltpu.make_async_copy(whole.at[slot(u)], out_got.at[spot(u)], store_got.at[slot(u)])

    def stage(u, fn, role=None):
        ok = (u >= 0) & (u < total)
        if role is not None:
            ok = ok & role

        @pl.when(ok)
        def _():
            fn(u)

    def within(t, first, count, fn):
        @pl.when((t >= first) & (t < first + count))
        def _():
            fn(t - first)

    def unit_block(k, s, lhs, rhs):
        left = lhs[:, span(k * size, size)].T
        for side, ref in ((1, x_src), (0, part)):
            for q in range(half // BC):
                right = rhs[:, side * half + q * BC : side * half + (q + 1) * BC]
                ref[s, q * size : (q + 1) * size] = jnp.dot(left, right, preferred_element_type=F32).astype(BF)

    def feature_block(k, s, rhs, source, following):
        columns = rhs.shape[1] // BC

        for i in range(half // BR):

            @pl.when(k == i * columns)
            def _(i=i):
                wait(turn_load(source, i))
                for side in range(2):
                    turn[side] = turn_in[side].T
                following_load = following if i + 1 == half // BR else (source, i + 1)
                if following_load is not None:
                    start(turn_load(*following_load))

        right = rhs[:, span(lax.rem(k, columns) * BC, BC)]
        for side, ref in ((1, x_src), (0, part)):
            ref[s] = jnp.dot(turn[side], right, preferred_element_type=F32).astype(BF)

    def produce(u):
        s = slot(u)

        @pl.when(u == 0)
        def _():
            wait((load_inner, load_cot))

        within(u, firsts[0], segments[0], lambda k: unit_block(k, s, joint, branch))
        within(u, firsts[1], segments[1], lambda k: feature_block(k, s, pair, act_two, (act_one, 0)))
        within(u, firsts[2], segments[2], lambda k: unit_block(k, s, att, branch))
        within(u, firsts[3], segments[3], lambda k: feature_block(k, s, joint, act_one, None))
        x_copy(u).start()
        y_copy(u).start()

    def t1_a(u):
        s = slot(u)
        y_copy(u).wait_recv()
        acc[s] = part[s, halves(y)] + y_dst[s]
        pl.when(outer)(lambda: e_in(u).start())

    def t1_b(u):
        s = slot(u)
        e_in(u).wait_recv()
        low[s] = acc[s] + e_dst[s]
        m_copy(u).start()

    def t1_c(u):
        s = slot(u)
        m_copy(u).wait_recv()
        full[s] = low[s] + m_dst[s]
        e_out(u).start()
        g_mid(u).start()
        keep_own(u, full.at[s]).start()

    def t1_d(u):
        e_out(u).wait_recv()
        g_out(u).start()
        keep_own(u, e_dst.at[slot(u)]).start()

    def t2_a(u):
        x_copy(u).wait_recv()
        pl.when(outer)(lambda: f_in(u).start())

    def t2_b(u):
        s = slot(u)
        f_in(u).wait_recv()
        deep[s] = x_dst[s] + f_dst[s]
        n_copy(u).start()

    def t2_c(u):
        s = slot(u)
        n_copy(u).wait_recv()
        key[s] = deep[s, halves(upper)] + n_dst[s]
        k_copy(u).start()

    def t2_d(u):
        s = slot(u)
        k_copy(u).wait_recv()
        whole[s, halves(upper)] = key[s] + k_dst[s]
        w_copy(u).start()

    def t2_e(u):
        w_copy(u).wait_recv()
        f_out(u).start()
        keep_got(u).start()

    pieces = width // BC
    own_part, far_part = c * part_rows, (1 - c) * part_rows

    def core_copy(n):
        s = lax.rem(n, 3)
        return pltpu.make_async_remote_copy(
            src_ref=sent.at[s],
            dst_ref=core_in.at[s],
            send_sem=piece_sem.at[s],
            recv_sem=piece_sem.at[3 + s],
            device_id=c_peer,
            device_id_type=MESH,
        )

    def row_copy(n):
        s = lax.rem(n, 4)
        return pltpu.make_async_remote_copy(
            src_ref=row_src.at[s],
            dst_ref=row_in.at[s],
            send_sem=piece_sem.at[6 + s],
            recv_sem=piece_sem.at[10 + s],
            device_id=x_peer,
            device_id_type=MESH,
        )

    def sum_piece(n, product):
        s = lax.rem(n, 3)
        sent[s] = product(span(far_part, part_rows)).astype(BF)
        core_copy(n).start()
        kept[s] = product(span(own_part, part_rows)).astype(BF)

    def sum_core(n, i):
        s, q = lax.rem(n, 3), lax.rem(n, 4)
        core_copy(n).wait_recv()
        core_copy(n).wait_send()
        far, near = span((1 - r) * block, block), span(r * block, block)
        row_src[q] = kept[s, far] + core_in[s, far]
        row_copy(n).start()
        acc_rows[:, span(order(i) * BC, BC)] = kept[s, near].astype(F32) + core_in[s, near].astype(F32)

    def sum_row(n, i):
        q = lax.rem(n, 4)
        row_copy(n).wait_recv()
        row_copy(n).wait_send()
        partner = lax.rem(order(i) + half // BC, pieces)
        cols = span(partner * BC, BC)
        acc_rows[:, cols] = acc_rows[:, cols] + row_in[q].astype(F32)

    def summed(t, first, base, product, load, wait_for=None):
        within(t, first + 3, pieces, lambda i: sum_row(base + i, i))
        within(t, first + 1, pieces, lambda i: sum_core(base + i, i))

        def task(i):
            if wait_for is not None:
                pl.when(i == 0)(lambda: wait(wait_for))
            pl.when(i + 1 < pieces)(lambda: start(load(i + 1)))
            wait(load(i))
            sum_piece(base + i, lambda at: product(lax.rem(i, 2), at))

        within(t, first, pieces, task)

    def feed_product(s, at):
        return jnp.dot(joint[at, :hidden], down_columns[s], preferred_element_type=F32)

    def act_two_product(s, at):
        return nt(pair[at, :hidden], wide_w[s, 0]) + nt(pair[at, hidden:], wide_w[s, 1])

    def act_one_product(s, at):
        out = nt(joint[at, :units], wide_w[s, 0, :, :units])
        out = out + nt(joint[at, units : 2 * units], wide_w[s, 0, :, units : 2 * units])
        return out + nt(joint[at, 2 * units :], wide_w[s, 1, :, :units])

    def gate_task(i):
        s = lax.rem(i, 2)

        @pl.when(i + 1 < hidden // 128)
        def _():
            start(down_rows_load(i + 1))

        wait(down_rows_load(i))

        def some(j, carry):
            at = span(j * 256, 256)
            grad = nt(branch[at], down_rows[s])
            g, u = gate_in[s, 0, at].astype(F32), gate_in[s, 1, at].astype(F32)
            rate = 1.0 / (1.0 + jnp.exp(-g))
            pair[at, span(i * 128, 128)] = (grad * u * (rate * (1.0 + g * (1.0 - rate)))).astype(BF)
            pair[at, span(hidden + i * 128, 128)] = (grad * (g * rate)).astype(BF)
            return carry

        lax.fori_loop(0, length // 256, some, 0)

    def result_copy():
        return pltpu.make_async_remote_copy(
            src_ref=result.at[:, hi],
            dst_ref=res_got,
            send_sem=gather_sem.at[0],
            recv_sem=gather_sem.at[1],
            device_id=x_peer,
            device_id_type=MESH,
        )

    store_result = local_copy(9, result.at[:, lo], res_own)

    def result_task(i):
        load_hid.wait()
        load_own.wait()
        result[...] = (hid[...] + acc_rows[...]).astype(BF)
        result_copy().start()
        store_result.start()

    chunk = 64
    chunks = block // chunk

    def norm_rows(values, at, grads, gain):
        mean = jnp.sum(values, axis=1, keepdims=True) / width
        spread_of = jnp.sum(values * values, axis=1, keepdims=True) / width - mean * mean
        inverse = lax.rsqrt(spread_of + EPSILON)
        normal = (values - mean) * inverse
        scaled = grads * gain
        terms = grads * normal
        first = jnp.sum(scaled, axis=1, keepdims=True) / width
        second = jnp.sum(terms * gain, axis=1, keepdims=True) / width
        return inverse * (scaled - first - normal * second), terms

    def gather_copies(i):
        at = span(c * part_rows + r * block + i * chunk, chunk)

        def one(n, src, dst, peer):
            return pltpu.make_async_remote_copy(
                src_ref=src,
                dst_ref=dst,
                send_sem=gather_sem.at[2 + 2 * (n * chunks + i)],
                recv_sem=gather_sem.at[3 + 2 * (n * chunks + i)],
                device_id=peer,
                device_id_type=MESH,
            )

        got = span(c * part_rows + (1 - r) * block + i * chunk, chunk)
        return (
            one(0, branch.at[at, lo], branch.at[at, hi], x_peer),
            one(1, branch.at[at, hi], branch.at[at, lo], x_peer),
            one(2, branch.at[at], branch.at[at], c_peer),
            one(3, branch.at[got], branch.at[got], c_peer),
        )

    def norm_two_task(i):
        at = span(i * chunk, chunk)
        grads = acc_rows[at]
        grad, terms = norm_rows(hid[at], at, grads, params_ref[2:3])
        norm_sums[2:3] = norm_sums[2:3] + jnp.sum(terms, axis=0, keepdims=True)
        norm_sums[3:4] = norm_sums[3:4] + jnp.sum(grads, axis=0, keepdims=True)
        grad = own[at].astype(F32) + grad
        grad_rows[at] = grad
        branch[span(c * part_rows + r * block + i * chunk, chunk)] = grad.astype(BF)
        start(gather_copies(i)[:3])

    def forward_task(i):
        copies = gather_copies(i)
        copies[0].wait_recv()
        copies[1].wait_recv()
        copies[3].start()

    def gathered_task(i):
        copies = gather_copies(i)
        copies[2].wait_recv()
        copies[3].wait_recv()
        for one in copies:
            one.wait_send()

    def att_grad_task(i):
        at = span(i * part_rows, part_rows)
        att_grad[at] = nt(branch[at], w_o[...]).astype(BF)

    def attention_task(i):
        p, second = i // 2, lax.rem(i, 2)
        s = lax.rem(p, 2)
        lanes0 = span(p * 128, 128)

        @pl.when(second == 0)
        def _():
            pl.when(p + 1 < pairs)(lambda: start(heads_load(p + 1)))
            wait(heads_load(p))
            key_sums[...] = jnp.zeros_like(key_sums)
            value_sums[...] = jnp.zeros_like(value_sums)

        def window(begin, low, end):
            bar = barred(starts_ref[begin:end], begin, low, end)
            q2, k2, v2 = heads[s, 0, begin:end], heads[s, 1, low:end], heads[s, 2, low:end]
            g2, a2 = att_grad[begin:end, lanes0], att[begin:end, lanes0]
            outs, dks, dvs = [], [], []
            for h in range(2):
                lanes = slice(h * HEAD, (h + 1) * HEAD)
                q, k, v, g = q2[:, lanes], k2[:, lanes], v2[:, lanes], g2[:, lanes]
                weights = jnp.exp(nt(q, k) + bar - head_logs[s, begin:end, h : h + 1])
                dvs.append(tn(weights.astype(BF), g))
                inside = jnp.sum(g.astype(F32) * a2[:, lanes].astype(F32), axis=1, keepdims=True)
                grads = (weights * (nt(g, v) - inside)).astype(BF)
                outs.append(jnp.dot(grads, k, preferred_element_type=F32))
                dks.append(tn(grads, q))
            table = (table_ref[0, begin:end], -table_ref[1, begin:end], -table_ref[2, begin:end])
            dq = turned(jnp.concatenate(outs, axis=1) * HEAD ** (-0.5), table).astype(BF)
            joint[begin:end, lanes0] = dq
            bias_sums[0:1, lanes0] = bias_sums[0:1, lanes0] + jnp.sum(dq.astype(F32), axis=0, keepdims=True)
            key_sums[low:end] += jnp.concatenate(dks, axis=1)
            value_sums[low:end] += jnp.concatenate(dvs, axis=1)

        spans = list(windows(length))
        middle = len(spans) // 2

        @pl.when(second == 0)
        def _():
            for one in spans[:middle]:
                window(*one)

        @pl.when(second == 1)
        def _():
            for one in spans[middle:]:
                window(*one)
            table = (table_ref[0], -table_ref[1], -table_ref[2])
            dk = turned(key_sums[...], table).astype(BF)
            dv = value_sums[...].astype(BF)
            for k, v in ((1, dk), (2, dv)):
                joint[:, span(k * units + p * 128, 128)] = v
                bias_sums[k : k + 1, lanes0] = jnp.sum(v.astype(F32), axis=0, keepdims=True)

    def grad_copies(i):
        at = span(i * chunk, chunk)
        n = 2 + 8 * chunks + 2 * i
        return (
            pltpu.make_async_remote_copy(
                src_ref=grad_rows.at[at, hi],
                dst_ref=grad_got.at[at],
                send_sem=gather_sem.at[n],
                recv_sem=gather_sem.at[n + 1],
                device_id=x_peer,
                device_id_type=MESH,
            ),
            local_copy(10 + i, grad_rows.at[at, lo], grad_own.at[at]),
        )

    def norm_one_task(i):
        pl.when(i == 0)(lambda: load_inputs.wait())
        at = span(i * chunk, chunk)
        grads = acc_rows[at]
        grad, terms = norm_rows(own[at].astype(F32), at, grads, params_ref[0:1])
        norm_sums[0:1] = norm_sums[0:1] + jnp.sum(terms, axis=0, keepdims=True)
        norm_sums[1:2] = norm_sums[1:2] + jnp.sum(grads, axis=0, keepdims=True)
        grad_rows[at] = grad_rows[at] + grad
        start(grad_copies(i))

    norm_sums[...] = jnp.zeros_like(norm_sums)
    bias_sums[...] = jnp.zeros_like(bias_sums)
    gates = hidden // 128
    at_two = max(gates, pieces + 3)
    at_norm = at_two + pieces + 3
    at_att = at_norm + chunks // 2 + 3
    at_heads = at_att + 2
    at_one = at_heads + 2 * pairs
    at_last = at_one + pieces + 3

    def tasks(t):
        within(t, 0, gates, gate_task)
        summed(t, 0, 0, feed_product, down_columns_load)
        within(t, at_two, 1, result_task)
        pl.when(t == at_two - 1)(lambda: start(gate_load(0)))
        summed(t, at_two, pieces, act_two_product, gate_load)

        def two(task):
            def both(i):
                task(2 * i)
                task(2 * i + 1)

            return both

        within(t, at_norm + 3, chunks // 2, two(gathered_task))
        within(t, at_norm + 2, chunks // 2, two(forward_task))
        within(t, at_norm, chunks // 2, two(norm_two_task))

        @pl.when(t == at_att)
        def _():
            load_wo.wait()
            load_att.wait()
            load_inputs.start()
            start(heads_load(0))

        within(t, at_att, 2, att_grad_task)
        within(t, at_heads, 2 * pairs, attention_task)
        pl.when(t == at_one - 1)(lambda: start(qkv_load(0)))
        summed(t, at_one, 2 * pieces, act_one_product, qkv_load)
        within(t, at_last, chunks // 2, two(norm_one_task))

    def body(t, carry):
        def free_all(u):
            x_copy(u).wait_send()
            y_copy(u).wait_send()

        def free_mid(u):
            m_copy(u).wait_send()
            n_copy(u).wait_send()

        def free_out(u):
            e_out(u).wait_send()
            g_mid(u).wait_send()
            keep_own(u, full.at[slot(u)]).wait()

        def free_far(u):
            g_out(u).wait_send()
            keep_own(u, e_dst.at[slot(u)]).wait()

        def free_got(u):
            f_out(u).wait_send()
            keep_got(u).wait()

        stage(t - 2, free_all)
        stage(t - 3, lambda u: e_in(u).wait_send(), outer)
        stage(t - 3, lambda u: f_in(u).wait_send(), outer)
        stage(t - 4, free_mid, mid)
        stage(t - 5, lambda u: k_copy(u).wait_send(), mid)
        stage(t - 6, lambda u: w_copy(u).wait_send(), mid)
        stage(t - 5, free_out, mid)
        stage(t - 5, free_far, outer)
        stage(t - 7, free_got, mid)
        stage(t - 5, lambda u: g_mid(u).wait_recv(), mid)
        stage(t - 6, lambda u: g_out(u).wait_recv(), outer)
        stage(t - 7, lambda u: f_out(u).wait_recv(), outer)
        stage(t - 5, t2_e, mid)
        stage(t - 4, t2_d, mid)
        stage(t - 3, t2_c, mid)
        stage(t - 2, t2_b, mid)
        stage(t - 1, t2_a)
        stage(t - 4, t1_d, outer)
        stage(t - 3, t1_c, mid)
        stage(t - 2, t1_b, mid)
        stage(t - 1, t1_a)
        stage(t, produce)
        tasks(t)
        return carry

    lax.fori_loop(0, max(total + 8, at_last + chunks // 2), body, 0)
    result_copy().wait()
    store_result.wait()
    for i in range(chunks):
        wait(grad_copies(i))


def back(
    inner,
    cotangent,
    gate,
    up,
    act_two,
    attended,
    queries,
    keys,
    values,
    logs,
    starts,
    table,
    act_one,
    hidden_state,
    own_inputs,
    params,
    w_down,
    w_gate,
    w_out,
    w_qkv,
):
    length, width = cotangent.shape
    hidden, units = inner.shape[1], attended.shape[1]
    half, part_rows, block = width // 2, length // 2, length // 4
    area, chunks = BR * BC, block // 64
    counts = [hidden * half // area, half * 2 * hidden // area, units * half // area, half * 3 * units // area]
    bases, end = [], 0
    for blocks in counts:
        bases.append(-(-end // blocks) * blocks)
        end = bases[-1] + blocks

    def bf(*shape):
        return jax.ShapeDtypeStruct(shape, BF)

    def f32(*shape):
        return jax.ShapeDtypeStruct(shape, F32)

    outs = [
        bf(2, end, BR, BC),
        bf(block, half),
        bf(block, half),
        f32(block, half),
        f32(block, half),
        f32(8, width),
        f32(8, units),
    ]
    any_spec, vmem_spec = pl.BlockSpec(memory_space=pl.ANY), pl.BlockSpec(memory_space=pltpu.VMEM)
    wide, thin = bf(SLOTS, BR, BC), bf(SLOTS, BR // 2, BC)
    scratch = [
        bf(2, BR, length),
        bf(2, length, BR),
        bf(length, max(hidden, 3 * units)),
        bf(length, width),
        bf(length, 2 * hidden),
        bf(length, units),
        bf(length, units),
        bf(2, 3, length, 128),
        f32(2, length, 2),
        f32(length, 128),
        f32(length, 128),
        bf(2, 128, width),
        bf(2, 2, length, 128),
        bf(2, hidden, BC),
        bf(2, 2, BC, max(hidden, 2 * units)),
        bf(units, width),
        bf(3, part_rows, BC),
        bf(3, part_rows, BC),
        bf(3, part_rows, BC),
        bf(4, block, BC),
        bf(4, block, BC),
        f32(block, width),
        f32(block, width),
        f32(block, width),
        bf(block, width),
        bf(block, width),
        wide,
        wide,
        wide,
        thin,
        thin,
        thin,
        thin,
        thin,
        thin,
        wide,
        wide,
        thin,
        thin,
        thin,
        wide,
    ]
    dma = pltpu.SemaphoreType.DMA
    flops = 2 * length * width * (8 * units + 6 * hidden) + 2 * length * 640 * 5 * units
    outs = pl.pallas_call(
        functools.partial(back_kernel, bases),
        out_shape=outs,
        in_specs=[any_spec] * 10 + [vmem_spec] * 2 + [any_spec] * 3 + [vmem_spec] + [any_spec] * 4,
        out_specs=[any_spec] * 5 + [vmem_spec] * 2,
        scratch_shapes=[pltpu.VMEM(v.shape, v.dtype) for v in scratch]
        + [dma((10 + chunks,)), dma((24,)), dma((14,)), dma((2 + 10 * chunks,))]
        + [dma((SEMAPHORES,))] * 22
        + [dma((SLOTS,))] * 2,
        compiler_params=pltpu.CompilerParams(
            collective_id=1, has_side_effects=True, vmem_limit_bytes=63 * 2**20
        ),
        cost_estimate=pl.CostEstimate(flops=flops, bytes_accessed=200 * 2**20, transcendentals=length * 8192),
    )(
        inner,
        cotangent,
        gate,
        up,
        act_two,
        attended,
        queries,
        keys,
        values,
        logs,
        starts,
        table,
        act_one,
        hidden_state,
        own_inputs,
        params,
        w_down,
        w_gate,
        w_out,
        w_qkv,
    )
    return outs[0], bases, *outs[1:]


def spread_qkv_kernel(side_ref, block_ref, out_ref):
    per = out_ref.shape[2] // BC
    for j in range(block_ref.shape[1]):
        at = j % per * BC
        out_ref[j // per, :, at : at + BC] = block_ref[0, j].astype(F32)


def spread_pair_kernel(side_ref, block_ref, out_ref):
    units = out_ref.shape[2]
    for j in range(block_ref.shape[1]):
        for at in range(0, BC, 128):
            unit = j * BC + at
            out_ref[:, unit // units, unit % units : unit % units + 128] = block_ref[
                0, j, :, at : at + 128
            ].astype(F32)


def spread_rows_kernel(side_ref, block_ref, out_ref):
    size = block_ref.shape[2]
    for k in range(block_ref.shape[1]):
        out_ref[k * size : (k + 1) * size] = block_ref[0, k].astype(F32)


def spread(body, side, blocks, steps, in_spec, out_spec, out_shape):
    return pl.pallas_call(
        body,
        grid_spec=pltpu.PrefetchScalarGridSpec(
            num_scalar_prefetch=1, grid=(2, steps), in_specs=[in_spec], out_specs=out_spec
        ),
        out_shape=jax.ShapeDtypeStruct(out_shape, F32),
        compiler_params=pltpu.CompilerParams(vmem_limit_bytes=48 * 2**20),
    )(side, blocks)


def place_of(which, side_ref):
    return which + side_ref[0] - 2 * which * side_ref[0]


def spread_columns(side, blocks, base, half, units, kinds, rows):
    columns, per = kinds * units // BC, BR // rows
    first = base // columns
    in_spec = pl.BlockSpec(
        (1, columns, rows, BC), lambda w, i, s: (w, first + i // per, i % per, 0)
    )
    if kinds == 3:
        return spread(
            spread_qkv_kernel,
            side,
            blocks,
            half // rows,
            in_spec,
            pl.BlockSpec((3, rows, units), lambda w, i, s: (0, i, place_of(w, s))),
            (3, half, 2 * units),
        ).transpose(1, 0, 2)
    return spread(
        spread_pair_kernel,
        side,
        blocks,
        half // rows,
        in_spec,
        pl.BlockSpec((rows, 2, units), lambda w, i, s: (i, 0, place_of(w, s))),
        (half, 2, 2 * units),
    )


def spread_rows(side, blocks, base, half, units):
    size = BR * BC // half
    count = units // size
    return spread(
        spread_rows_kernel,
        side,
        blocks,
        half // BC,
        pl.BlockSpec((1, count, size, BC), lambda w, q, s: (w, base // count, q, 0)),
        pl.BlockSpec((units, BC), lambda w, q, s: (place_of(w, s), q)),
        (2 * units, half),
    )


def front_kernel(
    tokens,
    starts_ref,
    table_ref,
    params_ref,
    bias_ref,
    qkv_w,
    out_w,
    gate_w,
    down_w,
    cotangent,
    act_one,
    q_out,
    k_out,
    v_out,
    att_out,
    log_out,
    hid_out,
    act_two,
    gate_out,
    up_out,
    inner_out,
    wq_out,
    wo_out,
    wg_out,
    wd_out,
    cot_out,
    own_out,
    tok,
    act,
    wq,
    wo,
    wg,
    gate_far,
    gate_own,
    qs,
    ks,
    vs,
    att,
    logs,
    core_in,
    row_src,
    row_in,
    own_in,
    hid,
    tile,
    send_sem,
    recv_sem,
    load_sem,
    store_sem,
):
    r, c, d = lax.axis_index("row"), lax.axis_index("col"), lax.axis_index("dp")
    y, zp = lax.rem(d, 2), lax.rem(d // 2, 2)
    length, width = tok.shape
    half = width // 2
    part, block = length // 2, length // 4
    units, hidden = qs.shape[1], wg.shape[2]
    sub = zp * 2 + y
    dy, dz = 1 - 2 * y, 2 - 4 * zp
    row_peer, col_peer = {"row": 1 - r}, {"col": 1 - c}
    near = ({"dp": d + dy}, {"dp": d + dz}, {"dp": d + dy + dz})

    barrier = pltpu.get_barrier_semaphore()
    for peer in (row_peer, col_peer) + near:
        pl.semaphore_signal(barrier, inc=1, device_id=peer, device_id_type=MESH)

    stores = []

    def span(start, size):
        return pl.ds(pl.multiple_of(start, size), size)

    def load(n, src, dst):
        copy = pltpu.make_async_copy(src, dst, load_sem.at[n])
        copy.start()
        return copy

    def store(src, dst):
        copy = pltpu.make_async_copy(src, dst, store_sem.at[len(stores)])
        copy.start()
        stores.append(copy)
        return copy

    def remote(n, src, dst, peer):
        return pltpu.make_async_remote_copy(
            src_ref=src,
            dst_ref=dst,
            send_sem=send_sem.at[n],
            recv_sem=recv_sem.at[n],
            device_id=peer,
            device_id_type=MESH,
        )

    mine, theirs = span(r * units, units), span((1 - r) * units, units)
    own_rows, far_rows = span(c * part, part), span((1 - c) * part, part)
    lo, hi = pl.ds(0, half), pl.ds(half, half)
    quarter, eighth = half // 4, half // 8
    down_quarter = hidden // 4

    load_tok = load(0, tokens, tok.at[own_rows, lo])
    load_q = load(1, qkv_w.at[:, :, mine], wq.at[:, lo])
    load_o = load(2, out_w.at[mine], wo.at[:, lo])
    gate_cols = span(r * hidden, hidden)

    def load_gate(i):
        return load(3 + i % 2, gate_w.at[pl.ds(i * eighth, eighth), :, gate_cols], gate_own.at[i % 2])

    load_d = load(5, down_w.at[span(r * hidden, hidden)], wd_out.at[:, lo])
    load_c = load(6, cotangent, cot_out.at[own_rows, lo])
    gates = [load_gate(0), load_gate(1)]

    rows_sub = span(sub * quarter, quarter)
    rows_far = span(half + sub * quarter, quarter)
    q_x = remote(0, qkv_w.at[:, rows_sub, theirs], wq.at[:, rows_far], row_peer)
    q_n = [remote(1 + k, wq.at[:, rows_far], wq.at[:, rows_far], p) for k, p in enumerate(near)]
    tok_x = remote(4, tokens, tok.at[own_rows, hi], row_peer)
    tok_c = remote(5, tokens, tok.at[own_rows, lo], col_peer)
    tok_f = remote(6, tok.at[own_rows, hi], tok.at[own_rows, hi], col_peer)
    out_rows = units // 4
    out_sub = span(sub * out_rows, out_rows)
    o_x = remote(
        7, out_w.at[span((1 - r) * units + sub * out_rows, out_rows)], wo.at[out_sub, hi], row_peer
    )
    o_n = [remote(8 + k, wo.at[out_sub, hi], wo.at[out_sub, hi], p) for k, p in enumerate(near)]
    g_x = remote(
        11, gate_w.at[rows_sub, :, span((1 - r) * hidden, hidden)], gate_far.at[sub], row_peer
    )
    g_n = [remote(12 + k, gate_far.at[sub], gate_far.at[sub], p) for k, p in enumerate(near)]
    down_sub = span(sub * down_quarter, down_quarter)
    d_x = remote(
        15,
        down_w.at[span((1 - r) * hidden + sub * down_quarter, down_quarter)],
        wd_out.at[down_sub, hi],
        row_peer,
    )
    d_n = [
        remote(16 + k, wd_out.at[down_sub, hi], wd_out.at[down_sub, hi], p)
        for k, p in enumerate(near)
    ]
    c_x = remote(19, cotangent, cot_out.at[own_rows, hi], row_peer)
    c_c = remote(20, cotangent, cot_out.at[own_rows, lo], col_peer)
    c_f = remote(21, cot_out.at[own_rows, hi], cot_out.at[own_rows, hi], col_peer)
    rs_c = remote(22, act.at[far_rows], core_in, col_peer)
    rs_x = remote(23, row_src, row_in, row_peer)
    own_block = span(c * part + r * block, block)
    x_block = span(c * part + (1 - r) * block, block)
    ag_x = [
        remote(24, tok.at[own_block, lo], tok.at[own_block, hi], row_peer),
        remote(25, tok.at[own_block, hi], tok.at[own_block, lo], row_peer),
    ]
    ag_c = remote(26, tok.at[own_block], tok.at[own_block], col_peer)
    ag_f = remote(27, tok.at[x_block], tok.at[x_block], col_peer)

    def start(copies):
        for copy in copies:
            copy.start()

    def arrived(copies):
        for copy in copies:
            copy.wait_recv()

    def part_gate(ref, at):
        wg[0, at] = ref[:, 0, :]
        wg[1, at] = ref[:, 1, :]

    pl.semaphore_wait(barrier, 5)
    q_x.start()
    tok_c.start()
    c_c.start()
    for i in range(8):
        if i == 4:
            q_x.wait_recv()
            start(q_n)
            tok_x.start()
        gates[i].wait()
        part_gate(gate_own.at[i % 2], pl.ds(i * eighth, eighth))
        if i + 2 < 8:
            gates.append(load_gate(i + 2))
    tok_x.wait_recv()
    tok_f.start()
    o_x.start()
    g_x.start()

    load_tok.wait()
    tok_c.wait_recv()

    def normed(v, at):
        mean = jnp.sum(v, axis=1, keepdims=True) / width
        spread_of = jnp.sum(v * v, axis=1, keepdims=True) / width - mean * mean
        v = (v - mean) * lax.rsqrt(spread_of + EPSILON)
        return (v * params_ref[at : at + 1] + params_ref[at + 1 : at + 2]).astype(BF)

    norm_rows = 64

    def norm_one(base):
        def body(i, carry):
            at = span(base + i * norm_rows, norm_rows)
            act[at] = normed(tok[at].astype(F32), 0)
            return carry

        lax.fori_loop(0, part // norm_rows, body, 0)

    norm_one(c * part)
    own_in[...] = tok[own_block]
    tok_f.wait_recv()
    norm_one((1 - c) * part)
    store(act, act_one)
    store(own_in, own_out)

    load_q.wait()
    arrived(q_n)
    o_x.wait_recv()
    start(o_n)
    store(wq, wq_out)
    chunk = 256

    def project(i, carry):
        at = span(i * chunk, chunk)
        rows = act[at]
        for kind, ref in enumerate((qs, ks, vs)):
            out = jnp.dot(rows, wq[kind], preferred_element_type=F32) + bias_ref[kind : kind + 1]
            if kind == 2:
                ref[at] = out.astype(BF)
                continue
            table = (table_ref[0, at], table_ref[1, at], table_ref[2, at])
            for g in range(units // 128):
                lanes = slice(g * 128, (g + 1) * 128)
                v = turned(out[:, lanes], table).astype(BF)
                if kind == 0:
                    v = (v.astype(F32) * HEAD ** (-0.5)).astype(BF)
                ref[at, lanes] = v
        return carry

    lax.fori_loop(0, length // chunk, project, 0)
    for ref, out in ((qs, q_out), (ks, k_out), (vs, v_out)):
        store(ref, out)

    pairs = units // 128

    def attend(p, carry):
        @pl.when(p == pairs // 2)
        def _():
            g_x.wait_recv()
            start(g_n)
            d_x.start()

        lane0 = p * 128
        q2 = qs[:, span(lane0, 128)]
        k2 = ks[:, span(lane0, 128)]
        v2 = vs[:, span(lane0, 128)]
        for begin, low, end in windows(length):
            bar = barred(starts_ref[begin:end], begin, low, end)
            outs = []
            for h in range(2):
                lanes = slice(h * HEAD, (h + 1) * HEAD)
                scores = nt(q2[begin:end, lanes], k2[low:end, lanes]) + bar
                maxima = jnp.max(scores, axis=1, keepdims=True)
                shifted = jnp.exp(scores - maxima).astype(BF)
                wide = jnp.concatenate([v2[low:end, lanes], jnp.ones((end - low, HEAD), BF)], axis=1)
                got = jnp.dot(shifted, wide, preferred_element_type=F32)
                totals = got[:, HEAD : HEAD + 1]
                outs.append(got[:, :HEAD] / totals)
                logs[p, begin:end, h : h + 1] = maxima + jnp.log(totals)
            out = jnp.concatenate(outs, axis=1)
            att[begin:end, span(lane0, 128)] = out.astype(BF)
        return carry

    lax.fori_loop(0, pairs, attend, 0)
    store(att, att_out)
    store(logs, log_out)

    load_o.wait()
    arrived(o_n)
    store(wo, wo_out)
    stores[0].wait()
    tok_f.wait_send()

    def branch(base):
        def body(i, carry):
            at = span(base + i * chunk, chunk)
            act[at] = jnp.dot(att[at], wo[...], preferred_element_type=F32).astype(BF)
            return carry

        lax.fori_loop(0, part // chunk, body, 0)

    branch((1 - c) * part)
    rs_c.start()
    branch(c * part)
    rs_c.wait_recv()
    row_src[...] = act[x_block] + core_in[span((1 - r) * block, block)]
    rs_x.start()
    part_gate(gate_far.at[sub], span(half + sub * quarter, quarter))
    subs = (zp * 2 + 1 - y, (1 - zp) * 2 + y, (1 - zp) * 2 + 1 - y)
    rs_x.wait_recv()
    hid_rows = 64

    def norm_two(i, carry):
        at = span(i * hid_rows, hid_rows)
        kept = act[span(c * part + r * block + i * hid_rows, hid_rows)].astype(F32)
        kept = kept + core_in[span(r * block + i * hid_rows, hid_rows)].astype(F32)
        got = row_in[at].astype(F32)
        kept = kept + jnp.concatenate([got[:, half:], got[:, :half]], axis=1)
        kept = own_in[at].astype(F32) + kept
        hid[at] = kept
        tok[span(c * part + r * block + i * hid_rows, hid_rows)] = normed(kept, 2)
        return carry

    lax.fori_loop(0, block // hid_rows, norm_two, 0)
    start(ag_x)
    ag_c.start()
    store(hid, hid_out)
    d_x.wait_recv()
    start(d_n)
    c_x.start()
    for k in range(3):
        g_n[k].wait_recv()
        part_gate(gate_far.at[subs[k]], span(half + subs[k] * quarter, quarter))
    store(wg, wg_out)

    stores_of = []
    columns = [(at, min(512, hidden - at)) for at in range(0, hidden, 512)]
    for b in range(4):
        cc = c if b % 2 == 0 else 1 - c
        rr = r if b < 2 else 1 - r
        at = span(cc * part + rr * block, block)
        if b == 1:
            ag_c.wait_recv()
        elif b == 2:
            arrived(ag_x)
            ag_f.start()
        elif b == 3:
            ag_f.wait_recv()
        s = b % 2
        for copy in stores_of[3 * (b - 2) : 3 * (b - 1)] if b >= 2 else ():
            copy.wait()
        rows = tok[at]
        for first, size in columns:
            cols = slice(first, first + size)
            gate = jnp.dot(rows, wg[0, :, cols], preferred_element_type=F32)
            up = jnp.dot(rows, wg[1, :, cols], preferred_element_type=F32)
            tile[s, 0, :, cols] = gate.astype(BF)
            tile[s, 1, :, cols] = up.astype(BF)
            tile[s, 2, :, cols] = (gate / (1.0 + jnp.exp(-gate)) * up).astype(BF)
        for k, out in enumerate((gate_out, up_out, inner_out)):
            copy = pltpu.make_async_copy(tile.at[s, k], out.at[at], load_sem.at[7 + 3 * s + k])
            copy.start()
            stores_of.append(copy)
    store(tok, act_two)
    c_x.wait_recv()
    load_c.wait()
    c_f.start()
    for copy in stores_of[6:] + stores[1:] + [load_d]:
        copy.wait()
    arrived(d_n)
    c_c.wait_recv()
    c_f.wait_recv()
    for copy in [q_x, tok_x, tok_c, o_x, g_x, d_x, c_x, c_c, c_f, rs_c, rs_x, ag_c, ag_f] + (
        q_n + o_n + g_n + d_n + ag_x
    ):
        copy.wait_send()


def front(tokens, starts, table, params, bias, qkv_w, out_w, gate_w, down_w, cotangent):
    part, half = tokens.shape
    length, width, block = 2 * part, 2 * half, part // 2
    units, hidden = out_w.shape[0] // 2, down_w.shape[0] // 2
    any_spec, vmem_spec = pl.BlockSpec(memory_space=pl.ANY), pl.BlockSpec(memory_space=pltpu.VMEM)
    pairs = units // 128

    def bf(*shape):
        return jax.ShapeDtypeStruct(shape, BF)

    def f32(*shape):
        return jax.ShapeDtypeStruct(shape, F32)

    outs = [
        bf(length, width),
        bf(length, units),
        bf(length, units),
        bf(length, units),
        bf(length, units),
        f32(pairs, length, 2),
        f32(block, width),
        bf(length, width),
        bf(length, hidden),
        bf(length, hidden),
        bf(length, hidden),
        bf(3, width, units),
        bf(units, width),
        bf(2, width, hidden),
        bf(hidden, width),
        bf(length, width),
        bf(block, width),
    ]
    scratch = [
        bf(length, width),
        bf(length, width),
        bf(3, width, units),
        bf(units, width),
        bf(2, width, hidden),
        bf(4, half // 4, 2, hidden),
        bf(2, half // 8, 2, hidden),
        bf(length, units),
        bf(length, units),
        bf(length, units),
        bf(length, units),
        f32(pairs, length, 2),
        bf(part, width),
        bf(block, width),
        bf(block, width),
        bf(block, width),
        f32(block, width),
        bf(2, 3, block, hidden),
    ]
    dma = pltpu.SemaphoreType.DMA
    return pl.pallas_call(
        front_kernel,
        out_shape=outs,
        in_specs=[any_spec] + [vmem_spec] * 4 + [any_spec] * 5,
        out_specs=[any_spec] * len(outs),
        scratch_shapes=[pltpu.VMEM(v.shape, v.dtype) for v in scratch]
        + [dma((28,)), dma((28,)), dma((13,)), dma((16,))],
        compiler_params=pltpu.CompilerParams(
            collective_id=2, has_side_effects=True, vmem_limit_bytes=62 * 2**20
        ),
        cost_estimate=pl.CostEstimate(
            flops=2 * length * width * (4 * units + 2 * hidden),
            bytes_accessed=100 * 2**20,
            transcendentals=length * 2048,
        ),
    )(tokens, starts, table, params, bias, qkv_w, out_w, gate_w, down_w, cotangent)


def local(
    tokens,
    segments,
    ln1_gain,
    ln1_bias,
    qkv_weight,
    qkv_bias,
    out_weight,
    ln2_gain,
    ln2_bias,
    gate_up_weight,
    down_weight,
    cotangent,
):
    place = Place()
    r, c = place.r, place.c
    ids = segments[0]
    length = ids.shape[0]
    factor = HEAD ** (-0.5)
    half = qkv_weight.shape[0]
    units = qkv_weight.shape[2] // 2
    heads = units // HEAD
    hidden = gate_up_weight.shape[2] // 2

    params = jnp.stack([ln1_gain, ln1_bias, ln2_gain, ln2_bias])
    params = jnp.concatenate([params, swap(params, "row")], axis=1)
    cosines, sines = rotary_tables(ids)
    table = tables(cosines, sines)
    starts = (jnp.arange(length, dtype=jnp.int32) - doc_positions(ids))[:, None]
    bias = piece(qkv_bias, r, 2, 1)
    (
        act_one,
        queries,
        keys,
        values,
        attended,
        logs,
        hidden_state,
        act_two,
        gate,
        up,
        inner,
        w_qkv,
        w_out,
        w_gate,
        w_down,
        cot_all,
        own_inputs,
    ) = front(
        tokens,
        starts,
        table,
        params,
        bias,
        qkv_weight.transpose(1, 0, 2),
        out_weight,
        gate_up_weight,
        down_weight,
        cotangent,
    )
    if place.count == 8:
        sums, bases, result, result_far, input_grad, input_far, norm_grads, bias_grad = back(
            inner,
            cot_all,
            gate,
            up,
            act_two,
            attended,
            queries,
            keys,
            values,
            logs,
            starts,
            table,
            act_one,
            hidden_state,
            own_inputs,
            params,
            w_down,
            w_gate,
            w_out,
            w_qkv,
        )
        result = ordered(r, result, result_far)
        input_grad = ordered(r, input_grad, input_far)
        ln1_gain_grad, ln1_bias_grad, ln2_gain_grad, ln2_bias_grad = norm_grads[:4]
        bias_grad = bias_grad[:3]
        side = r.reshape(1)
        down_grad = spread_rows(side, sums, bases[0], half, hidden)
        gate_up_grad = spread_columns(side, sums, bases[1], half, hidden, 2, 256)
        out_grad = spread_rows(side, sums, bases[2], half, units)
        qkv_grad = spread_columns(side, sums, bases[3], half, units, 3, 256)
    else:
        block = c * 2 + r
        own_inputs = own_inputs.astype(F32)
        _, normal_two, inverse_two = norm_forward(hidden_state, params[2], params[3])
        gate, up = gate.astype(F32), up.astype(F32)

        feed = reduce_blocks(dot(inner, w_down).astype(BF), place)
        result = (hidden_state + feed).astype(BF)
        result = ordered(r, result[:, :half], swap(result[:, half:], "row"))

        grad_inner = dot_t(cot_all, w_down)
        rate = 1.0 / (1.0 + jnp.exp(-gate))
        silu = gate * rate
        grad_gate = (grad_inner * up * (rate * (1.0 + gate * (1.0 - rate)))).astype(BF)
        grad_up = (grad_inner * silu).astype(BF)
        grad_two = jnp.stack([grad_gate, grad_up])
        grad_pair = jnp.concatenate([grad_gate, grad_up], axis=1)
        grad_act_two = reduce_blocks(
            jnp.einsum("ksf,kdf->sd", grad_two, w_gate, preferred_element_type=F32).astype(BF), place
        )
        grad_norm, ln2_gain_grad, ln2_bias_grad = norm_backward(
            grad_act_two, normal_two, inverse_two, params[2]
        )
        own_cot = piece(cot_all, block, 4).astype(F32)
        grad_hidden = own_cot + grad_norm
        grad_branch = gather_blocks(grad_hidden.astype(BF), place)
        grad_attended = dot_t(grad_branch, w_out).astype(BF)
        grad_joined = attention_backward(
            queries, keys, values, grad_attended, attended, logs, starts, table
        )
        grad_joined = jnp.concatenate(grad_joined, axis=1)
        bias_grad = jnp.sum(grad_joined, axis=0, dtype=F32)
        grad_kinds = grad_joined.reshape(length, 3, units)
        grad_act_one = reduce_blocks(
            jnp.einsum("sku,kdu->sd", grad_kinds, w_qkv, preferred_element_type=F32).astype(BF), place
        )
        _, normal_one, inverse_one = norm_forward(own_inputs, params[0], params[1])
        grad_norm, ln1_gain_grad, ln1_bias_grad = norm_backward(
            grad_act_one, normal_one, inverse_one, params[0]
        )
        input_grad = grad_hidden + grad_norm
        input_grad = ordered(r, input_grad[:, :half], swap(input_grad[:, half:], "row"))

        pairs = (
            ("D", act_two, grad_pair),
            ("D", act_one, grad_joined),
            ("U", attended, grad_branch),
            ("U", inner, cot_all),
        )
        sums = []
        for kind, left, right in pairs:
            both = t_dot(left, right).astype(BF)
            axis = 0 if kind == "D" else 1
            own, sent = jnp.split(both, 2, axis)
            sums.append([lax.psum(v, "dp").astype(F32) for v in (own, swap(sent, "row"))])
        gate_up_grad = ordered(r, *[v.reshape(half, 2, hidden) for v in sums[0]], 2)
        qkv_grad = ordered(r, *[v.reshape(half, 3, units) for v in sums[1]], 2)
        out_grad = ordered(r, *sums[2])
        down_grad = ordered(r, *sums[3])

    small = jnp.stack([ln1_gain_grad, ln1_bias_grad, ln2_gain_grad, ln2_bias_grad])
    small = small[:, :half] + swap(small[:, half:], "row")
    small = small + swap(small, "col")
    bias_grad = bias_grad.reshape(3, units)
    small = jnp.concatenate([small.reshape(-1), bias_grad.reshape(-1)])
    if place.count == 8:
        for bit in (1, 2, 4):
            small = small + lax.ppermute(small, "dp", dp_perm(bit, 8))
    else:
        small = lax.psum(small, "dp")
    norms = small[: 4 * half].reshape(4, half)
    bias_grad = small[4 * half :].reshape(3, units)
    bias_grad = ordered(r, bias_grad, swap(bias_grad, "row"), 1)

    return (
        result,
        input_grad,
        norms[0],
        norms[1],
        qkv_grad,
        bias_grad,
        out_grad,
        norms[2],
        norms[3],
        gate_up_grad,
        down_grad,
    )


def solution(mesh):
    in_specs = (
        P(("dp", "col"), "row"),
        P("dp", None),
        P("row"),
        P("row"),
        P("row", None, "col"),
        P(None, "col"),
        P("col", "row"),
        P("row"),
        P("row"),
        P("row", None, "col"),
        P("col", "row"),
        P(("dp", "col"), "row"),
    )
    out_specs = (
        P(("dp", "col"), "row"),
        P(("dp", "col"), "row"),
        P("row"),
        P("row"),
        P("row", None, "col"),
        P(None, "col"),
        P("col", "row"),
        P("row"),
        P("row"),
        P("row", None, "col"),
        P("col", "row"),
    )
    return jax.shard_map(local, mesh=mesh, in_specs=in_specs, out_specs=out_specs, check_vma=False)
```

```python
import functools
import math

import jax
import jax.numpy as jnp
from jax import lax
from jax.experimental import pallas as pl
from jax.experimental.pallas import tpu as pltpu
from jax.sharding import PartitionSpec as P

HEAD = 64
ROT = 16
EPSILON = 1e-05
ROPE_BASE = 10000.0
NEGATIVE = -1e30
BF = jnp.bfloat16
F32 = jnp.float32
SWAP = [(0, 1), (1, 0)]
MESH = pl.DeviceIdType.MESH


def swap(v, axis):
    return lax.ppermute(v, axis, SWAP)


def ordered(flag, mine, other, axis=0):
    first = jnp.where(flag == 0, mine, other)
    second = jnp.where(flag == 0, other, mine)
    return jnp.concatenate([first, second], axis=axis)


def piece(v, index, count, axis=0):
    size = v.shape[axis] // count
    return lax.dynamic_slice_in_dim(v, index * size, size, axis)


def add(a, b):
    return (a.astype(F32) + b.astype(F32)).astype(BF)


def dot(a, b):
    return jnp.dot(a, b, preferred_element_type=F32)


def dot_t(a, b):
    return lax.dot_general(a, b, (((1,), (1,)), ((), ())), preferred_element_type=F32)


def t_dot(a, b):
    return lax.dot_general(a, b, (((0,), (0,)), ((), ())), preferred_element_type=F32)


class Place:
    def __init__(self):
        self.r = lax.axis_index("row")
        self.c = lax.axis_index("col")
        self.d = lax.axis_index("dp")
        self.count = lax.axis_size("dp")
        self.y = lax.rem(self.d, 2)
        self.zp = lax.rem(self.d // 2, 2)
        self.z = self.d // 2
        self.mid = (self.z == 1) | (self.z == 2)
        self.upper = (self.z >= 2).astype(jnp.int32)


def dp_perm(bit, count):
    return [(i, i ^ bit) for i in range(count)]


def cross(v):
    half = v.shape[-1] // 2
    return jnp.concatenate([v[..., half:], v[..., :half]], axis=-1)


def gather_blocks(block, place):
    other = cross(swap(block, "row"))
    pair = ordered(place.r, block, other)
    rest = swap(pair, "col")
    return ordered(place.c, pair, rest)


def reduce_blocks(partial, place):
    kept = piece(partial, place.c, 2)
    got = swap(piece(partial, 1 - place.c, 2), "col")
    held = add(kept, got)
    kept = piece(held, place.r, 2)
    got = cross(swap(piece(held, 1 - place.r, 2), "row"))
    return kept.astype(F32) + got.astype(F32)


def norm_forward(values, gain, shift):
    count = values.shape[-1]
    mean = jnp.sum(values, axis=-1, keepdims=True) / count
    spread = jnp.sum(values * values, axis=-1, keepdims=True) / count - mean * mean
    inverse = lax.rsqrt(spread + EPSILON)
    normal = (values - mean) * inverse
    return normal * gain + shift, normal, inverse


def norm_backward(grad, normal, inverse, gain):
    count = grad.shape[-1]
    scaled = grad * gain
    first = jnp.sum(scaled, axis=-1, keepdims=True) / count
    second = jnp.sum(scaled * normal, axis=-1, keepdims=True) / count
    grad_input = inverse * (scaled - first - normal * second)
    return grad_input, jnp.sum(grad * normal, axis=0), jnp.sum(grad, axis=0)


def first_places(segment_ids):
    return jnp.sum(segment_ids[None, :] < segment_ids[:, None], axis=1, dtype=jnp.int32)


def rotary_table(places):
    lane = jnp.arange(128, dtype=jnp.int32) % HEAD
    half_rot = ROT // 2
    inverse = jnp.exp((lane % half_rot).astype(F32) * (-2.0 / ROT) * math.log(ROPE_BASE))
    angles = places.astype(F32)[:, None] * inverse[None, :]
    cosines, sines = jnp.cos(angles), jnp.sin(angles)
    low, turns = (lane < half_rot)[None, :], (lane < ROT)[None, :]
    return jnp.stack(
        [
            jnp.where(turns, cosines, 1.0),
            jnp.where(low, -sines, 0.0),
            jnp.where(turns & ~low, sines, 0.0),
        ]
    )


LONGEST = 512
QB = 256

def windows(length):
    for begin in range(0, length, QB):
        low = max(0, (begin - LONGEST + 1) // QB * QB)
        yield begin, low, begin + QB


def barred(starts, begin, low, end):
    shape = (end - begin, end - low)
    query = begin + lax.broadcasted_iota(jnp.int32, shape, 0)
    key = low + lax.broadcasted_iota(jnp.int32, shape, 1)
    return jnp.where((key <= query) & (key >= starts), 0.0, NEGATIVE)


def turned(v, table):
    width = v.shape[-1]
    return v * table[0] + pltpu.roll(v, width - 8, 1) * table[1] + pltpu.roll(v, 8, 1) * table[2]


def nt(a, b):
    return lax.dot_general(a, b, (((1,), (1,)), ((), ())), preferred_element_type=F32)


def tn(a, b):
    return lax.dot_general(a, b, (((0,), (0,)), ((), ())), preferred_element_type=F32)


def backward_kernel(q_ref, k_ref, v_ref, g_ref, att_ref, log_ref, starts_ref, table_ref, dq_ref, dk_ref, dv_ref, dk_acc, dv_acc):
    length = q_ref.shape[0]
    dk_acc[...] = jnp.zeros_like(dk_acc)
    dv_acc[...] = jnp.zeros_like(dv_acc)
    for begin, low, end in windows(length):
        bar = barred(starts_ref[begin:end], begin, low, end)
        outs, dks, dvs = [], [], []
        for h in range(2):
            lanes = slice(h * HEAD, (h + 1) * HEAD)
            q, k, v, g = q_ref[begin:end, lanes], k_ref[low:end, lanes], v_ref[low:end, lanes], g_ref[begin:end, lanes]
            weights = jnp.exp(nt(q, k) + bar - log_ref[0, begin:end, h : h + 1])
            dvs.append(tn(weights.astype(BF), g))
            inner = jnp.sum(g.astype(F32) * att_ref[begin:end, lanes].astype(F32), axis=1, keepdims=True)
            grads = (weights * (nt(g, v) - inner)).astype(BF)
            outs.append(jnp.dot(grads, k, preferred_element_type=F32))
            dks.append(tn(grads, q))
        table = (table_ref[0, begin:end], -table_ref[1, begin:end], -table_ref[2, begin:end])
        dq_ref[begin:end] = turned(jnp.concatenate(outs, axis=1) * HEAD ** (-0.5), table).astype(BF)
        dk_acc[low:end] += jnp.concatenate(dks, axis=1)
        dv_acc[low:end] += jnp.concatenate(dvs, axis=1)
    table = (table_ref[0], -table_ref[1], -table_ref[2])
    dk_ref[...] = turned(dk_acc[...], table).astype(BF)
    dv_ref[...] = dv_acc[...].astype(BF)


def attention_backward(queries, keys, values, grads, attended, logs, starts, table):
    length, units = queries.shape
    pairs = units // 128
    same = pl.BlockSpec((length, 128), lambda p: (0, p))
    half = jax.ShapeDtypeStruct((length, units), BF)
    return pl.pallas_call(
        backward_kernel,
        grid=(pairs,),
        in_specs=[same] * 5
        + [
            pl.BlockSpec((1, length, 2), lambda p: (p, 0, 0)),
            pl.BlockSpec((length, 1), lambda p: (0, 0)),
            pl.BlockSpec((3, length, 128), lambda p: (0, 0, 0)),
        ],
        out_specs=[same] * 3,
        out_shape=[half] * 3,
        scratch_shapes=[pltpu.VMEM((length, 128), F32)] * 2,
        compiler_params=pltpu.CompilerParams(vmem_limit_bytes=48 * 2**20),
        cost_estimate=pl.CostEstimate(flops=pairs * 2 * length * 640 * 640, bytes_accessed=8 * 2**20, transcendentals=pairs * 2 * length * 640),
    )(queries, keys, values, grads, attended, logs, starts, table)


BR = 512
BC = 256
SLOTS = 5
SEMAPHORES = 10
SHORT = 3
FAR_SLOTS = 8
LEAD = 2


def back_kernel(
    bases,
    inner,
    cotangent,
    gate,
    up,
    act_two,
    attended,
    queries,
    keys,
    values,
    logs,
    starts_ref,
    table_ref,
    act_one,
    hidden_state,
    own_inputs,
    params_ref,
    w_down,
    w_gate,
    w_out,
    w_qkv,
    out_ref,
    res_own,
    res_got,
    grad_own,
    grad_got,
    small_out,
    norm_sums,
    bias_sums,
    small_src,
    small_in,
    turn,
    turn_in,
    joint,
    branch,
    pair,
    att,
    att_grad,
    heads,
    head_logs,
    key_sums,
    value_sums,
    down_rows,
    gate_in,
    down_columns,
    wide_w,
    w_o,
    sent,
    kept,
    core_in,
    row_src,
    row_in,
    acc_rows,
    grad_rows,
    hid,
    own,
    result,
    part,
    x_src,
    x_dst,
    y_dst,
    acc,
    e_dst,
    low,
    m_dst,
    full,
    f_dst,
    deep,
    n_dst,
    key,
    k_dst,
    whole,
    load_sem,
    once_sem,
    piece_sem,
    gather_sem,
    small_sem,
    *sems,
):
    out_own, out_got = out_ref.at[0], out_ref.at[1]
    names = ("x", "y", "ei", "eo", "m", "g", "fi", "fo", "n", "k", "w")
    send = {k: sems[i] for i, k in enumerate(names)}
    recv = {k: sems[len(names) + i] for i, k in enumerate(names)}
    store_own, store_got = sems[2 * len(names)], sems[2 * len(names) + 1]

    length, width = branch.shape
    half, part_rows, block = width // 2, length // 2, length // 4
    hidden, units = pair.shape[1] // 2, att.shape[1]
    pairs = units // 128
    size = BR * BC // half
    segments = (hidden // size, half * 2 * hidden // (BR * BC), units // size, half * 3 * units // (BR * BC))
    total = sum(segments)
    firsts = [sum(segments[:i]) for i in range(4)]

    d, r, c = lax.axis_index("dp"), lax.axis_index("row"), lax.axis_index("col")
    y, z = lax.rem(d, 2), d // 2
    upper = d // 4
    mid = (z == 1) | (z == 2)
    outer = (z == 0) | (z == 3)
    x_peer, c_peer = {"row": 1 - r}, {"col": 1 - c}
    y_peer = {"dp": d + 1 - 2 * y}
    e_peer = {"dp": d + 2 - 4 * lax.rem(z, 2)}
    m_peer = {"dp": d + 2 - 4 * upper}

    def span(start, count):
        return pl.ds(pl.multiple_of(start, count), count)

    def local_copy(n, src, dst):
        return pltpu.make_async_copy(src, dst, load_sem.at[n])

    barrier = pltpu.get_barrier_semaphore()
    for peer in (x_peer, y_peer, e_peer, c_peer):
        pl.semaphore_signal(barrier, inc=1, device_id=peer, device_id_type=MESH)

    @pl.when(mid)
    def _():
        pl.semaphore_signal(barrier, inc=1, device_id=m_peer, device_id_type=MESH)

    own_block = span(c * part_rows + r * block, block)
    x_block = span(c * part_rows + (1 - r) * block, block)
    lo, hi = pl.ds(0, half), pl.ds(half, half)
    load_inner = local_copy(0, inner, joint.at[:, pl.ds(0, hidden)])
    load_cot = local_copy(1, cotangent, branch)
    load_hid = local_copy(2, hidden_state, hid)
    load_own = local_copy(3, cotangent.at[own_block], own)
    load_att = local_copy(4, attended, att)
    load_wo = local_copy(5, w_out, w_o)
    load_inputs = local_copy(6, own_inputs, own)

    def down_rows_load(i):
        s = lax.rem(i, 2)
        at = span(i * 128, 128)
        return (
            pltpu.make_async_copy(w_down.at[at], down_rows.at[s], once_sem.at[s]),
            pltpu.make_async_copy(gate.at[:, at], gate_in.at[s, 0], once_sem.at[2 + s]),
            pltpu.make_async_copy(up.at[:, at], gate_in.at[s, 1], once_sem.at[4 + s]),
        )

    def order(i):
        return lax.rem(i, 2) * (half // BC) + i // 2

    def down_columns_load(i):
        s = lax.rem(i, 2)
        return (pltpu.make_async_copy(w_down.at[:, span(order(i) * BC, BC)], down_columns.at[s], once_sem.at[6 + s]),)

    def gate_load(i):
        s = lax.rem(i, 2)
        return (pltpu.make_async_copy(w_gate.at[:, span(order(i) * BC, BC)], wide_w.at[s], once_sem.at[8 + s]),)

    def qkv_load(i):
        s = lax.rem(i, 2)
        rows = span(order(i) * BC, BC)
        return tuple(
            pltpu.make_async_copy(
                w_qkv.at[k, rows], wide_w.at[s, k // 2, :, pl.ds(k % 2 * units, units)], once_sem.at[10 + 2 * k + s]
            )
            for k in range(3)
        )

    def heads_load(p):
        s = lax.rem(p, 2)
        lanes = span(p * 128, 128)
        return tuple(
            pltpu.make_async_copy(ref.at[:, lanes], heads.at[s, k], once_sem.at[16 + 2 * k + s])
            for k, ref in enumerate((queries, keys, values))
        ) + (pltpu.make_async_copy(logs.at[p], head_logs.at[s], once_sem.at[22 + s]),)

    def turn_load(source, i, side):
        return local_copy(7 + side, source.at[:, span(side * half + i * BR, BR)], turn_in.at[side])

    def start(copies):
        for copy in copies:
            copy.start()

    def wait(copies):
        for copy in copies:
            copy.wait()

    start((load_inner, load_cot, load_hid, load_own, load_att, load_wo))
    start(down_rows_load(0))
    start(down_columns_load(0))
    start((turn_load(act_two, 0, 0), turn_load(act_two, 0, 1)))

    @pl.when(mid)
    def _():
        pl.semaphore_wait(barrier, 5)

    @pl.when(outer)
    def _():
        pl.semaphore_wait(barrier, 4)

    rows = BR // 2

    def halves(index):
        return span(index * rows, rows)

    def slot(u):
        return lax.rem(u, SLOTS)

    def short(u):
        return lax.rem(u, SHORT)

    def far_slot(u):
        return lax.rem(u, FAR_SLOTS)

    def copy(name, u, src, dst, peer):
        s = lax.rem(u, SEMAPHORES)
        return pltpu.make_async_remote_copy(
            src_ref=src,
            dst_ref=dst,
            send_sem=send[name].at[s],
            recv_sem=recv[name].at[s],
            device_id=peer,
            device_id_type=MESH,
        )

    def spot(u):
        place = u
        for first, base in zip(firsts, bases):
            place = jnp.where(u >= first, u + (base - first), place)
        return place

    def out_half(ref, u, index):
        return ref.at[spot(u), halves(index)]

    def x_copy(u):
        return copy("x", u, x_src.at[short(u)], x_dst.at[far_slot(u)], x_peer)

    def y_copy(u):
        return copy("y", u, part.at[short(u), halves(1 - y)], y_dst.at[slot(u)], y_peer)

    def e_in(u):
        return copy("ei", u, acc.at[short(u)], e_dst.at[slot(u)], e_peer)

    def e_out(u):
        return copy("eo", u, full.at[short(u)], e_dst.at[slot(u)], e_peer)

    def m_copy(u):
        return copy("m", u, low.at[short(u)], m_dst.at[slot(u)], m_peer)

    def g_mid(u):
        return copy("g", u, full.at[short(u)], out_half(out_own, u, y), y_peer)

    def g_out(u):
        return copy("g", u, e_dst.at[slot(u)], out_half(out_own, u, y), y_peer)

    def f_in(u):
        return copy("fi", u, x_dst.at[far_slot(u)], f_dst.at[slot(u)], e_peer)

    def f_out(u):
        return copy("fo", u, whole.at[slot(u)], out_got.at[spot(u)], e_peer)

    def n_copy(u):
        return copy("n", u, deep.at[short(u), halves(1 - upper)], n_dst.at[slot(u)], m_peer)

    def k_copy(u):
        return copy("k", u, key.at[short(u)], k_dst.at[slot(u)], y_peer)

    def w_copy(u):
        place = whole.at[slot(u), halves(upper)]
        return copy("w", u, place, place, m_peer)

    def keep_own(u, src):
        return pltpu.make_async_copy(src, out_half(out_own, u, y), store_own.at[slot(u)])

    def keep_got(u):
        return pltpu.make_async_copy(whole.at[slot(u)], out_got.at[spot(u)], store_got.at[slot(u)])

    def stage(u, fn, role=None):
        ok = (u >= 0) & (u < total)
        if role is not None:
            ok = ok & role

        @pl.when(ok)
        def _():
            fn(u)

    def within(t, first, count, fn):
        @pl.when((t >= first) & (t < first + count))
        def _():
            fn(t - first)

    def unit_block(k, side, ref, s, lhs, rhs):
        left = lhs[:, span(k * size, size)].T
        for q in range(half // BC):
            right = rhs[:, side * half + q * BC : side * half + (q + 1) * BC]
            ref[s, q * size : (q + 1) * size] = jnp.dot(left, right, preferred_element_type=F32).astype(BF)

    def feature_block(k, side, ref, s, rhs, source, following):
        columns = rhs.shape[1] // BC

        for i in range(half // BR):

            @pl.when(k == i * columns)
            def _(i=i):
                turn_load(source, i, side).wait()
                turn[side] = turn_in[side].T
                if i + 1 < half // BR:
                    turn_load(source, i + 1, side).start()
                elif following is not None:
                    turn_load(following, 0, side).start()

        right = rhs[:, span(lax.rem(k, columns) * BC, BC)]
        ref[s] = jnp.dot(turn[side], right, preferred_element_type=F32).astype(BF)

    def produce(u, side, ref):
        s = short(u)
        within(u, firsts[0], segments[0], lambda k: unit_block(k, side, ref, s, joint, branch))
        within(u, firsts[1], segments[1], lambda k: feature_block(k, side, ref, s, pair, act_two, act_one))
        within(u, firsts[2], segments[2], lambda k: unit_block(k, side, ref, s, att, branch))
        within(u, firsts[3], segments[3], lambda k: feature_block(k, side, ref, s, joint, act_one, None))

    def produce_own(u):
        produce(u, 0, part)
        y_copy(u).start()

    def produce_far(u):
        @pl.when(u == 0)
        def _():
            wait((load_inner, load_cot))

        produce(u, 1, x_src)
        x_copy(u).start()

    def t1_a(u):
        y_copy(u).wait_recv()
        acc[short(u)] = part[short(u), halves(y)] + y_dst[slot(u)]
        pl.when(outer)(lambda: e_in(u).start())

    def t1_b(u):
        e_in(u).wait_recv()
        low[short(u)] = acc[short(u)] + e_dst[slot(u)]
        m_copy(u).start()

    def t1_c(u):
        m_copy(u).wait_recv()
        full[short(u)] = low[short(u)] + m_dst[slot(u)]
        e_out(u).start()
        g_mid(u).start()
        keep_own(u, full.at[short(u)]).start()

    def t1_d(u):
        e_out(u).wait_recv()
        g_out(u).start()
        keep_own(u, e_dst.at[slot(u)]).start()

    def t2_a(u):
        x_copy(u).wait_recv()
        pl.when(outer)(lambda: f_in(u).start())

    def t2_b(u):
        f_in(u).wait_recv()
        deep[short(u)] = x_dst[far_slot(u)] + f_dst[slot(u)]
        n_copy(u).start()

    def t2_c(u):
        n_copy(u).wait_recv()
        key[short(u)] = deep[short(u), halves(upper)] + n_dst[slot(u)]
        k_copy(u).start()

    def t2_d(u):
        k_copy(u).wait_recv()
        whole[slot(u), halves(upper)] = key[short(u)] + k_dst[slot(u)]
        w_copy(u).start()

    def t2_e(u):
        w_copy(u).wait_recv()
        f_out(u).start()
        keep_got(u).start()

    pieces = width // BC
    own_part, far_part = c * part_rows, (1 - c) * part_rows

    def core_copy(n):
        s = lax.rem(n, 3)
        return pltpu.make_async_remote_copy(
            src_ref=sent.at[s],
            dst_ref=core_in.at[s],
            send_sem=piece_sem.at[s],
            recv_sem=piece_sem.at[3 + s],
            device_id=c_peer,
            device_id_type=MESH,
        )

    def row_copy(n):
        s = lax.rem(n, 4)
        return pltpu.make_async_remote_copy(
            src_ref=row_src.at[s],
            dst_ref=row_in.at[s],
            send_sem=piece_sem.at[6 + s],
            recv_sem=piece_sem.at[10 + s],
            device_id=x_peer,
            device_id_type=MESH,
        )

    def sum_piece(n, product):
        s = lax.rem(n, 3)
        sent[s] = product(span(far_part, part_rows)).astype(BF)
        core_copy(n).start()
        kept[s] = product(span(own_part, part_rows)).astype(BF)

    def sum_core(n, i):
        s, q = lax.rem(n, 3), lax.rem(n, 4)
        core_copy(n).wait_recv()
        core_copy(n).wait_send()
        far, near = span((1 - r) * block, block), span(r * block, block)
        row_src[q] = kept[s, far] + core_in[s, far]
        row_copy(n).start()
        acc_rows[:, span(order(i) * BC, BC)] = kept[s, near].astype(F32) + core_in[s, near].astype(F32)

    def sum_row(n, i):
        q = lax.rem(n, 4)
        row_copy(n).wait_recv()
        row_copy(n).wait_send()
        partner = lax.rem(order(i) + half // BC, pieces)
        cols = span(partner * BC, BC)
        acc_rows[:, cols] = acc_rows[:, cols] + row_in[q].astype(F32)

    def summed(t, first, base, product, load, wait_for=None):
        within(t, first + 3, pieces, lambda i: sum_row(base + i, i))
        within(t, first + 1, pieces, lambda i: sum_core(base + i, i))

        def task(i):
            if wait_for is not None:
                pl.when(i == 0)(lambda: wait(wait_for))
            pl.when(i + 1 < pieces)(lambda: start(load(i + 1)))
            wait(load(i))
            sum_piece(base + i, lambda at: product(lax.rem(i, 2), at))

        within(t, first, pieces, task)

    def feed_product(s, at):
        return jnp.dot(joint[at, :hidden], down_columns[s], preferred_element_type=F32)

    def act_two_product(s, at):
        return nt(pair[at, :hidden], wide_w[s, 0]) + nt(pair[at, hidden:], wide_w[s, 1])

    def act_one_product(s, at):
        out = nt(joint[at, :units], wide_w[s, 0, :, :units])
        out = out + nt(joint[at, units : 2 * units], wide_w[s, 0, :, units : 2 * units])
        return out + nt(joint[at, 2 * units :], wide_w[s, 1, :, :units])

    def gate_task(i):
        s = lax.rem(i, 2)

        @pl.when(i + 1 < hidden // 128)
        def _():
            start(down_rows_load(i + 1))

        wait(down_rows_load(i))

        def some(j, carry):
            at = span(j * 256, 256)
            grad = nt(branch[at], down_rows[s])
            g, u = gate_in[s, 0, at].astype(F32), gate_in[s, 1, at].astype(F32)
            rate = 1.0 / (1.0 + jnp.exp(-g))
            pair[at, span(i * 128, 128)] = (grad * u * (rate * (1.0 + g * (1.0 - rate)))).astype(BF)
            pair[at, span(hidden + i * 128, 128)] = (grad * (g * rate)).astype(BF)
            return carry

        lax.fori_loop(0, length // 256, some, 0)

    def result_copy():
        return pltpu.make_async_remote_copy(
            src_ref=result.at[:, hi],
            dst_ref=res_got,
            send_sem=gather_sem.at[0],
            recv_sem=gather_sem.at[1],
            device_id=x_peer,
            device_id_type=MESH,
        )

    store_result = local_copy(9, result.at[:, lo], res_own)

    def result_task(i):
        load_hid.wait()
        load_own.wait()
        result[...] = (hid[...] + acc_rows[...]).astype(BF)
        result_copy().start()
        store_result.start()

    chunk = 64
    chunks = block // chunk

    def norm_rows(values, at, grads, gain):
        mean = jnp.sum(values, axis=1, keepdims=True) / width
        spread_of = jnp.sum(values * values, axis=1, keepdims=True) / width - mean * mean
        inverse = lax.rsqrt(spread_of + EPSILON)
        normal = (values - mean) * inverse
        scaled = grads * gain
        terms = grads * normal
        first = jnp.sum(scaled, axis=1, keepdims=True) / width
        second = jnp.sum(terms * gain, axis=1, keepdims=True) / width
        return inverse * (scaled - first - normal * second), terms

    def gather_copies(i):
        at = span(c * part_rows + r * block + i * chunk, chunk)

        def one(n, src, dst, peer):
            return pltpu.make_async_remote_copy(
                src_ref=src,
                dst_ref=dst,
                send_sem=gather_sem.at[2 + 2 * (n * chunks + i)],
                recv_sem=gather_sem.at[3 + 2 * (n * chunks + i)],
                device_id=peer,
                device_id_type=MESH,
            )

        got = span(c * part_rows + (1 - r) * block + i * chunk, chunk)
        return (
            one(0, branch.at[at, lo], branch.at[at, hi], x_peer),
            one(1, branch.at[at, hi], branch.at[at, lo], x_peer),
            one(2, branch.at[at], branch.at[at], c_peer),
            one(3, branch.at[got], branch.at[got], c_peer),
        )

    def norm_two_task(i):
        at = span(i * chunk, chunk)
        grads = acc_rows[at]
        grad, terms = norm_rows(hid[at], at, grads, params_ref[2:3])
        norm_sums[2:3] = norm_sums[2:3] + jnp.sum(terms, axis=0, keepdims=True)
        norm_sums[3:4] = norm_sums[3:4] + jnp.sum(grads, axis=0, keepdims=True)
        grad = own[at].astype(F32) + grad
        grad_rows[at] = grad
        branch[span(c * part_rows + r * block + i * chunk, chunk)] = grad.astype(BF)
        start(gather_copies(i)[:3])

    def forward_task(i):
        copies = gather_copies(i)
        copies[0].wait_recv()
        copies[1].wait_recv()
        copies[3].start()

    def gathered_task(i):
        copies = gather_copies(i)
        copies[2].wait_recv()
        copies[3].wait_recv()
        for one in copies:
            one.wait_send()

    def att_grad_task(i):
        at = span(i * part_rows, part_rows)
        att_grad[at] = nt(branch[at], w_o[...]).astype(BF)

    def attention_task(i):
        p, second = i // 2, lax.rem(i, 2)
        s = lax.rem(p, 2)
        lanes0 = span(p * 128, 128)

        @pl.when(second == 0)
        def _():
            pl.when(p + 1 < pairs)(lambda: start(heads_load(p + 1)))
            wait(heads_load(p))
            key_sums[...] = jnp.zeros_like(key_sums)
            value_sums[...] = jnp.zeros_like(value_sums)

        def window(begin, low, end):
            bar = barred(starts_ref[begin:end], begin, low, end)
            q2, k2, v2 = heads[s, 0, begin:end], heads[s, 1, low:end], heads[s, 2, low:end]
            g2, a2 = att_grad[begin:end, lanes0], att[begin:end, lanes0]
            outs, dks, dvs = [], [], []
            for h in range(2):
                lanes = slice(h * HEAD, (h + 1) * HEAD)
                q, k, v, g = q2[:, lanes], k2[:, lanes], v2[:, lanes], g2[:, lanes]
                weights = jnp.exp(nt(q, k) + bar - head_logs[s, begin:end, h : h + 1])
                dvs.append(tn(weights.astype(BF), g))
                inside = jnp.sum(g.astype(F32) * a2[:, lanes].astype(F32), axis=1, keepdims=True)
                grads = (weights * (nt(g, v) - inside)).astype(BF)
                outs.append(jnp.dot(grads, k, preferred_element_type=F32))
                dks.append(tn(grads, q))
            table = (table_ref[0, begin:end], -table_ref[1, begin:end], -table_ref[2, begin:end])
            dq = turned(jnp.concatenate(outs, axis=1) * HEAD ** (-0.5), table).astype(BF)
            joint[begin:end, lanes0] = dq
            bias_sums[0:1, lanes0] = bias_sums[0:1, lanes0] + jnp.sum(dq.astype(F32), axis=0, keepdims=True)
            key_sums[low:end] += jnp.concatenate(dks, axis=1)
            value_sums[low:end] += jnp.concatenate(dvs, axis=1)

        spans = list(windows(length))
        middle = len(spans) // 2

        @pl.when(second == 0)
        def _():
            for one in spans[:middle]:
                window(*one)

        @pl.when(second == 1)
        def _():
            for one in spans[middle:]:
                window(*one)
            table = (table_ref[0], -table_ref[1], -table_ref[2])
            dk = turned(key_sums[...], table).astype(BF)
            dv = value_sums[...].astype(BF)
            for k, v in ((1, dk), (2, dv)):
                joint[:, span(k * units + p * 128, 128)] = v
                bias_sums[k : k + 1, lanes0] = jnp.sum(v.astype(F32), axis=0, keepdims=True)

    def grad_copies(i):
        at = span(i * chunk, chunk)
        n = 2 + 8 * chunks + 2 * i
        return (
            pltpu.make_async_remote_copy(
                src_ref=grad_rows.at[at, hi],
                dst_ref=grad_got.at[at],
                send_sem=gather_sem.at[n],
                recv_sem=gather_sem.at[n + 1],
                device_id=x_peer,
                device_id_type=MESH,
            ),
            local_copy(10 + i, grad_rows.at[at, lo], grad_own.at[at]),
        )

    def norm_one_task(i):
        pl.when(i == 0)(lambda: load_inputs.wait())
        at = span(i * chunk, chunk)
        grads = acc_rows[at]
        grad, terms = norm_rows(own[at].astype(F32), at, grads, params_ref[0:1])
        norm_sums[0:1] = norm_sums[0:1] + jnp.sum(terms, axis=0, keepdims=True)
        norm_sums[1:2] = norm_sums[1:2] + jnp.sum(grads, axis=0, keepdims=True)
        grad_rows[at] = grad_rows[at] + grad
        start(grad_copies(i))

    def small_copy(n, peer, cols=None):
        src, dst = small_src.at[n], small_in.at[n]
        if cols is not None:
            src, dst = src.at[:, cols], dst.at[:, cols]
        return pltpu.make_async_remote_copy(
            src_ref=src,
            dst_ref=dst,
            send_sem=small_sem.at[n],
            recv_sem=small_sem.at[8 + n],
            device_id=peer,
            device_id_type=MESH,
        )

    def small_hop(n, peer, step_peer):
        small_copy(n, peer).wait_recv()
        small_src[n + 1] = small_src[n] + small_in[n]
        small_copy(n + 1, step_peer).start()

    first_cols = pl.ds(0, half + units)

    def small_task(i):
        @pl.when(i == 0)
        def _():
            small_src[0, :, :half] = norm_sums[:, half:]
            small_src[0, :, half : half + units] = bias_sums[...]
            small_copy(0, x_peer, first_cols).start()

        @pl.when(i == 1)
        def _():
            small_copy(0, x_peer, first_cols).wait_recv()
            small_src[1, :, :half] = norm_sums[:, :half] + small_in[0, :, :half]
            small_copy(1, c_peer, lo).start()

        @pl.when(i == 2)
        def _():
            small_copy(1, c_peer, lo).wait_recv()
            small_src[2, :, :half] = small_src[1, :, :half] + small_in[1, :, :half]
            small_src[2, :, half : half + units] = bias_sums[...]
            small_src[2, :, half + units :] = small_in[0, :, half : half + units]
            small_copy(2, y_peer).start()

        @pl.when(i == 3)
        def _():
            small_hop(2, y_peer, e_peer)

        @pl.when(i == 4)
        def _():
            small_copy(3, e_peer).wait_recv()
            small_src[4] = small_src[3] + small_in[3]
            pl.when(mid)(lambda: small_copy(4, m_peer).start())

        @pl.when((i == 5) & mid)
        def _():
            small_hop(4, m_peer, e_peer)

        @pl.when(i == 6)
        def _():
            @pl.when(mid)
            def _():
                small_out[...] = small_src[5]
                small_copy(4, m_peer).wait_send()
                small_copy(5, e_peer).wait_send()

            @pl.when(outer)
            def _():
                small_copy(5, e_peer).wait_recv()
                small_out[...] = small_in[5]

            for n, cols in ((0, first_cols), (1, lo), (2, None), (3, None)):
                small_copy(n, x_peer, cols).wait_send()

    norm_sums[...] = jnp.zeros_like(norm_sums)
    bias_sums[...] = jnp.zeros_like(bias_sums)
    gates = hidden // 128
    at_two = max(gates, pieces + 3)
    at_norm = at_two + pieces + 3
    at_att = at_norm + chunks // 2 + 3
    at_heads = at_att + 2
    at_one = at_heads + 2 * pairs
    at_last = at_one + pieces + 3

    def tasks(t):
        within(t, 0, gates, gate_task)
        summed(t, 0, 0, feed_product, down_columns_load)
        within(t, at_two, 1, result_task)
        pl.when(t == at_two - 1)(lambda: start(gate_load(0)))
        summed(t, at_two, pieces, act_two_product, gate_load)

        def two(task):
            def both(i):
                task(2 * i)
                task(2 * i + 1)

            return both

        within(t, at_norm + 3, chunks // 2, two(gathered_task))
        within(t, at_norm + 2, chunks // 2, two(forward_task))
        within(t, at_norm, chunks // 2, two(norm_two_task))

        @pl.when(t == at_att)
        def _():
            load_wo.wait()
            load_att.wait()
            load_inputs.start()
            start(heads_load(0))

        within(t, at_att, 2, att_grad_task)
        within(t, at_heads, 2 * pairs, attention_task)
        pl.when(t == at_one - 1)(lambda: start(qkv_load(0)))
        summed(t, at_one, 2 * pieces, act_one_product, qkv_load)
        within(t, at_last, chunks // 2, two(norm_one_task))
        within(t, at_last + chunks // 2, 7, small_task)

    def body(step, carry):
        t = step - LEAD

        def free_all(u):
            y_copy(u).wait_send()

        def free_mid(u):
            m_copy(u).wait_send()
            n_copy(u).wait_send()

        def free_out(u):
            e_out(u).wait_send()
            g_mid(u).wait_send()
            keep_own(u, full.at[short(u)]).wait()

        def free_far(u):
            g_out(u).wait_send()
            keep_own(u, e_dst.at[slot(u)]).wait()

        def free_got(u):
            f_out(u).wait_send()
            keep_got(u).wait()

        stage(t + LEAD - 2, lambda u: x_copy(u).wait_send())
        stage(t - 2, free_all)
        stage(t - 3, lambda u: e_in(u).wait_send(), outer)
        stage(t - 3, lambda u: f_in(u).wait_send(), outer)
        stage(t - 4, free_mid, mid)
        stage(t - 5, lambda u: k_copy(u).wait_send(), mid)
        stage(t - 6, lambda u: w_copy(u).wait_send(), mid)
        stage(t - 5, free_out, mid)
        stage(t - 5, free_far, outer)
        stage(t - 7, free_got, mid)
        stage(t - 5, lambda u: g_mid(u).wait_recv(), mid)
        stage(t - 6, lambda u: g_out(u).wait_recv(), outer)
        stage(t - 6, lambda u: f_out(u).wait_recv(), outer)
        stage(t - 4, t2_e, mid)
        stage(t - 3, t2_d, mid)
        stage(t - 2, t2_c, mid)
        stage(t - 1, t2_b, mid)
        stage(t, t2_a)
        stage(t - 4, t1_d, outer)
        stage(t - 3, t1_c, mid)
        stage(t - 2, t1_b, mid)
        stage(t - 1, t1_a)
        stage(t, produce_own)
        stage(t + LEAD, produce_far)
        tasks(step)
        return carry

    lax.fori_loop(0, max(total + 7 + LEAD, at_last + chunks // 2 + 7), body, 0)
    result_copy().wait()
    store_result.wait()
    for i in range(chunks):
        wait(grad_copies(i))


def back(
    inner,
    cotangent,
    gate,
    up,
    act_two,
    attended,
    queries,
    keys,
    values,
    logs,
    starts,
    table,
    act_one,
    hidden_state,
    own_inputs,
    params,
    w_down,
    w_gate,
    w_out,
    w_qkv,
):
    length, width = cotangent.shape
    hidden, units = inner.shape[1], attended.shape[1]
    half, part_rows, block = width // 2, length // 2, length // 4
    area, chunks = BR * BC, block // 64
    counts = [hidden * half // area, half * 2 * hidden // area, units * half // area, half * 3 * units // area]
    bases, end = [], 0
    for blocks in counts:
        bases.append(-(-end // blocks) * blocks)
        end = bases[-1] + blocks

    def bf(*shape):
        return jax.ShapeDtypeStruct(shape, BF)

    def f32(*shape):
        return jax.ShapeDtypeStruct(shape, F32)

    outs = [
        bf(2, end, BR, BC),
        bf(block, half),
        bf(block, half),
        f32(block, half),
        f32(block, half),
        f32(8, half + 2 * units),
    ]
    any_spec, vmem_spec = pl.BlockSpec(memory_space=pl.ANY), pl.BlockSpec(memory_space=pltpu.VMEM)
    wide, thin = bf(SLOTS, BR, BC), bf(SLOTS, BR // 2, BC)
    scratch = [
        f32(8, width),
        f32(8, units),
        f32(6, 8, half + 2 * units),
        f32(6, 8, half + 2 * units),
        bf(2, BR, length),
        bf(2, length, BR),
        bf(length, max(hidden, 3 * units)),
        bf(length, width),
        bf(length, 2 * hidden),
        bf(length, units),
        bf(length, units),
        bf(2, 3, length, 128),
        f32(2, length, 2),
        f32(length, 128),
        f32(length, 128),
        bf(2, 128, width),
        bf(2, 2, length, 128),
        bf(2, hidden, BC),
        bf(2, 2, BC, max(hidden, 2 * units)),
        bf(units, width),
        bf(3, part_rows, BC),
        bf(3, part_rows, BC),
        bf(3, part_rows, BC),
        bf(4, block, BC),
        bf(4, block, BC),
        f32(block, width),
        f32(block, width),
        f32(block, width),
        bf(block, width),
        bf(block, width),
        bf(SHORT, BR, BC),
        bf(SHORT, BR, BC),
        bf(FAR_SLOTS, BR, BC),
        thin,
        bf(SHORT, BR // 2, BC),
        thin,
        bf(SHORT, BR // 2, BC),
        thin,
        bf(SHORT, BR // 2, BC),
        wide,
        bf(SHORT, BR, BC),
        thin,
        bf(SHORT, BR // 2, BC),
        thin,
        wide,
    ]
    dma = pltpu.SemaphoreType.DMA
    flops = 2 * length * width * (8 * units + 6 * hidden) + 2 * length * 640 * 5 * units
    outs = pl.pallas_call(
        functools.partial(back_kernel, bases),
        out_shape=outs,
        in_specs=[any_spec] * 10 + [vmem_spec] * 2 + [any_spec] * 3 + [vmem_spec] + [any_spec] * 4,
        out_specs=[any_spec] * 5 + [vmem_spec],
        scratch_shapes=[pltpu.VMEM(v.shape, v.dtype) for v in scratch]
        + [dma((10 + chunks,)), dma((24,)), dma((14,)), dma((2 + 10 * chunks,)), dma((16,))]
        + [dma((SEMAPHORES,))] * 22
        + [dma((SLOTS,))] * 2,
        compiler_params=pltpu.CompilerParams(
            collective_id=1, has_side_effects=True, vmem_limit_bytes=63 * 2**20
        ),
        cost_estimate=pl.CostEstimate(flops=flops, bytes_accessed=200 * 2**20, transcendentals=length * 8192),
    )(
        inner,
        cotangent,
        gate,
        up,
        act_two,
        attended,
        queries,
        keys,
        values,
        logs,
        starts,
        table,
        act_one,
        hidden_state,
        own_inputs,
        params,
        w_down,
        w_gate,
        w_out,
        w_qkv,
    )
    return outs[0], bases, *outs[1:]


def spread_kernel(bases, sums, gate_up_out, qkv_out, out_out, down_out, *scratch):
    buffers, (load_sem, store_sem) = scratch[:-2], scratch[-2:]
    r = lax.axis_index("row")
    half, hidden = gate_up_out.shape[0], gate_up_out.shape[2] // 2
    units = out_out.shape[0] // 2
    size = BR * BC // half
    rows = BR // 2

    def span(start, count):
        return pl.ds(pl.multiple_of(start, count), count)

    def widen_pair(src, dst, s):
        def some(i, carry):
            at = span(i * 64, 64)
            for j in range(src.shape[1]):
                for first in range(0, BC, 128):
                    unit = j * BC + first
                    dst[s, at, unit // hidden, unit % hidden : unit % hidden + 128] = src[
                        s, j, at, first : first + 128
                    ].astype(F32)
            return carry

        lax.fori_loop(0, rows // 64, some, 0)

    def widen_kinds(src, dst, s):
        per = units // BC
        for j in range(src.shape[1]):
            dst[s, j // per, :, j % per * BC : (j % per + 1) * BC] = src[s, j].astype(F32)

    def widen_rows(src, dst, s):
        def some(k, carry):
            dst[s, span(k * size, size)] = src[s, k].astype(F32)
            return carry

        lax.fori_loop(0, src.shape[1], some, 0)

    tasks = []
    for w in range(2):
        side = r if w == 0 else 1 - r
        for i in range(half // rows):
            block, at = i * rows // BR, pl.ds(i * rows % BR, rows)
            per = 2 * hidden // BC
            tasks.append(
                (
                    0,
                    widen_pair,
                    sums.at[w, pl.ds(bases[1] + block * per, per), at],
                    gate_up_out.at[pl.ds(i * rows, rows), :, span(side * hidden, hidden)],
                )
            )
    for w in range(2):
        side = r if w == 0 else 1 - r
        for q in range(half // BC):
            at = pl.ds(q * size, size)
            for n, base, out, count in ((1, bases[0], down_out, hidden), (3, bases[2], out_out, units)):
                tasks.append(
                    (
                        n,
                        widen_rows,
                        sums.at[w, pl.ds(base, count // size), at],
                        out.at[span(side * count, count), pl.ds(q * BC, BC)],
                    )
                )
        for i in range(half // rows):
            block, at = i * rows // BR, pl.ds(i * rows % BR, rows)
            per = 3 * units // BC
            tasks.append(
                (
                    2,
                    widen_kinds,
                    sums.at[w, pl.ds(bases[3] + block * per, per), at],
                    qkv_out.at[:, pl.ds(i * rows, rows), span(side * units, units)],
                )
            )

    uses, plan = [0] * 4, []
    for n, widen, src, dst in tasks:
        s = uses[n] % 4
        uses[n] += 1
        held, wide = buffers[2 * n], buffers[2 * n + 1]
        load = pltpu.make_async_copy(src, held.at[s], load_sem.at[4 * n + s])
        store = pltpu.make_async_copy(wide.at[s], dst, store_sem.at[4 * n + s])
        plan.append((n, s, widen, held, wide, load, store))
    busy = {}
    ahead = 4
    for step in plan[:ahead]:
        step[5].start()
    for i, (n, s, widen, held, wide, load, store) in enumerate(plan):
        load.wait()
        if (n, s) in busy:
            busy.pop((n, s)).wait()
        widen(held, wide, s)
        store.start()
        busy[n, s] = store
        if i + ahead < len(plan):
            plan[i + ahead][5].start()
    for store in busy.values():
        store.wait()


def spread(sums, bases, half, units, hidden):
    size, rows = BR * BC // half, BR // 2
    shapes = [(half, 2, 2 * hidden), (3, half, 2 * units), (2 * units, half), (2 * hidden, half)]
    pair, kinds = 2 * hidden // BC, 3 * units // BC
    buffers = [
        ((4, pair, rows, BC), BF),
        ((4, rows, 2, hidden), F32),
        ((4, hidden // size, size, BC), BF),
        ((4, hidden, BC), F32),
        ((4, kinds, rows, BC), BF),
        ((4, 3, rows, units), F32),
        ((4, units // size, size, BC), BF),
        ((4, units, BC), F32),
    ]
    any_spec = pl.BlockSpec(memory_space=pl.ANY)
    return pl.pallas_call(
        functools.partial(spread_kernel, bases),
        out_shape=[jax.ShapeDtypeStruct(v, F32) for v in shapes],
        in_specs=[any_spec],
        out_specs=[any_spec] * 4,
        scratch_shapes=[pltpu.VMEM(*v) for v in buffers] + [pltpu.SemaphoreType.DMA((16,))] * 2,
        compiler_params=pltpu.CompilerParams(vmem_limit_bytes=56 * 2**20),
    )(sums)


def front_kernel(
    tokens,
    starts_ref,
    table_ref,
    params_in,
    bias_ref,
    qkv_w,
    out_w,
    gate_w,
    down_w,
    cotangent,
    act_one,
    q_out,
    k_out,
    v_out,
    att_out,
    log_out,
    hid_out,
    act_two,
    gate_out,
    up_out,
    inner_out,
    wq_out,
    wo_out,
    wg_out,
    wd_out,
    cot_out,
    own_out,
    params_ref,
    tok,
    act,
    wq,
    wo,
    wg,
    gate_far,
    gate_own,
    qs,
    ks,
    vs,
    att,
    logs,
    core_in,
    row_src,
    row_in,
    own_in,
    hid,
    tile,
    send_sem,
    recv_sem,
    load_sem,
    store_sem,
):
    r, c, d = lax.axis_index("row"), lax.axis_index("col"), lax.axis_index("dp")
    y, zp = lax.rem(d, 2), lax.rem(d // 2, 2)
    length, width = tok.shape
    half = width // 2
    part, block = length // 2, length // 4
    units, hidden = qs.shape[1], wg.shape[2]
    sub = zp * 2 + y
    dy, dz = 1 - 2 * y, 2 - 4 * zp
    row_peer, col_peer = {"row": 1 - r}, {"col": 1 - c}
    near = ({"dp": d + dy}, {"dp": d + dz}, {"dp": d + dy + dz})

    barrier = pltpu.get_barrier_semaphore()
    for peer in (row_peer, col_peer) + near:
        pl.semaphore_signal(barrier, inc=1, device_id=peer, device_id_type=MESH)

    stores = []

    def span(start, size):
        return pl.ds(pl.multiple_of(start, size), size)

    def load(n, src, dst):
        copy = pltpu.make_async_copy(src, dst, load_sem.at[n])
        copy.start()
        return copy

    def store(src, dst):
        copy = pltpu.make_async_copy(src, dst, store_sem.at[len(stores)])
        copy.start()
        stores.append(copy)
        return copy

    def remote(n, src, dst, peer):
        return pltpu.make_async_remote_copy(
            src_ref=src,
            dst_ref=dst,
            send_sem=send_sem.at[n],
            recv_sem=recv_sem.at[n],
            device_id=peer,
            device_id_type=MESH,
        )

    mine, theirs = span(r * units, units), span((1 - r) * units, units)
    own_rows, far_rows = span(c * part, part), span((1 - c) * part, part)
    lo, hi = pl.ds(0, half), pl.ds(half, half)
    quarter, eighth = half // 4, half // 8
    down_quarter = hidden // 4

    load_tok = load(0, tokens, tok.at[own_rows, lo])
    load_q = load(1, qkv_w.at[:, :, mine], wq.at[:, lo])
    load_o = load(2, out_w.at[mine], wo.at[:, lo])
    gate_cols = span(r * hidden, hidden)

    def load_gate(i):
        return load(3 + i % 2, gate_w.at[pl.ds(i * eighth, eighth), :, gate_cols], gate_own.at[i % 2])

    load_d = load(5, down_w.at[span(r * hidden, hidden)], wd_out.at[:, lo])
    load_c = load(6, cotangent, cot_out.at[own_rows, lo])
    gates = [load_gate(0), load_gate(1)]

    rows_sub = span(sub * quarter, quarter)
    rows_far = span(half + sub * quarter, quarter)
    q_x = remote(0, qkv_w.at[:, rows_sub, theirs], wq.at[:, rows_far], row_peer)
    q_n = [remote(1 + k, wq.at[:, rows_far], wq.at[:, rows_far], p) for k, p in enumerate(near)]
    tok_x = remote(4, tokens, tok.at[own_rows, hi], row_peer)
    tok_c = remote(5, tokens, tok.at[own_rows, lo], col_peer)
    tok_f = remote(6, tok.at[own_rows, hi], tok.at[own_rows, hi], col_peer)
    out_rows = units // 4
    out_sub = span(sub * out_rows, out_rows)
    o_x = remote(
        7, out_w.at[span((1 - r) * units + sub * out_rows, out_rows)], wo.at[out_sub, hi], row_peer
    )
    o_n = [remote(8 + k, wo.at[out_sub, hi], wo.at[out_sub, hi], p) for k, p in enumerate(near)]
    g_x = remote(
        11, gate_w.at[rows_sub, :, span((1 - r) * hidden, hidden)], gate_far.at[sub], row_peer
    )
    g_n = [remote(12 + k, gate_far.at[sub], gate_far.at[sub], p) for k, p in enumerate(near)]
    down_sub = span(sub * down_quarter, down_quarter)
    d_x = remote(
        15,
        down_w.at[span((1 - r) * hidden + sub * down_quarter, down_quarter)],
        wd_out.at[down_sub, hi],
        row_peer,
    )
    d_n = [
        remote(16 + k, wd_out.at[down_sub, hi], wd_out.at[down_sub, hi], p)
        for k, p in enumerate(near)
    ]
    c_x = remote(19, cotangent, cot_out.at[own_rows, hi], row_peer)
    c_c = remote(20, cotangent, cot_out.at[own_rows, lo], col_peer)
    c_f = remote(21, cot_out.at[own_rows, hi], cot_out.at[own_rows, hi], col_peer)
    rs_c = remote(22, act.at[far_rows], core_in, col_peer)
    rs_x = remote(23, row_src, row_in, row_peer)
    own_block = span(c * part + r * block, block)
    x_block = span(c * part + (1 - r) * block, block)
    ag_x = [
        remote(24, tok.at[own_block, lo], tok.at[own_block, hi], row_peer),
        remote(25, tok.at[own_block, hi], tok.at[own_block, lo], row_peer),
    ]
    ag_c = remote(26, tok.at[own_block], tok.at[own_block], col_peer)
    ag_f = remote(27, tok.at[x_block], tok.at[x_block], col_peer)

    p_x = remote(28, params_in, params_ref.at[:, hi], row_peer)

    def start(copies):
        for copy in copies:
            copy.start()

    def arrived(copies):
        for copy in copies:
            copy.wait_recv()

    def part_gate(ref, at):
        wg[0, at] = ref[:, 0, :]
        wg[1, at] = ref[:, 1, :]

    pl.semaphore_wait(barrier, 5)
    p_x.start()
    params_ref[:, :half] = params_in[...]
    q_x.start()
    tok_c.start()
    c_c.start()
    for i in range(8):
        if i == 4:
            q_x.wait_recv()
            start(q_n)
            tok_x.start()
        gates[i].wait()
        part_gate(gate_own.at[i % 2], pl.ds(i * eighth, eighth))
        if i + 2 < 8:
            gates.append(load_gate(i + 2))
    tok_x.wait_recv()
    tok_f.start()
    o_x.start()
    g_x.start()

    load_tok.wait()
    p_x.wait_recv()
    tok_c.wait_recv()

    def normed(v, at):
        mean = jnp.sum(v, axis=1, keepdims=True) / width
        spread_of = jnp.sum(v * v, axis=1, keepdims=True) / width - mean * mean
        v = (v - mean) * lax.rsqrt(spread_of + EPSILON)
        return (v * params_ref[at : at + 1] + params_ref[at + 1 : at + 2]).astype(BF)

    norm_rows = 64

    def norm_one(base):
        def body(i, carry):
            at = span(base + i * norm_rows, norm_rows)
            act[at] = normed(tok[at].astype(F32), 0)
            return carry

        lax.fori_loop(0, part // norm_rows, body, 0)

    norm_one(c * part)
    own_in[...] = tok[own_block]
    tok_f.wait_recv()
    norm_one((1 - c) * part)
    store(act, act_one)
    store(own_in, own_out)

    load_q.wait()
    arrived(q_n)
    o_x.wait_recv()
    start(o_n)
    store(wq, wq_out)
    chunk = 256

    def project(i, carry):
        at = span(i * chunk, chunk)
        rows = act[at]
        for kind, ref in enumerate((qs, ks, vs)):
            out = jnp.dot(rows, wq[kind], preferred_element_type=F32) + bias_ref[kind : kind + 1]
            if kind == 2:
                ref[at] = out.astype(BF)
                continue
            table = (table_ref[0, at], table_ref[1, at], table_ref[2, at])
            for g in range(units // 128):
                lanes = slice(g * 128, (g + 1) * 128)
                v = turned(out[:, lanes], table).astype(BF)
                if kind == 0:
                    v = (v.astype(F32) * HEAD ** (-0.5)).astype(BF)
                ref[at, lanes] = v
        return carry

    lax.fori_loop(0, length // chunk, project, 0)
    for ref, out in ((qs, q_out), (ks, k_out), (vs, v_out)):
        store(ref, out)

    pairs = units // 128

    def attend(p, carry):
        @pl.when(p == pairs // 2)
        def _():
            g_x.wait_recv()
            start(g_n)
            d_x.start()

        lane0 = p * 128
        q2 = qs[:, span(lane0, 128)]
        k2 = ks[:, span(lane0, 128)]
        v2 = vs[:, span(lane0, 128)]
        for begin, low, end in windows(length):
            bar = barred(starts_ref[begin:end], begin, low, end)
            outs = []
            for h in range(2):
                lanes = slice(h * HEAD, (h + 1) * HEAD)
                scores = nt(q2[begin:end, lanes], k2[low:end, lanes]) + bar
                maxima = jnp.max(scores, axis=1, keepdims=True)
                shifted = jnp.exp(scores - maxima).astype(BF)
                wide = jnp.concatenate([v2[low:end, lanes], jnp.ones((end - low, HEAD), BF)], axis=1)
                got = jnp.dot(shifted, wide, preferred_element_type=F32)
                totals = got[:, HEAD : HEAD + 1]
                outs.append(got[:, :HEAD] / totals)
                logs[p, begin:end, h : h + 1] = maxima + jnp.log(totals)
            out = jnp.concatenate(outs, axis=1)
            att[begin:end, span(lane0, 128)] = out.astype(BF)
        return carry

    lax.fori_loop(0, pairs, attend, 0)
    store(att, att_out)
    store(logs, log_out)

    load_o.wait()
    arrived(o_n)
    store(wo, wo_out)
    stores[0].wait()
    tok_f.wait_send()

    def branch(base):
        def body(i, carry):
            at = span(base + i * chunk, chunk)
            act[at] = jnp.dot(att[at], wo[...], preferred_element_type=F32).astype(BF)
            return carry

        lax.fori_loop(0, part // chunk, body, 0)

    branch((1 - c) * part)
    rs_c.start()
    branch(c * part)
    rs_c.wait_recv()
    row_src[...] = act[x_block] + core_in[span((1 - r) * block, block)]
    rs_x.start()
    part_gate(gate_far.at[sub], span(half + sub * quarter, quarter))
    subs = (zp * 2 + 1 - y, (1 - zp) * 2 + y, (1 - zp) * 2 + 1 - y)
    rs_x.wait_recv()
    hid_rows = 64

    def norm_two(i, carry):
        at = span(i * hid_rows, hid_rows)
        kept = act[span(c * part + r * block + i * hid_rows, hid_rows)].astype(F32)
        kept = kept + core_in[span(r * block + i * hid_rows, hid_rows)].astype(F32)
        got = row_in[at].astype(F32)
        kept = kept + jnp.concatenate([got[:, half:], got[:, :half]], axis=1)
        kept = own_in[at].astype(F32) + kept
        hid[at] = kept
        tok[span(c * part + r * block + i * hid_rows, hid_rows)] = normed(kept, 2)
        return carry

    lax.fori_loop(0, block // hid_rows, norm_two, 0)
    start(ag_x)
    ag_c.start()
    store(hid, hid_out)
    d_x.wait_recv()
    start(d_n)
    c_x.start()
    for k in range(3):
        g_n[k].wait_recv()
        part_gate(gate_far.at[subs[k]], span(half + subs[k] * quarter, quarter))
    store(wg, wg_out)

    stores_of = []
    columns = [(at, min(512, hidden - at)) for at in range(0, hidden, 512)]
    for b in range(4):
        cc = c if b % 2 == 0 else 1 - c
        rr = r if b < 2 else 1 - r
        at = span(cc * part + rr * block, block)
        if b == 1:
            ag_c.wait_recv()
        elif b == 2:
            arrived(ag_x)
            ag_f.start()
        elif b == 3:
            ag_f.wait_recv()
        s = b % 2
        for copy in stores_of[3 * (b - 2) : 3 * (b - 1)] if b >= 2 else ():
            copy.wait()
        rows = tok[at]
        for first, size in columns:
            cols = slice(first, first + size)
            gate = jnp.dot(rows, wg[0, :, cols], preferred_element_type=F32)
            up = jnp.dot(rows, wg[1, :, cols], preferred_element_type=F32)
            tile[s, 0, :, cols] = gate.astype(BF)
            tile[s, 1, :, cols] = up.astype(BF)
            tile[s, 2, :, cols] = (gate / (1.0 + jnp.exp(-gate)) * up).astype(BF)
        for k, out in enumerate((gate_out, up_out, inner_out)):
            copy = pltpu.make_async_copy(tile.at[s, k], out.at[at], load_sem.at[7 + 3 * s + k])
            copy.start()
            stores_of.append(copy)
    store(tok, act_two)
    c_x.wait_recv()
    load_c.wait()
    c_f.start()
    for copy in stores_of[6:] + stores[1:] + [load_d]:
        copy.wait()
    arrived(d_n)
    c_c.wait_recv()
    c_f.wait_recv()
    for copy in [p_x, q_x, tok_x, tok_c, o_x, g_x, d_x, c_x, c_c, c_f, rs_c, rs_x, ag_c, ag_f] + (
        q_n + o_n + g_n + d_n + ag_x
    ):
        copy.wait_send()


def front(tokens, starts, table, params, bias, qkv_w, out_w, gate_w, down_w, cotangent):
    part, half = tokens.shape
    length, width, block = 2 * part, 2 * half, part // 2
    units, hidden = out_w.shape[0] // 2, down_w.shape[0] // 2
    any_spec, vmem_spec = pl.BlockSpec(memory_space=pl.ANY), pl.BlockSpec(memory_space=pltpu.VMEM)
    pairs = units // 128

    def bf(*shape):
        return jax.ShapeDtypeStruct(shape, BF)

    def f32(*shape):
        return jax.ShapeDtypeStruct(shape, F32)

    outs = [
        bf(length, width),
        bf(length, units),
        bf(length, units),
        bf(length, units),
        bf(length, units),
        f32(pairs, length, 2),
        f32(block, width),
        bf(length, width),
        bf(length, hidden),
        bf(length, hidden),
        bf(length, hidden),
        bf(3, width, units),
        bf(units, width),
        bf(2, width, hidden),
        bf(hidden, width),
        bf(length, width),
        bf(block, width),
        f32(8, width),
    ]
    scratch = [
        bf(length, width),
        bf(length, width),
        bf(3, width, units),
        bf(units, width),
        bf(2, width, hidden),
        bf(4, half // 4, 2, hidden),
        bf(2, half // 8, 2, hidden),
        bf(length, units),
        bf(length, units),
        bf(length, units),
        bf(length, units),
        f32(pairs, length, 2),
        bf(part, width),
        bf(block, width),
        bf(block, width),
        bf(block, width),
        f32(block, width),
        bf(2, 3, block, hidden),
    ]
    dma = pltpu.SemaphoreType.DMA
    return pl.pallas_call(
        front_kernel,
        out_shape=outs,
        in_specs=[any_spec] + [vmem_spec] * 4 + [any_spec] * 5,
        out_specs=[any_spec] * (len(outs) - 1) + [vmem_spec],
        scratch_shapes=[pltpu.VMEM(v.shape, v.dtype) for v in scratch]
        + [dma((29,)), dma((29,)), dma((13,)), dma((16,))],
        compiler_params=pltpu.CompilerParams(
            collective_id=2, has_side_effects=True, vmem_limit_bytes=62 * 2**20
        ),
        cost_estimate=pl.CostEstimate(
            flops=2 * length * width * (4 * units + 2 * hidden),
            bytes_accessed=100 * 2**20,
            transcendentals=length * 2048,
        ),
    )(tokens, starts, table, params, bias, qkv_w, out_w, gate_w, down_w, cotangent)


def local(
    tokens,
    segments,
    ln1_gain,
    ln1_bias,
    qkv_weight,
    qkv_bias,
    out_weight,
    ln2_gain,
    ln2_bias,
    gate_up_weight,
    down_weight,
    cotangent,
):
    place = Place()
    r, c = place.r, place.c
    ids = segments[0]
    length = ids.shape[0]
    factor = HEAD ** (-0.5)
    half = qkv_weight.shape[0]
    units = qkv_weight.shape[2] // 2
    heads = units // HEAD
    hidden = gate_up_weight.shape[2] // 2

    none = jnp.zeros_like(ln1_gain)
    params = jnp.stack([ln1_gain, ln1_bias, ln2_gain, ln2_bias] + [none] * 4)
    firsts = first_places(ids)
    table = rotary_table(jnp.arange(length, dtype=jnp.int32) - firsts)
    starts = firsts[:, None]
    bias = piece(qkv_bias, r, 2, 1)
    (
        act_one,
        queries,
        keys,
        values,
        attended,
        logs,
        hidden_state,
        act_two,
        gate,
        up,
        inner,
        w_qkv,
        w_out,
        w_gate,
        w_down,
        cot_all,
        own_inputs,
        params,
    ) = front(
        tokens,
        starts,
        table,
        params,
        bias,
        qkv_weight.transpose(1, 0, 2),
        out_weight,
        gate_up_weight,
        down_weight,
        cotangent,
    )
    if place.count == 8:
        sums, bases, result, result_far, input_grad, input_far, small = back(
            inner,
            cot_all,
            gate,
            up,
            act_two,
            attended,
            queries,
            keys,
            values,
            logs,
            starts,
            table,
            act_one,
            hidden_state,
            own_inputs,
            params,
            w_down,
            w_gate,
            w_out,
            w_qkv,
        )
        result = ordered(r, result, result_far)
        input_grad = ordered(r, input_grad, input_far)
        norms = small[:4, :half]
        bias_grad = ordered(r, small[:3, half : half + units], small[:3, half + units :], 1)
        gate_up_grad, qkv_grad, out_grad, down_grad = spread(sums, bases, half, units, hidden)
        qkv_grad = qkv_grad.transpose(1, 0, 2)
    else:
        block = c * 2 + r
        own_inputs = own_inputs.astype(F32)
        _, normal_two, inverse_two = norm_forward(hidden_state, params[2], params[3])
        gate, up = gate.astype(F32), up.astype(F32)

        feed = reduce_blocks(dot(inner, w_down).astype(BF), place)
        result = (hidden_state + feed).astype(BF)
        result = ordered(r, result[:, :half], swap(result[:, half:], "row"))

        grad_inner = dot_t(cot_all, w_down)
        rate = 1.0 / (1.0 + jnp.exp(-gate))
        silu = gate * rate
        grad_gate = (grad_inner * up * (rate * (1.0 + gate * (1.0 - rate)))).astype(BF)
        grad_up = (grad_inner * silu).astype(BF)
        grad_two = jnp.stack([grad_gate, grad_up])
        grad_pair = jnp.concatenate([grad_gate, grad_up], axis=1)
        grad_act_two = reduce_blocks(
            jnp.einsum("ksf,kdf->sd", grad_two, w_gate, preferred_element_type=F32).astype(BF), place
        )
        grad_norm, ln2_gain_grad, ln2_bias_grad = norm_backward(
            grad_act_two, normal_two, inverse_two, params[2]
        )
        own_cot = piece(cot_all, block, 4).astype(F32)
        grad_hidden = own_cot + grad_norm
        grad_branch = gather_blocks(grad_hidden.astype(BF), place)
        grad_attended = dot_t(grad_branch, w_out).astype(BF)
        grad_joined = attention_backward(
            queries, keys, values, grad_attended, attended, logs, starts, table
        )
        grad_joined = jnp.concatenate(grad_joined, axis=1)
        bias_grad = jnp.sum(grad_joined, axis=0, dtype=F32)
        grad_kinds = grad_joined.reshape(length, 3, units)
        grad_act_one = reduce_blocks(
            jnp.einsum("sku,kdu->sd", grad_kinds, w_qkv, preferred_element_type=F32).astype(BF), place
        )
        _, normal_one, inverse_one = norm_forward(own_inputs, params[0], params[1])
        grad_norm, ln1_gain_grad, ln1_bias_grad = norm_backward(
            grad_act_one, normal_one, inverse_one, params[0]
        )
        input_grad = grad_hidden + grad_norm
        input_grad = ordered(r, input_grad[:, :half], swap(input_grad[:, half:], "row"))

        pairs = (
            ("D", act_two, grad_pair),
            ("D", act_one, grad_joined),
            ("U", attended, grad_branch),
            ("U", inner, cot_all),
        )
        sums = []
        for kind, left, right in pairs:
            both = t_dot(left, right).astype(BF)
            axis = 0 if kind == "D" else 1
            own, sent = jnp.split(both, 2, axis)
            sums.append([lax.psum(v, "dp").astype(F32) for v in (own, swap(sent, "row"))])
        gate_up_grad = ordered(r, *[v.reshape(half, 2, hidden) for v in sums[0]], 2)
        qkv_grad = ordered(r, *[v.reshape(half, 3, units) for v in sums[1]], 2)
        out_grad = ordered(r, *sums[2])
        down_grad = ordered(r, *sums[3])

        small = jnp.stack([ln1_gain_grad, ln1_bias_grad, ln2_gain_grad, ln2_bias_grad])
        small = small[:, :half] + swap(small[:, half:], "row")
        norms = lax.psum(small, ("dp", "col"))
        bias_grad = lax.psum(bias_grad.reshape(3, units), "dp")
        bias_grad = ordered(r, bias_grad, swap(bias_grad, "row"), 1)

    return (
        result,
        input_grad,
        norms[0],
        norms[1],
        qkv_grad,
        bias_grad,
        out_grad,
        norms[2],
        norms[3],
        gate_up_grad,
        down_grad,
    )


def solution(mesh):
    in_specs = (
        P(("dp", "col"), "row"),
        P("dp", None),
        P("row"),
        P("row"),
        P("row", None, "col"),
        P(None, "col"),
        P("col", "row"),
        P("row"),
        P("row"),
        P("row", None, "col"),
        P("col", "row"),
        P(("dp", "col"), "row"),
    )
    out_specs = (
        P(("dp", "col"), "row"),
        P(("dp", "col"), "row"),
        P("row"),
        P("row"),
        P("row", None, "col"),
        P(None, "col"),
        P("col", "row"),
        P("row"),
        P("row"),
        P("row", None, "col"),
        P("col", "row"),
    )
    return jax.shard_map(local, mesh=mesh, in_specs=in_specs, out_specs=out_specs, check_vma=False)
```

```python
import functools
import math

import jax
import jax.numpy as jnp
from jax import lax
from jax.experimental import pallas as pl
from jax.experimental.pallas import tpu as pltpu
from jax.sharding import PartitionSpec as P

HEAD = 64
ROT = 16
EPSILON = 1e-05
ROPE_BASE = 10000.0
NEGATIVE = -1e30
BF = jnp.bfloat16
F32 = jnp.float32
SWAP = [(0, 1), (1, 0)]
MESH = pl.DeviceIdType.MESH


def swap(v, axis):
    return lax.ppermute(v, axis, SWAP)


def ordered(flag, mine, other, axis=0):
    first = jnp.where(flag == 0, mine, other)
    second = jnp.where(flag == 0, other, mine)
    return jnp.concatenate([first, second], axis=axis)


def piece(v, index, count, axis=0):
    size = v.shape[axis] // count
    return lax.dynamic_slice_in_dim(v, index * size, size, axis)


def add(a, b):
    return (a.astype(F32) + b.astype(F32)).astype(BF)


def dot(a, b):
    return jnp.dot(a, b, preferred_element_type=F32)


def dot_t(a, b):
    return lax.dot_general(a, b, (((1,), (1,)), ((), ())), preferred_element_type=F32)


def t_dot(a, b):
    return lax.dot_general(a, b, (((0,), (0,)), ((), ())), preferred_element_type=F32)


class Place:
    def __init__(self):
        self.r = lax.axis_index("row")
        self.c = lax.axis_index("col")
        self.d = lax.axis_index("dp")
        self.count = lax.axis_size("dp")
        self.y = lax.rem(self.d, 2)
        self.zp = lax.rem(self.d // 2, 2)
        self.z = self.d // 2
        self.mid = (self.z == 1) | (self.z == 2)
        self.upper = (self.z >= 2).astype(jnp.int32)


def dp_perm(bit, count):
    return [(i, i ^ bit) for i in range(count)]


def cross(v):
    half = v.shape[-1] // 2
    return jnp.concatenate([v[..., half:], v[..., :half]], axis=-1)


def gather_blocks(block, place):
    other = cross(swap(block, "row"))
    pair = ordered(place.r, block, other)
    rest = swap(pair, "col")
    return ordered(place.c, pair, rest)


def reduce_blocks(partial, place):
    kept = piece(partial, place.c, 2)
    got = swap(piece(partial, 1 - place.c, 2), "col")
    held = add(kept, got)
    kept = piece(held, place.r, 2)
    got = cross(swap(piece(held, 1 - place.r, 2), "row"))
    return kept.astype(F32) + got.astype(F32)


def norm_forward(values, gain, shift):
    count = values.shape[-1]
    mean = jnp.sum(values, axis=-1, keepdims=True) / count
    spread = jnp.sum(values * values, axis=-1, keepdims=True) / count - mean * mean
    inverse = lax.rsqrt(spread + EPSILON)
    normal = (values - mean) * inverse
    return normal * gain + shift, normal, inverse


def norm_backward(grad, normal, inverse, gain):
    count = grad.shape[-1]
    scaled = grad * gain
    first = jnp.sum(scaled, axis=-1, keepdims=True) / count
    second = jnp.sum(scaled * normal, axis=-1, keepdims=True) / count
    grad_input = inverse * (scaled - first - normal * second)
    return grad_input, jnp.sum(grad * normal, axis=0), jnp.sum(grad, axis=0)


def first_places(segment_ids):
    return jnp.sum(segment_ids[None, :] < segment_ids[:, None], axis=1, dtype=jnp.int32)


def rotary_table(places):
    lane = jnp.arange(128, dtype=jnp.int32) % HEAD
    half_rot = ROT // 2
    inverse = jnp.exp((lane % half_rot).astype(F32) * (-2.0 / ROT) * math.log(ROPE_BASE))
    angles = places.astype(F32)[:, None] * inverse[None, :]
    cosines, sines = jnp.cos(angles), jnp.sin(angles)
    low, turns = (lane < half_rot)[None, :], (lane < ROT)[None, :]
    return jnp.stack(
        [
            jnp.where(turns, cosines, 1.0),
            jnp.where(low, -sines, 0.0),
            jnp.where(turns & ~low, sines, 0.0),
        ]
    )


LONGEST = 512
QB = 256

def windows(length):
    for begin in range(0, length, QB):
        low = max(0, (begin - LONGEST + 1) // QB * QB)
        yield begin, low, begin + QB


def barred(starts, begin, low, end):
    shape = (end - begin, end - low)
    query = begin + lax.broadcasted_iota(jnp.int32, shape, 0)
    key = low + lax.broadcasted_iota(jnp.int32, shape, 1)
    return jnp.where((key <= query) & (key >= starts), 0.0, NEGATIVE)


def turned(v, table):
    width = v.shape[-1]
    return v * table[0] + pltpu.roll(v, width - 8, 1) * table[1] + pltpu.roll(v, 8, 1) * table[2]


def nt(a, b):
    return lax.dot_general(a, b, (((1,), (1,)), ((), ())), preferred_element_type=F32)


def tn(a, b):
    return lax.dot_general(a, b, (((0,), (0,)), ((), ())), preferred_element_type=F32)


def backward_kernel(q_ref, k_ref, v_ref, g_ref, att_ref, log_ref, starts_ref, table_ref, dq_ref, dk_ref, dv_ref, dk_acc, dv_acc):
    length = q_ref.shape[0]
    dk_acc[...] = jnp.zeros_like(dk_acc)
    dv_acc[...] = jnp.zeros_like(dv_acc)
    for begin, low, end in windows(length):
        bar = barred(starts_ref[begin:end], begin, low, end)
        outs, dks, dvs = [], [], []
        for h in range(2):
            lanes = slice(h * HEAD, (h + 1) * HEAD)
            q, k, v, g = q_ref[begin:end, lanes], k_ref[low:end, lanes], v_ref[low:end, lanes], g_ref[begin:end, lanes]
            weights = jnp.exp(nt(q, k) + bar - log_ref[0, begin:end, h : h + 1])
            dvs.append(tn(weights.astype(BF), g))
            inner = jnp.sum(g.astype(F32) * att_ref[begin:end, lanes].astype(F32), axis=1, keepdims=True)
            grads = (weights * (nt(g, v) - inner)).astype(BF)
            outs.append(jnp.dot(grads, k, preferred_element_type=F32))
            dks.append(tn(grads, q))
        table = (table_ref[0, begin:end], -table_ref[1, begin:end], -table_ref[2, begin:end])
        dq_ref[begin:end] = turned(jnp.concatenate(outs, axis=1) * HEAD ** (-0.5), table).astype(BF)
        dk_acc[low:end] += jnp.concatenate(dks, axis=1)
        dv_acc[low:end] += jnp.concatenate(dvs, axis=1)
    table = (table_ref[0], -table_ref[1], -table_ref[2])
    dk_ref[...] = turned(dk_acc[...], table).astype(BF)
    dv_ref[...] = dv_acc[...].astype(BF)


def attention_backward(queries, keys, values, grads, attended, logs, starts, table):
    length, units = queries.shape
    pairs = units // 128
    same = pl.BlockSpec((length, 128), lambda p: (0, p))
    half = jax.ShapeDtypeStruct((length, units), BF)
    return pl.pallas_call(
        backward_kernel,
        grid=(pairs,),
        in_specs=[same] * 5
        + [
            pl.BlockSpec((1, length, 2), lambda p: (p, 0, 0)),
            pl.BlockSpec((length, 1), lambda p: (0, 0)),
            pl.BlockSpec((3, length, 128), lambda p: (0, 0, 0)),
        ],
        out_specs=[same] * 3,
        out_shape=[half] * 3,
        scratch_shapes=[pltpu.VMEM((length, 128), F32)] * 2,
        compiler_params=pltpu.CompilerParams(vmem_limit_bytes=48 * 2**20),
        cost_estimate=pl.CostEstimate(flops=pairs * 2 * length * 640 * 640, bytes_accessed=8 * 2**20, transcendentals=pairs * 2 * length * 640),
    )(queries, keys, values, grads, attended, logs, starts, table)


BR = 512
BC = 256
SLOTS = 5
SEMAPHORES = 10
SHORT = 3
FAR_SLOTS = 8
LEAD = 2


def back_kernel(
    bases,
    inner,
    cot_own,
    cotangent,
    gate,
    up,
    act_two,
    attended,
    queries,
    keys,
    values,
    logs,
    starts_ref,
    table_ref,
    act_one,
    hidden_state,
    own_inputs,
    params_ref,
    down_own,
    w_down,
    w_gate,
    w_out,
    w_qkv,
    out_ref,
    res_own,
    res_got,
    grad_own,
    grad_got,
    small_out,
    norm_sums,
    bias_sums,
    small_src,
    small_in,
    turn,
    turn_in,
    joint,
    branch,
    pair,
    att,
    att_grad,
    heads,
    head_logs,
    key_sums,
    value_sums,
    down_rows,
    gate_in,
    down_columns,
    wide_w,
    w_o,
    sent,
    kept,
    core_in,
    row_src,
    row_in,
    acc_rows,
    grad_rows,
    hid,
    own,
    result,
    part,
    x_src,
    x_dst,
    y_dst,
    acc,
    e_dst,
    low,
    m_dst,
    full,
    f_dst,
    deep,
    n_dst,
    key,
    k_dst,
    whole,
    load_sem,
    once_sem,
    piece_sem,
    gather_sem,
    small_sem,
    *sems,
):
    out_own, out_got = out_ref.at[0], out_ref.at[1]
    names = ("x", "y", "ei", "eo", "m", "g", "fi", "fo", "n", "k", "w")
    send = {k: sems[i] for i, k in enumerate(names)}
    recv = {k: sems[len(names) + i] for i, k in enumerate(names)}
    store_own, store_got = sems[2 * len(names)], sems[2 * len(names) + 1]

    length, width = branch.shape
    half, part_rows, block = width // 2, length // 2, length // 4
    hidden, units = pair.shape[1] // 2, att.shape[1]
    pairs = units // 128
    size = BR * BC // half
    segments = (hidden // size, half * 2 * hidden // (BR * BC), units // size, half * 3 * units // (BR * BC))
    total = sum(segments)
    firsts = [sum(segments[:i]) for i in range(4)]

    d, r, c = lax.axis_index("dp"), lax.axis_index("row"), lax.axis_index("col")
    y, z = lax.rem(d, 2), d // 2
    upper = d // 4
    mid = (z == 1) | (z == 2)
    outer = (z == 0) | (z == 3)
    x_peer, c_peer = {"row": 1 - r}, {"col": 1 - c}
    y_peer = {"dp": d + 1 - 2 * y}
    e_peer = {"dp": d + 2 - 4 * lax.rem(z, 2)}
    m_peer = {"dp": d + 2 - 4 * upper}

    def span(start, count):
        return pl.ds(pl.multiple_of(start, count), count)

    def local_copy(n, src, dst):
        return pltpu.make_async_copy(src, dst, load_sem.at[n])

    barrier = pltpu.get_barrier_semaphore()
    for peer in (x_peer, y_peer, e_peer, c_peer):
        pl.semaphore_signal(barrier, inc=1, device_id=peer, device_id_type=MESH)

    @pl.when(mid)
    def _():
        pl.semaphore_signal(barrier, inc=1, device_id=m_peer, device_id_type=MESH)

    own_block = span(c * part_rows + r * block, block)
    x_block = span(c * part_rows + (1 - r) * block, block)
    lo, hi = pl.ds(0, half), pl.ds(half, half)
    load_inner = local_copy(0, inner, joint.at[:, pl.ds(0, hidden)])
    near_rows, far_rows = span(c * part_rows, part_rows), span((1 - c) * part_rows, part_rows)
    load_cot = (
        local_copy(1, cot_own, branch.at[near_rows, lo]),
        local_copy(10 + block // 64, cotangent.at[near_rows, hi], branch.at[near_rows, hi]),
        local_copy(11 + block // 64, cotangent.at[far_rows], branch.at[far_rows]),
    )
    load_hid = local_copy(2, hidden_state, hid)
    load_own = (
        local_copy(3, cot_own.at[span(r * block, block)], own.at[:, lo]),
        local_copy(12 + block // 64, cotangent.at[own_block, hi], own.at[:, hi]),
    )
    load_att = local_copy(4, attended, att)
    load_wo = local_copy(5, w_out, w_o)
    load_inputs = local_copy(6, own_inputs, own)

    def down_rows_load(i):
        s = lax.rem(i, 2)
        at = span(i * 128, 128)
        return (
            pltpu.make_async_copy(
                down_own.at[span(r * hidden + i * 128, 128)], down_rows.at[s, :, lo], once_sem.at[s]
            ),
            pltpu.make_async_copy(w_down.at[at], down_rows.at[s, :, hi], once_sem.at[24 + s]),
            pltpu.make_async_copy(gate.at[:, at], gate_in.at[s, 0], once_sem.at[2 + s]),
            pltpu.make_async_copy(up.at[:, at], gate_in.at[s, 1], once_sem.at[4 + s]),
        )

    def order(i):
        return lax.rem(i, 2) * (half // BC) + i // 2

    class Either:
        def __init__(self, flag, first, second):
            self.flag, self.first, self.second = flag, first, second

        def start(self):
            pl.when(self.flag)(lambda: self.first().start())
            pl.when(jnp.logical_not(self.flag))(lambda: self.second().start())

        def wait(self):
            self.first().wait()

    def down_columns_load(i):
        s = lax.rem(i, 2)
        cols = span(i // 2 * BC, BC)

        def of(ref):
            return pltpu.make_async_copy(ref, down_columns.at[s], once_sem.at[6 + s])

        return (
            Either(
                s == 0,
                lambda: of(down_own.at[span(r * hidden, hidden), cols]),
                lambda: of(w_down.at[:, cols]),
            ),
        )

    def gate_load(i):
        s = lax.rem(i, 2)
        return (pltpu.make_async_copy(w_gate.at[:, span(order(i) * BC, BC)], wide_w.at[s], once_sem.at[8 + s]),)

    def qkv_load(i):
        s = lax.rem(i, 2)
        rows = span(order(i) * BC, BC)
        return tuple(
            pltpu.make_async_copy(
                w_qkv.at[k, rows], wide_w.at[s, k // 2, :, pl.ds(k % 2 * units, units)], once_sem.at[10 + 2 * k + s]
            )
            for k in range(3)
        )

    def heads_load(p):
        s = lax.rem(p, 2)
        lanes = span(p * 128, 128)
        return tuple(
            pltpu.make_async_copy(ref.at[:, lanes], heads.at[s, k], once_sem.at[16 + 2 * k + s])
            for k, ref in enumerate((queries, keys, values))
        ) + (pltpu.make_async_copy(logs.at[p], head_logs.at[s], once_sem.at[22 + s]),)

    def turn_load(source, i, side):
        return local_copy(7 + side, source.at[:, span(side * half + i * BR, BR)], turn_in.at[side])

    def start(copies):
        for copy in copies:
            copy.start()

    def wait(copies):
        for copy in copies:
            copy.wait()

    start((load_inner, *load_cot, load_hid, *load_own, load_att, load_wo))
    start(down_rows_load(0))
    start(down_columns_load(0))
    start((turn_load(act_two, 0, 0), turn_load(act_two, 0, 1)))

    @pl.when(mid)
    def _():
        pl.semaphore_wait(barrier, 5)

    @pl.when(outer)
    def _():
        pl.semaphore_wait(barrier, 4)

    rows = BR // 2

    def halves(index):
        return span(index * rows, rows)

    def slot(u):
        return lax.rem(u, SLOTS)

    def short(u):
        return lax.rem(u, SHORT)

    def far_slot(u):
        return lax.rem(u, FAR_SLOTS)

    def copy(name, u, src, dst, peer):
        s = lax.rem(u, SEMAPHORES)
        return pltpu.make_async_remote_copy(
            src_ref=src,
            dst_ref=dst,
            send_sem=send[name].at[s],
            recv_sem=recv[name].at[s],
            device_id=peer,
            device_id_type=MESH,
        )

    def spot(u):
        place = u
        for first, base in zip(firsts, bases):
            place = jnp.where(u >= first, u + (base - first), place)
        return place

    def out_half(ref, u, index):
        return ref.at[spot(u), halves(index)]

    def x_copy(u):
        return copy("x", u, x_src.at[short(u)], x_dst.at[far_slot(u)], x_peer)

    def y_copy(u):
        return copy("y", u, part.at[short(u), halves(1 - y)], y_dst.at[slot(u)], y_peer)

    def e_in(u):
        return copy("ei", u, acc.at[short(u)], e_dst.at[slot(u)], e_peer)

    def e_out(u):
        return copy("eo", u, full.at[short(u)], e_dst.at[slot(u)], e_peer)

    def m_copy(u):
        return copy("m", u, low.at[short(u)], m_dst.at[slot(u)], m_peer)

    def g_mid(u):
        return copy("g", u, full.at[short(u)], out_half(out_own, u, y), y_peer)

    def g_out(u):
        return copy("g", u, e_dst.at[slot(u)], out_half(out_own, u, y), y_peer)

    def f_in(u):
        return copy("fi", u, x_dst.at[far_slot(u)], f_dst.at[slot(u)], e_peer)

    def f_out(u):
        return copy("fo", u, whole.at[slot(u)], out_got.at[spot(u)], e_peer)

    def n_copy(u):
        return copy("n", u, deep.at[short(u), halves(1 - upper)], n_dst.at[slot(u)], m_peer)

    def k_copy(u):
        return copy("k", u, key.at[short(u)], k_dst.at[slot(u)], y_peer)

    def w_copy(u):
        place = whole.at[slot(u), halves(upper)]
        return copy("w", u, place, place, m_peer)

    def keep_own(u, src):
        return pltpu.make_async_copy(src, out_half(out_own, u, y), store_own.at[slot(u)])

    def keep_got(u):
        return pltpu.make_async_copy(whole.at[slot(u)], out_got.at[spot(u)], store_got.at[slot(u)])

    def stage(u, fn, role=None):
        ok = (u >= 0) & (u < total)
        if role is not None:
            ok = ok & role

        @pl.when(ok)
        def _():
            fn(u)

    def within(t, first, count, fn):
        @pl.when((t >= first) & (t < first + count))
        def _():
            fn(t - first)

    def unit_block(k, side, ref, s, lhs, rhs):
        left = lhs[:, span(k * size, size)].T
        for q in range(half // BC):
            right = rhs[:, side * half + q * BC : side * half + (q + 1) * BC]
            ref[s, q * size : (q + 1) * size] = jnp.dot(left, right, preferred_element_type=F32).astype(BF)

    def feature_block(k, side, ref, s, rhs, source, following):
        columns = rhs.shape[1] // BC

        for i in range(half // BR):

            @pl.when(k == i * columns)
            def _(i=i):
                turn_load(source, i, side).wait()
                turn[side] = turn_in[side].T
                if i + 1 < half // BR:
                    turn_load(source, i + 1, side).start()
                elif following is not None:
                    turn_load(following, 0, side).start()

        right = rhs[:, span(lax.rem(k, columns) * BC, BC)]
        ref[s] = jnp.dot(turn[side], right, preferred_element_type=F32).astype(BF)

    def produce(u, side, ref):
        s = short(u)
        within(u, firsts[0], segments[0], lambda k: unit_block(k, side, ref, s, joint, branch))
        within(u, firsts[1], segments[1], lambda k: feature_block(k, side, ref, s, pair, act_two, act_one))
        within(u, firsts[2], segments[2], lambda k: unit_block(k, side, ref, s, att, branch))
        within(u, firsts[3], segments[3], lambda k: feature_block(k, side, ref, s, joint, act_one, None))

    def produce_own(u):
        produce(u, 0, part)
        y_copy(u).start()

    def produce_far(u):
        @pl.when(u == 0)
        def _():
            wait((load_inner, *load_cot))

        produce(u, 1, x_src)
        x_copy(u).start()

    def t1_a(u):
        y_copy(u).wait_recv()
        acc[short(u)] = part[short(u), halves(y)] + y_dst[slot(u)]
        pl.when(outer)(lambda: e_in(u).start())

    def t1_b(u):
        e_in(u).wait_recv()
        low[short(u)] = acc[short(u)] + e_dst[slot(u)]
        m_copy(u).start()

    def t1_c(u):
        m_copy(u).wait_recv()
        full[short(u)] = low[short(u)] + m_dst[slot(u)]
        e_out(u).start()
        g_mid(u).start()
        keep_own(u, full.at[short(u)]).start()

    def t1_d(u):
        e_out(u).wait_recv()
        g_out(u).start()
        keep_own(u, e_dst.at[slot(u)]).start()

    def t2_a(u):
        x_copy(u).wait_recv()
        pl.when(outer)(lambda: f_in(u).start())

    def t2_b(u):
        f_in(u).wait_recv()
        deep[short(u)] = x_dst[far_slot(u)] + f_dst[slot(u)]
        n_copy(u).start()

    def t2_c(u):
        n_copy(u).wait_recv()
        key[short(u)] = deep[short(u), halves(upper)] + n_dst[slot(u)]
        k_copy(u).start()

    def t2_d(u):
        k_copy(u).wait_recv()
        whole[slot(u), halves(upper)] = key[short(u)] + k_dst[slot(u)]
        w_copy(u).start()

    def t2_e(u):
        w_copy(u).wait_recv()
        f_out(u).start()
        keep_got(u).start()

    pieces = width // BC
    own_part, far_part = c * part_rows, (1 - c) * part_rows

    def core_copy(n):
        s = lax.rem(n, 3)
        return pltpu.make_async_remote_copy(
            src_ref=sent.at[s],
            dst_ref=core_in.at[s],
            send_sem=piece_sem.at[s],
            recv_sem=piece_sem.at[3 + s],
            device_id=c_peer,
            device_id_type=MESH,
        )

    def row_copy(n):
        s = lax.rem(n, 4)
        return pltpu.make_async_remote_copy(
            src_ref=row_src.at[s],
            dst_ref=row_in.at[s],
            send_sem=piece_sem.at[6 + s],
            recv_sem=piece_sem.at[10 + s],
            device_id=x_peer,
            device_id_type=MESH,
        )

    def sum_piece(n, product):
        s = lax.rem(n, 3)
        sent[s] = product(span(far_part, part_rows)).astype(BF)
        core_copy(n).start()
        kept[s] = product(span(own_part, part_rows)).astype(BF)

    def sum_core(n, i):
        s, q = lax.rem(n, 3), lax.rem(n, 4)
        core_copy(n).wait_recv()
        core_copy(n).wait_send()
        far, near = span((1 - r) * block, block), span(r * block, block)
        row_src[q] = kept[s, far] + core_in[s, far]
        row_copy(n).start()
        acc_rows[:, span(order(i) * BC, BC)] = kept[s, near].astype(F32) + core_in[s, near].astype(F32)

    def sum_row(n, i):
        q = lax.rem(n, 4)
        row_copy(n).wait_recv()
        row_copy(n).wait_send()
        partner = lax.rem(order(i) + half // BC, pieces)
        cols = span(partner * BC, BC)
        acc_rows[:, cols] = acc_rows[:, cols] + row_in[q].astype(F32)

    def summed(t, first, base, product, load, wait_for=None):
        within(t, first + 3, pieces, lambda i: sum_row(base + i, i))
        within(t, first + 1, pieces, lambda i: sum_core(base + i, i))

        def task(i):
            if wait_for is not None:
                pl.when(i == 0)(lambda: wait(wait_for))
            pl.when(i + 1 < pieces)(lambda: start(load(i + 1)))
            wait(load(i))
            sum_piece(base + i, lambda at: product(lax.rem(i, 2), at))

        within(t, first, pieces, task)

    def feed_product(s, at):
        return jnp.dot(joint[at, :hidden], down_columns[s], preferred_element_type=F32)

    def act_two_product(s, at):
        return nt(pair[at, :hidden], wide_w[s, 0]) + nt(pair[at, hidden:], wide_w[s, 1])

    def act_one_product(s, at):
        out = nt(joint[at, :units], wide_w[s, 0, :, :units])
        out = out + nt(joint[at, units : 2 * units], wide_w[s, 0, :, units : 2 * units])
        return out + nt(joint[at, 2 * units :], wide_w[s, 1, :, :units])

    def gate_task(i):
        s = lax.rem(i, 2)

        @pl.when(i + 1 < hidden // 128)
        def _():
            start(down_rows_load(i + 1))

        wait(down_rows_load(i))

        def some(j, carry):
            at = span(j * 256, 256)
            grad = nt(branch[at], down_rows[s])
            g, u = gate_in[s, 0, at].astype(F32), gate_in[s, 1, at].astype(F32)
            rate = 1.0 / (1.0 + jnp.exp(-g))
            pair[at, span(i * 128, 128)] = (grad * u * (rate * (1.0 + g * (1.0 - rate)))).astype(BF)
            pair[at, span(hidden + i * 128, 128)] = (grad * (g * rate)).astype(BF)
            return carry

        lax.fori_loop(0, length // 256, some, 0)

    def result_copy():
        return pltpu.make_async_remote_copy(
            src_ref=result.at[:, hi],
            dst_ref=res_got,
            send_sem=gather_sem.at[0],
            recv_sem=gather_sem.at[1],
            device_id=x_peer,
            device_id_type=MESH,
        )

    store_result = local_copy(9, result.at[:, lo], res_own)

    def result_task(i):
        load_hid.wait()
        wait(load_own)
        result[...] = (hid[...] + acc_rows[...]).astype(BF)
        result_copy().start()
        store_result.start()

    chunk = 64
    chunks = block // chunk

    def norm_rows(values, at, grads, gain):
        mean = jnp.sum(values, axis=1, keepdims=True) / width
        spread_of = jnp.sum(values * values, axis=1, keepdims=True) / width - mean * mean
        inverse = lax.rsqrt(spread_of + EPSILON)
        normal = (values - mean) * inverse
        scaled = grads * gain
        terms = grads * normal
        first = jnp.sum(scaled, axis=1, keepdims=True) / width
        second = jnp.sum(terms * gain, axis=1, keepdims=True) / width
        return inverse * (scaled - first - normal * second), terms

    def gather_copies(i):
        at = span(c * part_rows + r * block + i * chunk, chunk)

        def one(n, src, dst, peer):
            return pltpu.make_async_remote_copy(
                src_ref=src,
                dst_ref=dst,
                send_sem=gather_sem.at[2 + 2 * (n * chunks + i)],
                recv_sem=gather_sem.at[3 + 2 * (n * chunks + i)],
                device_id=peer,
                device_id_type=MESH,
            )

        got = span(c * part_rows + (1 - r) * block + i * chunk, chunk)
        return (
            one(0, branch.at[at, lo], branch.at[at, hi], x_peer),
            one(1, branch.at[at, hi], branch.at[at, lo], x_peer),
            one(2, branch.at[at], branch.at[at], c_peer),
            one(3, branch.at[got], branch.at[got], c_peer),
        )

    def norm_two_task(i):
        at = span(i * chunk, chunk)
        grads = acc_rows[at]
        grad, terms = norm_rows(hid[at], at, grads, params_ref[2:3])
        norm_sums[2:3] = norm_sums[2:3] + jnp.sum(terms, axis=0, keepdims=True)
        norm_sums[3:4] = norm_sums[3:4] + jnp.sum(grads, axis=0, keepdims=True)
        grad = own[at].astype(F32) + grad
        grad_rows[at] = grad
        branch[span(c * part_rows + r * block + i * chunk, chunk)] = grad.astype(BF)
        start(gather_copies(i)[:3])

    def forward_task(i):
        copies = gather_copies(i)
        copies[0].wait_recv()
        copies[1].wait_recv()
        copies[3].start()

    def gathered_task(i):
        copies = gather_copies(i)
        copies[2].wait_recv()
        copies[3].wait_recv()
        for one in copies:
            one.wait_send()

    def att_grad_task(i):
        at = span(i * part_rows, part_rows)
        att_grad[at] = nt(branch[at], w_o[...]).astype(BF)

    def attention_task(i):
        p, second = i // 2, lax.rem(i, 2)
        s = lax.rem(p, 2)
        lanes0 = span(p * 128, 128)

        @pl.when(second == 0)
        def _():
            pl.when(p + 1 < pairs)(lambda: start(heads_load(p + 1)))
            wait(heads_load(p))
            key_sums[...] = jnp.zeros_like(key_sums)
            value_sums[...] = jnp.zeros_like(value_sums)

        def window(begin, low, end):
            bar = barred(starts_ref[begin:end], begin, low, end)
            q2, k2, v2 = heads[s, 0, begin:end], heads[s, 1, low:end], heads[s, 2, low:end]
            g2, a2 = att_grad[begin:end, lanes0], att[begin:end, lanes0]
            outs, dks, dvs = [], [], []
            for h in range(2):
                lanes = slice(h * HEAD, (h + 1) * HEAD)
                q, k, v, g = q2[:, lanes], k2[:, lanes], v2[:, lanes], g2[:, lanes]
                weights = jnp.exp(nt(q, k) + bar - head_logs[s, begin:end, h : h + 1])
                dvs.append(tn(weights.astype(BF), g))
                inside = jnp.sum(g.astype(F32) * a2[:, lanes].astype(F32), axis=1, keepdims=True)
                grads = (weights * (nt(g, v) - inside)).astype(BF)
                outs.append(jnp.dot(grads, k, preferred_element_type=F32))
                dks.append(tn(grads, q))
            table = (table_ref[0, begin:end], -table_ref[1, begin:end], -table_ref[2, begin:end])
            dq = turned(jnp.concatenate(outs, axis=1) * HEAD ** (-0.5), table).astype(BF)
            joint[begin:end, lanes0] = dq
            bias_sums[0:1, lanes0] = bias_sums[0:1, lanes0] + jnp.sum(dq.astype(F32), axis=0, keepdims=True)
            key_sums[low:end] += jnp.concatenate(dks, axis=1)
            value_sums[low:end] += jnp.concatenate(dvs, axis=1)

        spans = list(windows(length))
        middle = len(spans) // 2

        @pl.when(second == 0)
        def _():
            for one in spans[:middle]:
                window(*one)

        @pl.when(second == 1)
        def _():
            for one in spans[middle:]:
                window(*one)
            table = (table_ref[0], -table_ref[1], -table_ref[2])
            dk = turned(key_sums[...], table).astype(BF)
            dv = value_sums[...].astype(BF)
            for k, v in ((1, dk), (2, dv)):
                joint[:, span(k * units + p * 128, 128)] = v
                bias_sums[k : k + 1, lanes0] = jnp.sum(v.astype(F32), axis=0, keepdims=True)

    def grad_copies(i):
        at = span(i * chunk, chunk)
        n = 2 + 8 * chunks + 2 * i
        return (
            pltpu.make_async_remote_copy(
                src_ref=grad_rows.at[at, hi],
                dst_ref=grad_got.at[at],
                send_sem=gather_sem.at[n],
                recv_sem=gather_sem.at[n + 1],
                device_id=x_peer,
                device_id_type=MESH,
            ),
            local_copy(10 + i, grad_rows.at[at, lo], grad_own.at[at]),
        )

    def norm_one_task(i):
        pl.when(i == 0)(lambda: load_inputs.wait())
        at = span(i * chunk, chunk)
        grads = acc_rows[at]
        grad, terms = norm_rows(own[at].astype(F32), at, grads, params_ref[0:1])
        norm_sums[0:1] = norm_sums[0:1] + jnp.sum(terms, axis=0, keepdims=True)
        norm_sums[1:2] = norm_sums[1:2] + jnp.sum(grads, axis=0, keepdims=True)
        grad_rows[at] = grad_rows[at] + grad
        start(grad_copies(i))

    def small_copy(n, peer, cols=None):
        src, dst = small_src.at[n], small_in.at[n]
        if cols is not None:
            src, dst = src.at[:, cols], dst.at[:, cols]
        return pltpu.make_async_remote_copy(
            src_ref=src,
            dst_ref=dst,
            send_sem=small_sem.at[n],
            recv_sem=small_sem.at[8 + n],
            device_id=peer,
            device_id_type=MESH,
        )

    def small_hop(n, peer, step_peer):
        small_copy(n, peer).wait_recv()
        small_src[n + 1] = small_src[n] + small_in[n]
        small_copy(n + 1, step_peer).start()

    first_cols = pl.ds(0, half + units)

    def small_task(i):
        @pl.when(i == 0)
        def _():
            small_src[0, :, :half] = norm_sums[:, half:]
            small_src[0, :, half : half + units] = bias_sums[...]
            small_copy(0, x_peer, first_cols).start()

        @pl.when(i == 1)
        def _():
            small_copy(0, x_peer, first_cols).wait_recv()
            small_src[1, :, :half] = norm_sums[:, :half] + small_in[0, :, :half]
            small_copy(1, c_peer, lo).start()

        @pl.when(i == 2)
        def _():
            small_copy(1, c_peer, lo).wait_recv()
            small_src[2, :, :half] = small_src[1, :, :half] + small_in[1, :, :half]
            small_src[2, :, half : half + units] = bias_sums[...]
            small_src[2, :, half + units :] = small_in[0, :, half : half + units]
            small_copy(2, y_peer).start()

        @pl.when(i == 3)
        def _():
            small_hop(2, y_peer, e_peer)

        @pl.when(i == 4)
        def _():
            small_copy(3, e_peer).wait_recv()
            small_src[4] = small_src[3] + small_in[3]
            pl.when(mid)(lambda: small_copy(4, m_peer).start())

        @pl.when((i == 5) & mid)
        def _():
            small_hop(4, m_peer, e_peer)

        @pl.when(i == 6)
        def _():
            @pl.when(mid)
            def _():
                small_out[...] = small_src[5]
                small_copy(4, m_peer).wait_send()
                small_copy(5, e_peer).wait_send()

            @pl.when(outer)
            def _():
                small_copy(5, e_peer).wait_recv()
                small_out[...] = small_in[5]

            for n, cols in ((0, first_cols), (1, lo), (2, None), (3, None)):
                small_copy(n, x_peer, cols).wait_send()

    norm_sums[...] = jnp.zeros_like(norm_sums)
    bias_sums[...] = jnp.zeros_like(bias_sums)
    gates = hidden // 128
    at_two = max(gates, pieces + 3)
    at_norm = at_two + pieces + 3
    at_att = at_norm + chunks // 2 + 3
    at_heads = at_att + 2
    at_one = at_heads + 2 * pairs
    at_last = at_one + pieces + 3

    def tasks(t):
        within(t, 0, gates, gate_task)
        summed(t, 0, 0, feed_product, down_columns_load)
        within(t, at_two, 1, result_task)
        pl.when(t == at_two - 1)(lambda: start(gate_load(0)))
        summed(t, at_two, pieces, act_two_product, gate_load)

        def two(task):
            def both(i):
                task(2 * i)
                task(2 * i + 1)

            return both

        within(t, at_norm + 3, chunks // 2, two(gathered_task))
        within(t, at_norm + 2, chunks // 2, two(forward_task))
        within(t, at_norm, chunks // 2, two(norm_two_task))

        @pl.when(t == at_att)
        def _():
            load_wo.wait()
            load_att.wait()
            load_inputs.start()
            start(heads_load(0))

        within(t, at_att, 2, att_grad_task)
        within(t, at_heads, 2 * pairs, attention_task)
        pl.when(t == at_one - 1)(lambda: start(qkv_load(0)))
        summed(t, at_one, 2 * pieces, act_one_product, qkv_load)
        within(t, at_last, chunks // 2, two(norm_one_task))
        within(t, at_last + chunks // 2, 7, small_task)

    def body(step, carry):
        t = step - LEAD

        def free_out(u):
            e_out(u).wait_send()
            g_mid(u).wait_send()
            keep_own(u, full.at[short(u)]).wait()

        def free_far(u):
            g_out(u).wait_send()
            keep_own(u, e_dst.at[slot(u)]).wait()

        def free_got(u):
            f_out(u).wait_send()
            keep_got(u).wait()

        stage(step - 2, lambda u: x_copy(u).wait_send())
        stage(step - 2, lambda u: y_copy(u).wait_send())
        stage(step - 3, lambda u: e_in(u).wait_send(), outer)
        stage(step - 4, lambda u: m_copy(u).wait_send(), mid)
        stage(step - 5, free_out, mid)
        stage(step - 5, free_far, outer)
        stage(step - 5, lambda u: g_mid(u).wait_recv(), mid)
        stage(step - 6, lambda u: g_out(u).wait_recv(), outer)
        stage(t - 3, lambda u: f_in(u).wait_send(), outer)
        stage(t - 4, lambda u: n_copy(u).wait_send(), mid)
        stage(t - 5, lambda u: k_copy(u).wait_send(), mid)
        stage(t - 6, lambda u: w_copy(u).wait_send(), mid)
        stage(t - 7, free_got, mid)
        stage(t - 6, lambda u: f_out(u).wait_recv(), outer)
        stage(t - 4, t2_e, mid)
        stage(t - 3, t2_d, mid)
        stage(t - 2, t2_c, mid)
        stage(t - 1, t2_b, mid)
        stage(t, t2_a)
        stage(step - 4, t1_d, outer)
        stage(step - 3, t1_c, mid)
        stage(step - 2, t1_b, mid)
        stage(step - 1, t1_a)
        stage(step, produce_far)
        stage(step, produce_own)
        tasks(step)
        return carry

    lax.fori_loop(0, max(total + 7 + LEAD, at_last + chunks // 2 + 7), body, 0)
    result_copy().wait()
    store_result.wait()
    for i in range(chunks):
        wait(grad_copies(i))


def back(
    inner,
    cot_own,
    cotangent,
    gate,
    up,
    act_two,
    attended,
    queries,
    keys,
    values,
    logs,
    starts,
    table,
    act_one,
    hidden_state,
    own_inputs,
    params,
    down_own,
    w_down,
    w_gate,
    w_out,
    w_qkv,
):
    length, width = cotangent.shape
    hidden, units = inner.shape[1], attended.shape[1]
    half, part_rows, block = width // 2, length // 2, length // 4
    area, chunks = BR * BC, block // 64
    counts = [hidden * half // area, half * 2 * hidden // area, units * half // area, half * 3 * units // area]
    bases, end = [], 0
    for blocks in counts:
        bases.append(-(-end // blocks) * blocks)
        end = bases[-1] + blocks

    def bf(*shape):
        return jax.ShapeDtypeStruct(shape, BF)

    def f32(*shape):
        return jax.ShapeDtypeStruct(shape, F32)

    outs = [
        bf(2, end, BR, BC),
        bf(block, half),
        bf(block, half),
        f32(block, half),
        f32(block, half),
        f32(8, half + 2 * units),
    ]
    any_spec, vmem_spec = pl.BlockSpec(memory_space=pl.ANY), pl.BlockSpec(memory_space=pltpu.VMEM)
    wide, thin = bf(SLOTS, BR, BC), bf(SLOTS, BR // 2, BC)
    scratch = [
        f32(8, width),
        f32(8, units),
        f32(6, 8, half + 2 * units),
        f32(6, 8, half + 2 * units),
        bf(2, BR, length),
        bf(2, length, BR),
        bf(length, max(hidden, 3 * units)),
        bf(length, width),
        bf(length, 2 * hidden),
        bf(length, units),
        bf(length, units),
        bf(2, 3, length, 128),
        f32(2, length, 2),
        f32(length, 128),
        f32(length, 128),
        bf(2, 128, width),
        bf(2, 2, length, 128),
        bf(2, hidden, BC),
        bf(2, 2, BC, max(hidden, 2 * units)),
        bf(units, width),
        bf(3, part_rows, BC),
        bf(3, part_rows, BC),
        bf(3, part_rows, BC),
        bf(4, block, BC),
        bf(4, block, BC),
        f32(block, width),
        f32(block, width),
        f32(block, width),
        bf(block, width),
        bf(block, width),
        bf(SHORT, BR, BC),
        bf(SHORT, BR, BC),
        bf(FAR_SLOTS, BR, BC),
        thin,
        bf(SHORT, BR // 2, BC),
        thin,
        bf(SHORT, BR // 2, BC),
        thin,
        bf(SHORT, BR // 2, BC),
        wide,
        bf(SHORT, BR, BC),
        thin,
        bf(SHORT, BR // 2, BC),
        thin,
        wide,
    ]
    dma = pltpu.SemaphoreType.DMA
    flops = 2 * length * width * (8 * units + 6 * hidden) + 2 * length * 640 * 5 * units
    outs = pl.pallas_call(
        functools.partial(back_kernel, bases),
        out_shape=outs,
        in_specs=[any_spec] * 11 + [vmem_spec] * 2 + [any_spec] * 3 + [vmem_spec] + [any_spec] * 5,
        out_specs=[any_spec] * 5 + [vmem_spec],
        scratch_shapes=[pltpu.VMEM(v.shape, v.dtype) for v in scratch]
        + [dma((13 + chunks,)), dma((26,)), dma((14,)), dma((2 + 10 * chunks,)), dma((16,))]
        + [dma((SEMAPHORES,))] * 22
        + [dma((SLOTS,))] * 2,
        compiler_params=pltpu.CompilerParams(
            collective_id=1, has_side_effects=True, vmem_limit_bytes=63 * 2**20
        ),
        cost_estimate=pl.CostEstimate(flops=flops, bytes_accessed=200 * 2**20, transcendentals=length * 8192),
    )(
        inner,
        cot_own,
        cotangent,
        gate,
        up,
        act_two,
        attended,
        queries,
        keys,
        values,
        logs,
        starts,
        table,
        act_one,
        hidden_state,
        own_inputs,
        params,
        down_own,
        w_down,
        w_gate,
        w_out,
        w_qkv,
    )
    return outs[0], bases, *outs[1:]


def spread_kernel(
    bases, sums, res_own, res_got, grad_own, grad_got, gate_up_out, qkv_out, out_out, down_out, res_out, grad_out, *scratch
):
    buffers, (load_sem, store_sem, row_sem) = scratch[:-3], scratch[-3:]
    r = lax.axis_index("row")
    half, hidden = gate_up_out.shape[0], gate_up_out.shape[2] // 2
    units = out_out.shape[0] // 2
    size = BR * BC // half
    rows = BR // 2

    def span(start, count):
        return pl.ds(pl.multiple_of(start, count), count)

    def widen_pair(src, dst, s):
        def some(i, carry):
            at = span(i * 64, 64)
            for j in range(src.shape[1]):
                for first in range(0, BC, 128):
                    unit = j * BC + first
                    dst[s, at, unit // hidden, unit % hidden : unit % hidden + 128] = src[
                        s, j, at, first : first + 128
                    ].astype(F32)
            return carry

        lax.fori_loop(0, rows // 64, some, 0)

    def widen_kinds(src, dst, s):
        per = units // BC
        for j in range(src.shape[1]):
            dst[s, j // per, :, j % per * BC : (j % per + 1) * BC] = src[s, j].astype(F32)

    def widen_rows(src, dst, s):
        def some(k, carry):
            dst[s, span(k * size, size)] = src[s, k].astype(F32)
            return carry

        lax.fori_loop(0, src.shape[1], some, 0)

    block = res_own.shape[0]
    moves, places = [], []
    for n, (src, dst) in enumerate(((res_own, res_out), (grad_own, grad_out), (res_got, res_out), (grad_got, grad_out))):
        held = buffers[8 + n % 2].at[n // 2]
        side = r if n < 2 else 1 - r
        moves.append(pltpu.make_async_copy(src, held, row_sem.at[n]))
        places.append(pltpu.make_async_copy(held, dst.at[span(side * block, block)], row_sem.at[4 + n]))
    tasks = []
    for w in range(2):
        side = r if w == 0 else 1 - r
        for i in range(half // rows):
            block, at = i * rows // BR, pl.ds(i * rows % BR, rows)
            per = 2 * hidden // BC
            tasks.append(
                (
                    0,
                    widen_pair,
                    sums.at[w, pl.ds(bases[1] + block * per, per), at],
                    gate_up_out.at[pl.ds(i * rows, rows), :, span(side * hidden, hidden)],
                )
            )
    for w in range(2):
        side = r if w == 0 else 1 - r
        for q in range(half // BC):
            at = pl.ds(q * size, size)
            for n, base, out, count in ((1, bases[0], down_out, hidden), (3, bases[2], out_out, units)):
                tasks.append(
                    (
                        n,
                        widen_rows,
                        sums.at[w, pl.ds(base, count // size), at],
                        out.at[span(side * count, count), pl.ds(q * BC, BC)],
                    )
                )
        for i in range(half // rows):
            block, at = i * rows // BR, pl.ds(i * rows % BR, rows)
            per = 3 * units // BC
            tasks.append(
                (
                    2,
                    widen_kinds,
                    sums.at[w, pl.ds(bases[3] + block * per, per), at],
                    qkv_out.at[:, pl.ds(i * rows, rows), span(side * units, units)],
                )
            )

    uses, plan = [0] * 4, []
    for n, widen, src, dst in tasks:
        s = uses[n] % 4
        uses[n] += 1
        held, wide = buffers[2 * n], buffers[2 * n + 1]
        load = pltpu.make_async_copy(src, held.at[s], load_sem.at[4 * n + s])
        store = pltpu.make_async_copy(wide.at[s], dst, store_sem.at[4 * n + s])
        plan.append((n, s, widen, held, wide, load, store))
    busy = {}
    ahead = 4
    for step in plan[:ahead]:
        step[5].start()
    for copy in moves:
        copy.start()
    for i, (n, s, widen, held, wide, load, store) in enumerate(plan):
        if i == ahead:
            for copy, placing in zip(moves, places):
                copy.wait()
                placing.start()
        load.wait()
        if (n, s) in busy:
            busy.pop((n, s)).wait()
        widen(held, wide, s)
        store.start()
        busy[n, s] = store
        if i + ahead < len(plan):
            plan[i + ahead][5].start()
    for copy in list(busy.values()) + places:
        copy.wait()


def spread(sums, bases, rows_of, half, units, hidden):
    block = rows_of[0].shape[0]
    size, rows = BR * BC // half, BR // 2
    shapes = [(half, 2, 2 * hidden), (3, half, 2 * units), (2 * units, half), (2 * hidden, half)]
    pair, kinds = 2 * hidden // BC, 3 * units // BC
    buffers = [
        ((4, pair, rows, BC), BF),
        ((4, rows, 2, hidden), F32),
        ((4, hidden // size, size, BC), BF),
        ((4, hidden, BC), F32),
        ((4, kinds, rows, BC), BF),
        ((4, 3, rows, units), F32),
        ((4, units // size, size, BC), BF),
        ((4, units, BC), F32),
        ((2, block, half), BF),
        ((2, block, half), F32),
    ]
    any_spec = pl.BlockSpec(memory_space=pl.ANY)
    return pl.pallas_call(
        functools.partial(spread_kernel, bases),
        out_shape=[jax.ShapeDtypeStruct(v, F32) for v in shapes]
        + [jax.ShapeDtypeStruct((2 * block, half), BF), jax.ShapeDtypeStruct((2 * block, half), F32)],
        in_specs=[any_spec] * 5,
        out_specs=[any_spec] * 6,
        scratch_shapes=[pltpu.VMEM(*v) for v in buffers] + [pltpu.SemaphoreType.DMA((16,))] * 2
        + [pltpu.SemaphoreType.DMA((8,))],
        compiler_params=pltpu.CompilerParams(vmem_limit_bytes=56 * 2**20),
    )(sums, *rows_of)


def front_kernel(
    tokens,
    starts_ref,
    table_ref,
    params_in,
    bias_ref,
    qkv_w,
    out_w,
    gate_w,
    down_w,
    cotangent,
    act_one,
    q_out,
    k_out,
    v_out,
    att_out,
    log_out,
    hid_out,
    act_two,
    gate_out,
    up_out,
    inner_out,
    wq_out,
    wo_out,
    wg_out,
    wd_out,
    cot_out,
    own_out,
    params_ref,
    tok,
    act,
    wq,
    wo,
    wg,
    gate_far,
    gate_own,
    qs,
    ks,
    vs,
    att,
    logs,
    core_in,
    row_src,
    row_in,
    own_in,
    hid,
    tile,
    send_sem,
    recv_sem,
    load_sem,
    store_sem,
):
    r, c, d = lax.axis_index("row"), lax.axis_index("col"), lax.axis_index("dp")
    y, zp = lax.rem(d, 2), lax.rem(d // 2, 2)
    length, width = tok.shape
    half = width // 2
    part, block = length // 2, length // 4
    units, hidden = qs.shape[1], wg.shape[2]
    sub = zp * 2 + y
    dy, dz = 1 - 2 * y, 2 - 4 * zp
    row_peer, col_peer = {"row": 1 - r}, {"col": 1 - c}
    near = ({"dp": d + dy}, {"dp": d + dz}, {"dp": d + dy + dz})
    level = lax.rem(d // 2, 4)
    mid = (level == 1) | (level == 2)
    line = level * 2 + y
    next_peer, last_peer = {"dp": d + 2}, {"dp": d - 2}
    mid_peer = {"dp": d + 2 - 4 * (level // 2)}

    barrier = pltpu.get_barrier_semaphore()
    for peer in (row_peer, col_peer) + near:
        pl.semaphore_signal(barrier, inc=1, device_id=peer, device_id_type=MESH)

    @pl.when(mid)
    def _():
        pl.semaphore_signal(barrier, inc=1, device_id=mid_peer, device_id_type=MESH)

    stores = []

    def span(start, size):
        return pl.ds(pl.multiple_of(start, size), size)

    def load(n, src, dst):
        copy = pltpu.make_async_copy(src, dst, load_sem.at[n])
        copy.start()
        return copy

    def store(src, dst):
        copy = pltpu.make_async_copy(src, dst, store_sem.at[len(stores)])
        copy.start()
        stores.append(copy)
        return copy

    def remote(n, src, dst, peer):
        return pltpu.make_async_remote_copy(
            src_ref=src,
            dst_ref=dst,
            send_sem=send_sem.at[n],
            recv_sem=recv_sem.at[n],
            device_id=peer,
            device_id_type=MESH,
        )

    mine, theirs = span(r * units, units), span((1 - r) * units, units)
    own_rows, far_rows = span(c * part, part), span((1 - c) * part, part)
    lo, hi = pl.ds(0, half), pl.ds(half, half)
    quarter, eighth = half // 4, half // 8
    down_quarter = hidden // 4

    load_tok = load(0, tokens, tok.at[own_rows, lo])
    load_q = load(1, qkv_w.at[:, :, mine], wq.at[:, lo])
    load_o = load(2, out_w.at[mine], wo.at[:, lo])
    gate_cols = span(r * hidden, hidden)

    def load_gate(i):
        return load(3 + i % 2, gate_w.at[pl.ds(i * eighth, eighth), :, gate_cols], gate_own.at[i % 2])

    gates = [load_gate(0), load_gate(1)]

    rows_sub = span(sub * quarter, quarter)
    rows_far = span(half + sub * quarter, quarter)
    q_x = remote(0, qkv_w.at[:, rows_sub, theirs], wq.at[:, rows_far], row_peer)
    q_n = [remote(1 + k, wq.at[:, rows_far], wq.at[:, rows_far], p) for k, p in enumerate(near)]
    tok_x = remote(4, tokens, tok.at[own_rows, hi], row_peer)
    tok_c = remote(5, tokens, tok.at[own_rows, lo], col_peer)
    tok_f = remote(6, tok.at[own_rows, hi], tok.at[own_rows, hi], col_peer)
    out_rows = units // 4
    out_sub = span(sub * out_rows, out_rows)
    o_x = remote(
        7, out_w.at[span((1 - r) * units + sub * out_rows, out_rows)], wo.at[out_sub, hi], row_peer
    )
    o_n = [remote(8 + k, wo.at[out_sub, hi], wo.at[out_sub, hi], p) for k, p in enumerate(near)]
    rows_line = span(line * eighth, eighth)
    g_x = remote(
        11, gate_w.at[rows_line, :, span((1 - r) * hidden, hidden)], gate_far.at[line], row_peer
    )

    def gate_copy(n, at, peer):
        place = gate_far.at[lax.rem(at + 4, 4) * 2 + y]
        return remote(29 + n, place, place, peer)

    def upward(h):
        return gate_copy(h, level - h, next_peer)

    def downward(h):
        return gate_copy(3 + h, level + h, last_peer)

    def across(n, at):
        return gate_copy(6 + n, at, near[0])

    def gate_hop(h):
        if h == 0:
            g_x.wait_recv()
            pl.when(level < 3)(lambda: upward(0).start())
            pl.when(level > 0)(lambda: downward(0).start())
            across(0, level).start()
            return

        @pl.when(level >= h)
        def _():
            upward(h - 1).wait_recv()
            if h < 3:
                pl.when(level < 3)(lambda: upward(h).start())
            across(h, level - h).start()

        @pl.when(level + h <= 3)
        def _():
            downward(h - 1).wait_recv()
            if h < 3:
                pl.when(level > 0)(lambda: downward(h).start())
            across(3 + h, level + h).start()

    def gates_across(act):
        act(across(0, level))
        for h in range(1, 4):
            pl.when(level >= h)(lambda h=h: act(across(h, level - h)))
            pl.when(level + h <= 3)(lambda h=h: act(across(3 + h, level + h)))

    def gates_sent():
        gates_across(lambda copy: copy.wait_send())
        for h in range(3):
            pl.when((level < 3) & (level >= h))(lambda h=h: upward(h).wait_send())
            pl.when((level > 0) & (level + h <= 3))(lambda h=h: downward(h).wait_send())

    def part_level(at, side):
        block_of = at * 2 + side
        part_gate(gate_far.at[block_of], span(half + block_of * eighth, eighth))

    down_sub = span(sub * down_quarter, down_quarter)
    d_x = remote(
        15,
        down_w.at[span((1 - r) * hidden + sub * down_quarter, down_quarter)],
        wd_out.at[down_sub],
        row_peer,
    )
    d_n = [
        remote(16 + k, wd_out.at[down_sub], wd_out.at[down_sub], p)
        for k, p in enumerate(near)
    ]
    c_x = remote(19, cotangent, cot_out.at[own_rows, hi], row_peer)
    c_c = remote(20, cotangent, cot_out.at[own_rows, lo], col_peer)
    c_f = remote(21, cot_out.at[own_rows, hi], cot_out.at[own_rows, hi], col_peer)
    rs_c = remote(22, act.at[far_rows], core_in, col_peer)
    rs_x = remote(23, row_src, row_in, row_peer)
    own_block = span(c * part + r * block, block)
    x_block = span(c * part + (1 - r) * block, block)
    ag_x = [
        remote(24, tok.at[own_block, lo], tok.at[own_block, hi], row_peer),
        remote(25, tok.at[own_block, hi], tok.at[own_block, lo], row_peer),
    ]
    ag_c = remote(26, tok.at[own_block], tok.at[own_block], col_peer)
    ag_f = remote(27, tok.at[x_block], tok.at[x_block], col_peer)

    p_x = remote(28, params_in, params_ref.at[:, hi], row_peer)

    def start(copies):
        for copy in copies:
            copy.start()

    def arrived(copies):
        for copy in copies:
            copy.wait_recv()

    def part_gate(ref, at):
        wg[0, at] = ref[:, 0, :]
        wg[1, at] = ref[:, 1, :]

    @pl.when(mid)
    def _():
        pl.semaphore_wait(barrier, 6)

    @pl.when(jnp.logical_not(mid))
    def _():
        pl.semaphore_wait(barrier, 5)

    p_x.start()
    params_ref[:, :half] = params_in[...]
    q_x.start()
    tok_c.start()
    c_c.start()
    for i in range(8):
        if i == 4:
            q_x.wait_recv()
            start(q_n)
            tok_x.start()
        gates[i].wait()
        part_gate(gate_own.at[i % 2], pl.ds(i * eighth, eighth))
        if i + 2 < 8:
            gates.append(load_gate(i + 2))
    tok_x.wait_recv()
    tok_f.start()
    o_x.start()
    g_x.start()

    load_tok.wait()
    p_x.wait_recv()
    tok_c.wait_recv()

    def normed(v, at):
        mean = jnp.sum(v, axis=1, keepdims=True) / width
        spread_of = jnp.sum(v * v, axis=1, keepdims=True) / width - mean * mean
        v = (v - mean) * lax.rsqrt(spread_of + EPSILON)
        return (v * params_ref[at : at + 1] + params_ref[at + 1 : at + 2]).astype(BF)

    norm_rows = 64

    def norm_one(base):
        def body(i, carry):
            at = span(base + i * norm_rows, norm_rows)
            act[at] = normed(tok[at].astype(F32), 0)
            return carry

        lax.fori_loop(0, part // norm_rows, body, 0)

    norm_one(c * part)
    own_in[...] = tok[own_block]
    tok_f.wait_recv()
    norm_one((1 - c) * part)
    store(act, act_one)
    store(own_in, own_out)

    load_q.wait()
    arrived(q_n)
    o_x.wait_recv()
    start(o_n)
    store(wq, wq_out)
    chunk = 256

    def project(i, carry):
        at = span(i * chunk, chunk)
        rows = act[at]
        for kind, ref in enumerate((qs, ks, vs)):
            out = jnp.dot(rows, wq[kind], preferred_element_type=F32) + bias_ref[kind : kind + 1]
            if kind == 2:
                ref[at] = out.astype(BF)
                continue
            table = (table_ref[0, at], table_ref[1, at], table_ref[2, at])
            for g in range(units // 128):
                lanes = slice(g * 128, (g + 1) * 128)
                v = turned(out[:, lanes], table).astype(BF)
                if kind == 0:
                    v = (v.astype(F32) * HEAD ** (-0.5)).astype(BF)
                ref[at, lanes] = v
        return carry

    lax.fori_loop(0, length // chunk, project, 0)
    gate_hop(0)
    d_x.start()
    for ref, out in ((qs, q_out), (ks, k_out), (vs, v_out)):
        store(ref, out)

    pairs = units // 128

    def attend(p, carry):
        @pl.when(p == pairs // 2)
        def _():
            gate_hop(1)
            c_x.start()


        lane0 = p * 128
        q2 = qs[:, span(lane0, 128)]
        k2 = ks[:, span(lane0, 128)]
        v2 = vs[:, span(lane0, 128)]
        for begin, low, end in windows(length):
            bar = barred(starts_ref[begin:end], begin, low, end)
            outs = []
            for h in range(2):
                lanes = slice(h * HEAD, (h + 1) * HEAD)
                scores = nt(q2[begin:end, lanes], k2[low:end, lanes]) + bar
                maxima = jnp.max(scores, axis=1, keepdims=True)
                shifted = jnp.exp(scores - maxima).astype(BF)
                wide = jnp.concatenate([v2[low:end, lanes], jnp.ones((end - low, HEAD), BF)], axis=1)
                got = jnp.dot(shifted, wide, preferred_element_type=F32)
                totals = got[:, HEAD : HEAD + 1]
                outs.append(got[:, :HEAD] / totals)
                logs[p, begin:end, h : h + 1] = maxima + jnp.log(totals)
            out = jnp.concatenate(outs, axis=1)
            att[begin:end, span(lane0, 128)] = out.astype(BF)
        return carry

    lax.fori_loop(0, pairs, attend, 0)
    gate_hop(2)
    store(att, att_out)
    store(logs, log_out)

    load_o.wait()
    arrived(o_n)
    store(wo, wo_out)
    stores[0].wait()
    tok_f.wait_send()

    def branch(base):
        def body(i, carry):
            at = span(base + i * chunk, chunk)
            act[at] = jnp.dot(att[at], wo[...], preferred_element_type=F32).astype(BF)
            return carry

        lax.fori_loop(0, part // chunk, body, 0)

    branch((1 - c) * part)
    rs_c.start()
    branch(c * part)
    rs_c.wait_recv()
    row_src[...] = act[x_block] + core_in[span((1 - r) * block, block)]
    rs_x.start()
    gate_hop(3)
    for at in range(4):
        part_level(at, y)
    rs_x.wait_recv()
    hid_rows = 64

    def norm_two(i, carry):
        at = span(i * hid_rows, hid_rows)
        kept = act[span(c * part + r * block + i * hid_rows, hid_rows)].astype(F32)
        kept = kept + core_in[span(r * block + i * hid_rows, hid_rows)].astype(F32)
        got = row_in[at].astype(F32)
        kept = kept + jnp.concatenate([got[:, half:], got[:, :half]], axis=1)
        kept = own_in[at].astype(F32) + kept
        hid[at] = kept
        tok[span(c * part + r * block + i * hid_rows, hid_rows)] = normed(kept, 2)
        return carry

    lax.fori_loop(0, block // hid_rows, norm_two, 0)
    start(ag_x)
    ag_c.start()
    store(hid, hid_out)
    d_x.wait_recv()
    start(d_n)
    c_x.wait_recv()
    c_f.start()
    gates_across(lambda copy: copy.wait_recv())
    for at in range(4):
        part_level(at, 1 - y)
    store(wg, wg_out)

    stores_of = []
    columns = [(at, min(512, hidden - at)) for at in range(0, hidden, 512)]
    for b in range(4):
        cc = c if b % 2 == 0 else 1 - c
        rr = r if b < 2 else 1 - r
        at = span(cc * part + rr * block, block)
        if b == 1:
            ag_c.wait_recv()
        elif b == 2:
            arrived(ag_x)
            ag_f.start()
        elif b == 3:
            ag_f.wait_recv()
        s = b % 2
        for copy in stores_of[3 * (b - 2) : 3 * (b - 1)] if b >= 2 else ():
            copy.wait()
        rows = tok[at]
        for first, size in columns:
            cols = slice(first, first + size)
            gate = jnp.dot(rows, wg[0, :, cols], preferred_element_type=F32)
            up = jnp.dot(rows, wg[1, :, cols], preferred_element_type=F32)
            tile[s, 0, :, cols] = gate.astype(BF)
            tile[s, 1, :, cols] = up.astype(BF)
            tile[s, 2, :, cols] = (gate / (1.0 + jnp.exp(-gate)) * up).astype(BF)
        for k, out in enumerate((gate_out, up_out, inner_out)):
            copy = pltpu.make_async_copy(tile.at[s, k], out.at[at], load_sem.at[7 + 3 * s + k])
            copy.start()
            stores_of.append(copy)
    store(tok, act_two)
    for copy in stores_of[6:] + stores[1:]:
        copy.wait()
    arrived(d_n)
    c_c.wait_recv()
    c_f.wait_recv()
    for copy in [p_x, q_x, tok_x, tok_c, o_x, g_x, d_x, c_x, c_c, c_f, rs_c, rs_x, ag_c, ag_f] + (
        q_n + o_n + d_n + ag_x
    ):
        copy.wait_send()
    gates_sent()


def front(tokens, starts, table, params, bias, qkv_w, out_w, gate_w, down_w, cotangent):
    part, half = tokens.shape
    length, width, block = 2 * part, 2 * half, part // 2
    units, hidden = out_w.shape[0] // 2, down_w.shape[0] // 2
    any_spec, vmem_spec = pl.BlockSpec(memory_space=pl.ANY), pl.BlockSpec(memory_space=pltpu.VMEM)
    pairs = units // 128

    def bf(*shape):
        return jax.ShapeDtypeStruct(shape, BF)

    def f32(*shape):
        return jax.ShapeDtypeStruct(shape, F32)

    outs = [
        bf(length, width),
        bf(length, units),
        bf(length, units),
        bf(length, units),
        bf(length, units),
        f32(pairs, length, 2),
        f32(block, width),
        bf(length, width),
        bf(length, hidden),
        bf(length, hidden),
        bf(length, hidden),
        bf(3, width, units),
        bf(units, width),
        bf(2, width, hidden),
        bf(hidden, half),
        bf(length, width),
        bf(block, width),
        f32(8, width),
    ]
    scratch = [
        bf(length, width),
        bf(length, width),
        bf(3, width, units),
        bf(units, width),
        bf(2, width, hidden),
        bf(8, half // 8, 2, hidden),
        bf(2, half // 8, 2, hidden),
        bf(length, units),
        bf(length, units),
        bf(length, units),
        bf(length, units),
        f32(pairs, length, 2),
        bf(part, width),
        bf(block, width),
        bf(block, width),
        bf(block, width),
        f32(block, width),
        bf(2, 3, block, hidden),
    ]
    dma = pltpu.SemaphoreType.DMA
    return pl.pallas_call(
        front_kernel,
        out_shape=outs,
        in_specs=[any_spec] + [vmem_spec] * 4 + [any_spec] * 5,
        out_specs=[any_spec] * (len(outs) - 1) + [vmem_spec],
        scratch_shapes=[pltpu.VMEM(v.shape, v.dtype) for v in scratch]
        + [dma((42,)), dma((42,)), dma((13,)), dma((16,))],
        compiler_params=pltpu.CompilerParams(
            collective_id=2, has_side_effects=True, vmem_limit_bytes=62 * 2**20
        ),
        cost_estimate=pl.CostEstimate(
            flops=2 * length * width * (4 * units + 2 * hidden),
            bytes_accessed=100 * 2**20,
            transcendentals=length * 2048,
        ),
    )(tokens, starts, table, params, bias, qkv_w, out_w, gate_w, down_w, cotangent)


def local(
    tokens,
    segments,
    ln1_gain,
    ln1_bias,
    qkv_weight,
    qkv_bias,
    out_weight,
    ln2_gain,
    ln2_bias,
    gate_up_weight,
    down_weight,
    cotangent,
):
    place = Place()
    r, c = place.r, place.c
    ids = segments[0]
    length = ids.shape[0]
    factor = HEAD ** (-0.5)
    half = qkv_weight.shape[0]
    units = qkv_weight.shape[2] // 2
    heads = units // HEAD
    hidden = gate_up_weight.shape[2] // 2

    none = jnp.zeros_like(ln1_gain)
    params = jnp.stack([ln1_gain, ln1_bias, ln2_gain, ln2_bias] + [none] * 4)
    firsts = first_places(ids)
    table = rotary_table(jnp.arange(length, dtype=jnp.int32) - firsts)
    starts = firsts[:, None]
    bias = piece(qkv_bias, r, 2, 1)
    (
        act_one,
        queries,
        keys,
        values,
        attended,
        logs,
        hidden_state,
        act_two,
        gate,
        up,
        inner,
        w_qkv,
        w_out,
        w_gate,
        w_down,
        cot_all,
        own_inputs,
        params,
    ) = front(
        tokens,
        starts,
        table,
        params,
        bias,
        qkv_weight.transpose(1, 0, 2),
        out_weight,
        gate_up_weight,
        down_weight,
        cotangent,
    )
    if place.count == 8:
        sums, bases, result, result_far, input_grad, input_far, small = back(
            inner,
            cotangent,
            cot_all,
            gate,
            up,
            act_two,
            attended,
            queries,
            keys,
            values,
            logs,
            starts,
            table,
            act_one,
            hidden_state,
            own_inputs,
            params,
            down_weight,
            w_down,
            w_gate,
            w_out,
            w_qkv,
        )
        norms = small[:4, :half]
        bias_grad = ordered(r, small[:3, half : half + units], small[:3, half + units :], 1)
        gate_up_grad, qkv_grad, out_grad, down_grad, result, input_grad = spread(
            sums, bases, (result, result_far, input_grad, input_far), half, units, hidden
        )
        qkv_grad = qkv_grad.transpose(1, 0, 2)
    else:
        block = c * 2 + r
        w_down = jnp.concatenate([piece(down_weight, r, 2), w_down], axis=1)
        cot_all = lax.dynamic_update_slice(cot_all, cotangent, (c * (length // 2), 0))
        own_inputs = own_inputs.astype(F32)
        _, normal_two, inverse_two = norm_forward(hidden_state, params[2], params[3])
        gate, up = gate.astype(F32), up.astype(F32)

        feed = reduce_blocks(dot(inner, w_down).astype(BF), place)
        result = (hidden_state + feed).astype(BF)
        result = ordered(r, result[:, :half], swap(result[:, half:], "row"))

        grad_inner = dot_t(cot_all, w_down)
        rate = 1.0 / (1.0 + jnp.exp(-gate))
        silu = gate * rate
        grad_gate = (grad_inner * up * (rate * (1.0 + gate * (1.0 - rate)))).astype(BF)
        grad_up = (grad_inner * silu).astype(BF)
        grad_two = jnp.stack([grad_gate, grad_up])
        grad_pair = jnp.concatenate([grad_gate, grad_up], axis=1)
        grad_act_two = reduce_blocks(
            jnp.einsum("ksf,kdf->sd", grad_two, w_gate, preferred_element_type=F32).astype(BF), place
        )
        grad_norm, ln2_gain_grad, ln2_bias_grad = norm_backward(
            grad_act_two, normal_two, inverse_two, params[2]
        )
        own_cot = piece(cot_all, block, 4).astype(F32)
        grad_hidden = own_cot + grad_norm
        grad_branch = gather_blocks(grad_hidden.astype(BF), place)
        grad_attended = dot_t(grad_branch, w_out).astype(BF)
        grad_joined = attention_backward(
            queries, keys, values, grad_attended, attended, logs, starts, table
        )
        grad_joined = jnp.concatenate(grad_joined, axis=1)
        bias_grad = jnp.sum(grad_joined, axis=0, dtype=F32)
        grad_kinds = grad_joined.reshape(length, 3, units)
        grad_act_one = reduce_blocks(
            jnp.einsum("sku,kdu->sd", grad_kinds, w_qkv, preferred_element_type=F32).astype(BF), place
        )
        _, normal_one, inverse_one = norm_forward(own_inputs, params[0], params[1])
        grad_norm, ln1_gain_grad, ln1_bias_grad = norm_backward(
            grad_act_one, normal_one, inverse_one, params[0]
        )
        input_grad = grad_hidden + grad_norm
        input_grad = ordered(r, input_grad[:, :half], swap(input_grad[:, half:], "row"))

        pairs = (
            ("D", act_two, grad_pair),
            ("D", act_one, grad_joined),
            ("U", attended, grad_branch),
            ("U", inner, cot_all),
        )
        sums = []
        for kind, left, right in pairs:
            both = t_dot(left, right).astype(BF)
            axis = 0 if kind == "D" else 1
            own, sent = jnp.split(both, 2, axis)
            sums.append([lax.psum(v, "dp").astype(F32) for v in (own, swap(sent, "row"))])
        gate_up_grad = ordered(r, *[v.reshape(half, 2, hidden) for v in sums[0]], 2)
        qkv_grad = ordered(r, *[v.reshape(half, 3, units) for v in sums[1]], 2)
        out_grad = ordered(r, *sums[2])
        down_grad = ordered(r, *sums[3])

        small = jnp.stack([ln1_gain_grad, ln1_bias_grad, ln2_gain_grad, ln2_bias_grad])
        small = small[:, :half] + swap(small[:, half:], "row")
        norms = lax.psum(small, ("dp", "col"))
        bias_grad = lax.psum(bias_grad.reshape(3, units), "dp")
        bias_grad = ordered(r, bias_grad, swap(bias_grad, "row"), 1)

    return (
        result,
        input_grad,
        norms[0],
        norms[1],
        qkv_grad,
        bias_grad,
        out_grad,
        norms[2],
        norms[3],
        gate_up_grad,
        down_grad,
    )


def solution(mesh):
    in_specs = (
        P(("dp", "col"), "row"),
        P("dp", None),
        P("row"),
        P("row"),
        P("row", None, "col"),
        P(None, "col"),
        P("col", "row"),
        P("row"),
        P("row"),
        P("row", None, "col"),
        P("col", "row"),
        P(("dp", "col"), "row"),
    )
    out_specs = (
        P(("dp", "col"), "row"),
        P(("dp", "col"), "row"),
        P("row"),
        P("row"),
        P("row", None, "col"),
        P(None, "col"),
        P("col", "row"),
        P("row"),
        P("row"),
        P("row", None, "col"),
        P("col", "row"),
    )
    return jax.shard_map(local, mesh=mesh, in_specs=in_specs, out_specs=out_specs, check_vma=False)
```

```python
import functools
import math

import jax
import jax.numpy as jnp
from jax import lax
from jax.experimental import pallas as pl
from jax.experimental.pallas import tpu as pltpu
from jax.sharding import PartitionSpec as P

HEAD = 64
ROT = 16
EPSILON = 1e-05
ROPE_BASE = 10000.0
NEGATIVE = -1e30
BF = jnp.bfloat16
F32 = jnp.float32
SWAP = [(0, 1), (1, 0)]
MESH = pl.DeviceIdType.MESH


def swap(v, axis):
    return lax.ppermute(v, axis, SWAP)


def ordered(flag, mine, other, axis=0):
    first = jnp.where(flag == 0, mine, other)
    second = jnp.where(flag == 0, other, mine)
    return jnp.concatenate([first, second], axis=axis)


def piece(v, index, count, axis=0):
    size = v.shape[axis] // count
    return lax.dynamic_slice_in_dim(v, index * size, size, axis)


def add(a, b):
    return (a.astype(F32) + b.astype(F32)).astype(BF)


def dot(a, b):
    return jnp.dot(a, b, preferred_element_type=F32)


def dot_t(a, b):
    return lax.dot_general(a, b, (((1,), (1,)), ((), ())), preferred_element_type=F32)


def t_dot(a, b):
    return lax.dot_general(a, b, (((0,), (0,)), ((), ())), preferred_element_type=F32)


class Place:
    def __init__(self):
        self.r = lax.axis_index("row")
        self.c = lax.axis_index("col")
        self.d = lax.axis_index("dp")
        self.count = lax.axis_size("dp")
        self.y = lax.rem(self.d, 2)
        self.zp = lax.rem(self.d // 2, 2)
        self.z = self.d // 2
        self.mid = (self.z == 1) | (self.z == 2)
        self.upper = (self.z >= 2).astype(jnp.int32)


def dp_perm(bit, count):
    return [(i, i ^ bit) for i in range(count)]


def cross(v):
    half = v.shape[-1] // 2
    return jnp.concatenate([v[..., half:], v[..., :half]], axis=-1)


def gather_blocks(block, place):
    other = cross(swap(block, "row"))
    pair = ordered(place.r, block, other)
    rest = swap(pair, "col")
    return ordered(place.c, pair, rest)


def reduce_blocks(partial, place):
    kept = piece(partial, place.c, 2)
    got = swap(piece(partial, 1 - place.c, 2), "col")
    held = add(kept, got)
    kept = piece(held, place.r, 2)
    got = cross(swap(piece(held, 1 - place.r, 2), "row"))
    return kept.astype(F32) + got.astype(F32)


def norm_forward(values, gain, shift):
    count = values.shape[-1]
    mean = jnp.sum(values, axis=-1, keepdims=True) / count
    spread = jnp.sum(values * values, axis=-1, keepdims=True) / count - mean * mean
    inverse = lax.rsqrt(spread + EPSILON)
    normal = (values - mean) * inverse
    return normal * gain + shift, normal, inverse


def norm_backward(grad, normal, inverse, gain):
    count = grad.shape[-1]
    scaled = grad * gain
    first = jnp.sum(scaled, axis=-1, keepdims=True) / count
    second = jnp.sum(scaled * normal, axis=-1, keepdims=True) / count
    grad_input = inverse * (scaled - first - normal * second)
    return grad_input, jnp.sum(grad * normal, axis=0), jnp.sum(grad, axis=0)


def first_places(segment_ids):
    return jnp.sum(
        segment_ids[None, :] < segment_ids[:, None], axis=1, keepdims=True, dtype=jnp.int32
    )


def rotary_table(places):
    lane = jnp.arange(128, dtype=jnp.int32) % HEAD
    half_rot = ROT // 2
    inverse = jnp.exp((lane % half_rot).astype(F32) * (-2.0 / ROT) * math.log(ROPE_BASE))
    angles = places.astype(F32) * inverse[None, :]
    cosines, sines = jnp.cos(angles), jnp.sin(angles)
    low, turns = (lane < half_rot)[None, :], (lane < ROT)[None, :]
    return (
        jnp.where(turns, cosines, 1.0),
        jnp.where(low, -sines, 0.0),
        jnp.where(turns & ~low, sines, 0.0),
    )


LONGEST = 512
QB = 256

def windows(length):
    for begin in range(0, length, QB):
        low = max(0, (begin - LONGEST + 1) // QB * QB)
        yield begin, low, begin + QB


def barred(starts, begin, low, end):
    shape = (end - begin, end - low)
    query = begin + lax.broadcasted_iota(jnp.int32, shape, 0)
    key = low + lax.broadcasted_iota(jnp.int32, shape, 1)
    return jnp.where((key <= query) & (key >= starts), 0.0, NEGATIVE)


def turned(v, table):
    width = v.shape[-1]
    return v * table[0] + pltpu.roll(v, width - 8, 1) * table[1] + pltpu.roll(v, 8, 1) * table[2]


def nt(a, b):
    return lax.dot_general(a, b, (((1,), (1,)), ((), ())), preferred_element_type=F32)


def tn(a, b):
    return lax.dot_general(a, b, (((0,), (0,)), ((), ())), preferred_element_type=F32)


def backward_kernel(q_ref, k_ref, v_ref, g_ref, att_ref, log_ref, starts_ref, table_ref, dq_ref, dk_ref, dv_ref, dk_acc, dv_acc):
    length = q_ref.shape[0]
    dk_acc[...] = jnp.zeros_like(dk_acc)
    dv_acc[...] = jnp.zeros_like(dv_acc)
    for begin, low, end in windows(length):
        bar = barred(starts_ref[begin:end], begin, low, end)
        outs, dks, dvs = [], [], []
        for h in range(2):
            lanes = slice(h * HEAD, (h + 1) * HEAD)
            q, k, v, g = q_ref[begin:end, lanes], k_ref[low:end, lanes], v_ref[low:end, lanes], g_ref[begin:end, lanes]
            weights = jnp.exp(nt(q, k) + bar - log_ref[0, begin:end, h : h + 1])
            dvs.append(tn(weights.astype(BF), g))
            inner = jnp.sum(g.astype(F32) * att_ref[begin:end, lanes].astype(F32), axis=1, keepdims=True)
            grads = (weights * (nt(g, v) - inner)).astype(BF)
            outs.append(jnp.dot(grads, k, preferred_element_type=F32))
            dks.append(tn(grads, q))
        table = (table_ref[0, begin:end], -table_ref[1, begin:end], -table_ref[2, begin:end])
        dq_ref[begin:end] = turned(jnp.concatenate(outs, axis=1) * HEAD ** (-0.5), table).astype(BF)
        dk_acc[low:end] += jnp.concatenate(dks, axis=1)
        dv_acc[low:end] += jnp.concatenate(dvs, axis=1)
    table = (table_ref[0], -table_ref[1], -table_ref[2])
    dk_ref[...] = turned(dk_acc[...], table).astype(BF)
    dv_ref[...] = dv_acc[...].astype(BF)


def attention_backward(queries, keys, values, grads, attended, logs, starts, table):
    length, units = queries.shape
    pairs = units // 128
    same = pl.BlockSpec((length, 128), lambda p: (0, p))
    half = jax.ShapeDtypeStruct((length, units), BF)
    return pl.pallas_call(
        backward_kernel,
        grid=(pairs,),
        in_specs=[same] * 5
        + [
            pl.BlockSpec((1, length, 2), lambda p: (p, 0, 0)),
            pl.BlockSpec((length, 1), lambda p: (0, 0)),
            pl.BlockSpec((3, length, 128), lambda p: (0, 0, 0)),
        ],
        out_specs=[same] * 3,
        out_shape=[half] * 3,
        scratch_shapes=[pltpu.VMEM((length, 128), F32)] * 2,
        compiler_params=pltpu.CompilerParams(vmem_limit_bytes=48 * 2**20),
        cost_estimate=pl.CostEstimate(flops=pairs * 2 * length * 640 * 640, bytes_accessed=8 * 2**20, transcendentals=pairs * 2 * length * 640),
    )(queries, keys, values, grads, attended, logs, starts, table)


BR = 512
BC = 256
SLOTS = 5
SEMAPHORES = 10
SHORT = 3
FAR_SLOTS = 8
LEAD = 2


def back_kernel(
    bases,
    inner,
    cot_own,
    cotangent,
    gate,
    up,
    act_two,
    attended,
    queries,
    keys,
    values,
    logs,
    starts_ref,
    one_ref,
    ahead_ref,
    behind_ref,
    act_one,
    hidden_state,
    own_inputs,
    params_ref,
    down_own,
    w_down,
    w_gate,
    w_out,
    w_qkv,
    out_ref,
    res_own,
    res_got,
    grad_own,
    grad_got,
    small_out,
    norm_sums,
    bias_sums,
    small_src,
    small_in,
    turn,
    turn_in,
    joint,
    branch,
    pair,
    att,
    att_grad,
    heads,
    head_logs,
    key_sums,
    value_sums,
    down_rows,
    gate_in,
    down_columns,
    wide_w,
    w_o,
    sent,
    kept,
    core_in,
    row_src,
    row_in,
    acc_rows,
    grad_rows,
    hid,
    own,
    result,
    part,
    x_src,
    x_dst,
    y_dst,
    acc,
    e_dst,
    low,
    m_dst,
    full,
    f_dst,
    deep,
    n_dst,
    key,
    k_dst,
    whole,
    load_sem,
    once_sem,
    piece_sem,
    gather_sem,
    small_sem,
    *sems,
):
    out_own, out_got = out_ref.at[0], out_ref.at[1]
    names = ("x", "y", "ei", "eo", "m", "g", "fi", "fo", "n", "k", "w")
    send = {k: sems[i] for i, k in enumerate(names)}
    recv = {k: sems[len(names) + i] for i, k in enumerate(names)}
    store_own, store_got = sems[2 * len(names)], sems[2 * len(names) + 1]

    length, width = branch.shape
    half, part_rows, block = width // 2, length // 2, length // 4
    hidden, units = pair.shape[1] // 2, att.shape[1]
    pairs = units // 128
    size = BR * BC // half
    segments = (hidden // size, half * 2 * hidden // (BR * BC), units // size, half * 3 * units // (BR * BC))
    total = sum(segments)
    firsts = [sum(segments[:i]) for i in range(4)]

    d, r, c = lax.axis_index("dp"), lax.axis_index("row"), lax.axis_index("col")
    y, z = lax.rem(d, 2), d // 2
    upper = d // 4
    mid = (z == 1) | (z == 2)
    outer = (z == 0) | (z == 3)
    x_peer, c_peer = {"row": 1 - r}, {"col": 1 - c}
    y_peer = {"dp": d + 1 - 2 * y}
    e_peer = {"dp": d + 2 - 4 * lax.rem(z, 2)}
    m_peer = {"dp": d + 2 - 4 * upper}

    def span(start, count):
        return pl.ds(pl.multiple_of(start, count), count)

    def local_copy(n, src, dst):
        return pltpu.make_async_copy(src, dst, load_sem.at[n])

    barrier = pltpu.get_barrier_semaphore()
    for peer in (x_peer, y_peer, e_peer, c_peer):
        pl.semaphore_signal(barrier, inc=1, device_id=peer, device_id_type=MESH)

    @pl.when(mid)
    def _():
        pl.semaphore_signal(barrier, inc=1, device_id=m_peer, device_id_type=MESH)

    own_block = span(c * part_rows + r * block, block)
    x_block = span(c * part_rows + (1 - r) * block, block)
    lo, hi = pl.ds(0, half), pl.ds(half, half)
    load_inner = local_copy(0, inner, joint.at[:, pl.ds(0, hidden)])
    near_rows, far_rows = span(c * part_rows, part_rows), span((1 - c) * part_rows, part_rows)
    load_cot = (
        local_copy(1, cot_own, branch.at[near_rows, lo]),
        local_copy(10 + block // 64, cotangent.at[near_rows, hi], branch.at[near_rows, hi]),
        local_copy(11 + block // 64, cotangent.at[far_rows], branch.at[far_rows]),
    )
    load_hid = local_copy(2, hidden_state, hid)
    load_own = (
        local_copy(3, cot_own.at[span(r * block, block)], own.at[:, lo]),
        local_copy(12 + block // 64, cotangent.at[own_block, hi], own.at[:, hi]),
    )
    load_att = local_copy(4, attended, att)
    load_wo = local_copy(5, w_out, w_o)
    load_inputs = local_copy(6, own_inputs, own)

    def down_rows_load(i):
        s = lax.rem(i, 2)
        at = span(i * 128, 128)
        return (
            pltpu.make_async_copy(
                down_own.at[span(r * hidden + i * 128, 128)], down_rows.at[s, :, lo], once_sem.at[s]
            ),
            pltpu.make_async_copy(w_down.at[at], down_rows.at[s, :, hi], once_sem.at[24 + s]),
            pltpu.make_async_copy(gate.at[:, at], gate_in.at[s, 0], once_sem.at[2 + s]),
            pltpu.make_async_copy(up.at[:, at], gate_in.at[s, 1], once_sem.at[4 + s]),
        )

    def order(i):
        return lax.rem(i, 2) * (half // BC) + i // 2

    class Either:
        def __init__(self, flag, first, second):
            self.flag, self.first, self.second = flag, first, second

        def start(self):
            pl.when(self.flag)(lambda: self.first().start())
            pl.when(jnp.logical_not(self.flag))(lambda: self.second().start())

        def wait(self):
            self.first().wait()

    def down_columns_load(i):
        s = lax.rem(i, 2)
        cols = span(i // 2 * BC, BC)

        def of(ref):
            return pltpu.make_async_copy(ref, down_columns.at[s], once_sem.at[6 + s])

        return (
            Either(
                s == 0,
                lambda: of(down_own.at[span(r * hidden, hidden), cols]),
                lambda: of(w_down.at[:, cols]),
            ),
        )

    def gate_load(i):
        s = lax.rem(i, 2)
        return (pltpu.make_async_copy(w_gate.at[:, span(order(i) * BC, BC)], wide_w.at[s], once_sem.at[8 + s]),)

    def qkv_load(i):
        s = lax.rem(i, 2)
        rows = span(order(i) * BC, BC)
        return tuple(
            pltpu.make_async_copy(
                w_qkv.at[k, rows], wide_w.at[s, k // 2, :, pl.ds(k % 2 * units, units)], once_sem.at[10 + 2 * k + s]
            )
            for k in range(3)
        )

    def heads_load(p):
        s = lax.rem(p, 2)
        lanes = span(p * 128, 128)
        return tuple(
            pltpu.make_async_copy(ref.at[:, lanes], heads.at[s, k], once_sem.at[16 + 2 * k + s])
            for k, ref in enumerate((queries, keys, values))
        ) + (pltpu.make_async_copy(logs.at[p], head_logs.at[s], once_sem.at[22 + s]),)

    def turn_load(source, i, side):
        return local_copy(7 + side, source.at[:, span(side * half + i * BR, BR)], turn_in.at[side])

    def start(copies):
        for copy in copies:
            copy.start()

    def wait(copies):
        for copy in copies:
            copy.wait()

    start((load_inner, *load_cot, load_hid, *load_own, load_att, load_wo))
    start(down_rows_load(0))
    start(down_columns_load(0))
    start((turn_load(act_two, 0, 0), turn_load(act_two, 0, 1)))

    @pl.when(mid)
    def _():
        pl.semaphore_wait(barrier, 5)

    @pl.when(outer)
    def _():
        pl.semaphore_wait(barrier, 4)

    rows = BR // 2

    def halves(index):
        return span(index * rows, rows)

    def slot(u):
        return lax.rem(u, SLOTS)

    def short(u):
        return lax.rem(u, SHORT)

    def far_slot(u):
        return lax.rem(u, FAR_SLOTS)

    def copy(name, u, src, dst, peer):
        s = lax.rem(u, SEMAPHORES)
        return pltpu.make_async_remote_copy(
            src_ref=src,
            dst_ref=dst,
            send_sem=send[name].at[s],
            recv_sem=recv[name].at[s],
            device_id=peer,
            device_id_type=MESH,
        )

    def spot(u):
        place = u
        for first, base in zip(firsts, bases):
            place = jnp.where(u >= first, u + (base - first), place)
        return place

    def out_half(ref, u, index):
        return ref.at[spot(u), halves(index)]

    def x_copy(u):
        return copy("x", u, x_src.at[short(u)], x_dst.at[far_slot(u)], x_peer)

    def y_copy(u):
        return copy("y", u, part.at[short(u), halves(1 - y)], y_dst.at[slot(u)], y_peer)

    def e_in(u):
        return copy("ei", u, acc.at[short(u)], e_dst.at[slot(u)], e_peer)

    def e_out(u):
        return copy("eo", u, full.at[short(u)], e_dst.at[slot(u)], e_peer)

    def m_copy(u):
        return copy("m", u, low.at[short(u)], m_dst.at[slot(u)], m_peer)

    def g_mid(u):
        return copy("g", u, full.at[short(u)], out_half(out_own, u, y), y_peer)

    def g_out(u):
        return copy("g", u, e_dst.at[slot(u)], out_half(out_own, u, y), y_peer)

    def f_in(u):
        return copy("fi", u, x_dst.at[far_slot(u)], f_dst.at[slot(u)], e_peer)

    def f_out(u):
        return copy("fo", u, whole.at[slot(u)], out_got.at[spot(u)], e_peer)

    def n_copy(u):
        return copy("n", u, deep.at[short(u), halves(1 - upper)], n_dst.at[slot(u)], m_peer)

    def k_copy(u):
        return copy("k", u, key.at[short(u)], k_dst.at[slot(u)], y_peer)

    def w_copy(u):
        place = whole.at[slot(u), halves(upper)]
        return copy("w", u, place, place, m_peer)

    def keep_own(u, src):
        return pltpu.make_async_copy(src, out_half(out_own, u, y), store_own.at[slot(u)])

    def keep_got(u):
        return pltpu.make_async_copy(whole.at[slot(u)], out_got.at[spot(u)], store_got.at[slot(u)])

    def stage(u, fn, role=None):
        ok = (u >= 0) & (u < total)
        if role is not None:
            ok = ok & role

        @pl.when(ok)
        def _():
            fn(u)

    def within(t, first, count, fn):
        @pl.when((t >= first) & (t < first + count))
        def _():
            fn(t - first)

    def unit_block(k, side, ref, s, lhs, rhs):
        left = lhs[:, span(k * size, size)].T
        for q in range(half // BC):
            right = rhs[:, side * half + q * BC : side * half + (q + 1) * BC]
            ref[s, q * size : (q + 1) * size] = jnp.dot(left, right, preferred_element_type=F32).astype(BF)

    def feature_block(k, side, ref, s, rhs, source, following):
        columns = rhs.shape[1] // BC

        for i in range(half // BR):

            @pl.when(k == i * columns)
            def _(i=i):
                turn_load(source, i, side).wait()
                turn[side] = turn_in[side].T
                if i + 1 < half // BR:
                    turn_load(source, i + 1, side).start()
                elif following is not None:
                    turn_load(following, 0, side).start()

        right = rhs[:, span(lax.rem(k, columns) * BC, BC)]
        ref[s] = jnp.dot(turn[side], right, preferred_element_type=F32).astype(BF)

    def produce(u, side, ref):
        s = short(u)
        within(u, firsts[0], segments[0], lambda k: unit_block(k, side, ref, s, joint, branch))
        within(u, firsts[1], segments[1], lambda k: feature_block(k, side, ref, s, pair, act_two, act_one))
        within(u, firsts[2], segments[2], lambda k: unit_block(k, side, ref, s, att, branch))
        within(u, firsts[3], segments[3], lambda k: feature_block(k, side, ref, s, joint, act_one, None))

    def produce_own(u):
        produce(u, 0, part)
        y_copy(u).start()

    def produce_far(u):
        @pl.when(u == 0)
        def _():
            wait((load_inner, *load_cot))

        produce(u, 1, x_src)
        x_copy(u).start()

    def t1_a(u):
        y_copy(u).wait_recv()
        acc[short(u)] = part[short(u), halves(y)] + y_dst[slot(u)]
        pl.when(outer)(lambda: e_in(u).start())

    def t1_b(u):
        e_in(u).wait_recv()
        low[short(u)] = acc[short(u)] + e_dst[slot(u)]
        m_copy(u).start()

    def t1_c(u):
        m_copy(u).wait_recv()
        full[short(u)] = low[short(u)] + m_dst[slot(u)]
        e_out(u).start()
        g_mid(u).start()
        keep_own(u, full.at[short(u)]).start()

    def t1_d(u):
        e_out(u).wait_recv()
        g_out(u).start()
        keep_own(u, e_dst.at[slot(u)]).start()

    def t2_a(u):
        x_copy(u).wait_recv()
        pl.when(outer)(lambda: f_in(u).start())

    def t2_b(u):
        f_in(u).wait_recv()
        deep[short(u)] = x_dst[far_slot(u)] + f_dst[slot(u)]
        n_copy(u).start()

    def t2_c(u):
        n_copy(u).wait_recv()
        key[short(u)] = deep[short(u), halves(upper)] + n_dst[slot(u)]
        k_copy(u).start()

    def t2_d(u):
        k_copy(u).wait_recv()
        whole[slot(u), halves(upper)] = key[short(u)] + k_dst[slot(u)]
        w_copy(u).start()

    def t2_e(u):
        w_copy(u).wait_recv()
        f_out(u).start()
        keep_got(u).start()

    pieces = width // BC
    own_part, far_part = c * part_rows, (1 - c) * part_rows

    def core_copy(n):
        s = lax.rem(n, 3)
        return pltpu.make_async_remote_copy(
            src_ref=sent.at[s],
            dst_ref=core_in.at[s],
            send_sem=piece_sem.at[s],
            recv_sem=piece_sem.at[3 + s],
            device_id=c_peer,
            device_id_type=MESH,
        )

    def row_copy(n):
        s = lax.rem(n, 4)
        return pltpu.make_async_remote_copy(
            src_ref=row_src.at[s],
            dst_ref=row_in.at[s],
            send_sem=piece_sem.at[6 + s],
            recv_sem=piece_sem.at[10 + s],
            device_id=x_peer,
            device_id_type=MESH,
        )

    def sum_piece(n, product):
        s = lax.rem(n, 3)
        sent[s] = product(span(far_part, part_rows)).astype(BF)
        core_copy(n).start()
        kept[s] = product(span(own_part, part_rows)).astype(BF)

    def sum_core(n, i):
        s, q = lax.rem(n, 3), lax.rem(n, 4)
        core_copy(n).wait_recv()
        core_copy(n).wait_send()
        far, near = span((1 - r) * block, block), span(r * block, block)
        row_src[q] = kept[s, far] + core_in[s, far]
        row_copy(n).start()
        acc_rows[:, span(order(i) * BC, BC)] = kept[s, near].astype(F32) + core_in[s, near].astype(F32)

    def sum_row(n, i):
        q = lax.rem(n, 4)
        row_copy(n).wait_recv()
        row_copy(n).wait_send()
        partner = lax.rem(order(i) + half // BC, pieces)
        cols = span(partner * BC, BC)
        acc_rows[:, cols] = acc_rows[:, cols] + row_in[q].astype(F32)

    def summed(t, first, base, product, load, wait_for=None):
        within(t, first + 3, pieces, lambda i: sum_row(base + i, i))
        within(t, first + 1, pieces, lambda i: sum_core(base + i, i))

        def task(i):
            if wait_for is not None:
                pl.when(i == 0)(lambda: wait(wait_for))
            pl.when(i + 1 < pieces)(lambda: start(load(i + 1)))
            wait(load(i))
            sum_piece(base + i, lambda at: product(lax.rem(i, 2), at))

        within(t, first, pieces, task)

    def feed_product(s, at):
        return jnp.dot(joint[at, :hidden], down_columns[s], preferred_element_type=F32)

    def act_two_product(s, at):
        return nt(pair[at, :hidden], wide_w[s, 0]) + nt(pair[at, hidden:], wide_w[s, 1])

    def act_one_product(s, at):
        out = nt(joint[at, :units], wide_w[s, 0, :, :units])
        out = out + nt(joint[at, units : 2 * units], wide_w[s, 0, :, units : 2 * units])
        return out + nt(joint[at, 2 * units :], wide_w[s, 1, :, :units])

    def gate_task(i):
        s = lax.rem(i, 2)

        @pl.when(i + 1 < hidden // 128)
        def _():
            start(down_rows_load(i + 1))

        wait(down_rows_load(i))

        def some(j, carry):
            at = span(j * 256, 256)
            grad = nt(branch[at], down_rows[s])
            g, u = gate_in[s, 0, at].astype(F32), gate_in[s, 1, at].astype(F32)
            rate = 1.0 / (1.0 + jnp.exp(-g))
            pair[at, span(i * 128, 128)] = (grad * u * (rate * (1.0 + g * (1.0 - rate)))).astype(BF)
            pair[at, span(hidden + i * 128, 128)] = (grad * (g * rate)).astype(BF)
            return carry

        lax.fori_loop(0, length // 256, some, 0)

    def result_copy():
        return pltpu.make_async_remote_copy(
            src_ref=result.at[:, hi],
            dst_ref=res_got,
            send_sem=gather_sem.at[0],
            recv_sem=gather_sem.at[1],
            device_id=x_peer,
            device_id_type=MESH,
        )

    store_result = local_copy(9, result.at[:, lo], res_own)

    def result_task(i):
        load_hid.wait()
        wait(load_own)
        result[...] = (hid[...] + acc_rows[...]).astype(BF)
        result_copy().start()
        store_result.start()

    chunk = 64
    chunks = block // chunk

    def norm_rows(values, at, grads, gain):
        mean = jnp.sum(values, axis=1, keepdims=True) / width
        spread_of = jnp.sum(values * values, axis=1, keepdims=True) / width - mean * mean
        inverse = lax.rsqrt(spread_of + EPSILON)
        normal = (values - mean) * inverse
        scaled = grads * gain
        terms = grads * normal
        first = jnp.sum(scaled, axis=1, keepdims=True) / width
        second = jnp.sum(terms * gain, axis=1, keepdims=True) / width
        return inverse * (scaled - first - normal * second), terms

    def gather_copies(i):
        at = span(c * part_rows + r * block + i * chunk, chunk)

        def one(n, src, dst, peer):
            return pltpu.make_async_remote_copy(
                src_ref=src,
                dst_ref=dst,
                send_sem=gather_sem.at[2 + 2 * (n * chunks + i)],
                recv_sem=gather_sem.at[3 + 2 * (n * chunks + i)],
                device_id=peer,
                device_id_type=MESH,
            )

        got = span(c * part_rows + (1 - r) * block + i * chunk, chunk)
        return (
            one(0, branch.at[at, lo], branch.at[at, hi], x_peer),
            one(1, branch.at[at, hi], branch.at[at, lo], x_peer),
            one(2, branch.at[at], branch.at[at], c_peer),
            one(3, branch.at[got], branch.at[got], c_peer),
        )

    def norm_two_task(i):
        at = span(i * chunk, chunk)
        grads = acc_rows[at]
        grad, terms = norm_rows(hid[at], at, grads, params_ref[2:3])
        norm_sums[2:3] = norm_sums[2:3] + jnp.sum(terms, axis=0, keepdims=True)
        norm_sums[3:4] = norm_sums[3:4] + jnp.sum(grads, axis=0, keepdims=True)
        grad = own[at].astype(F32) + grad
        grad_rows[at] = grad
        branch[span(c * part_rows + r * block + i * chunk, chunk)] = grad.astype(BF)
        start(gather_copies(i)[:3])

    def forward_task(i):
        copies = gather_copies(i)
        copies[0].wait_recv()
        copies[1].wait_recv()
        copies[3].start()

    def gathered_task(i):
        copies = gather_copies(i)
        copies[2].wait_recv()
        copies[3].wait_recv()
        for one in copies:
            one.wait_send()

    def att_grad_task(i):
        at = span(i * part_rows, part_rows)
        att_grad[at] = nt(branch[at], w_o[...]).astype(BF)

    def attention_task(i):
        p, second = i // 2, lax.rem(i, 2)
        s = lax.rem(p, 2)
        lanes0 = span(p * 128, 128)

        @pl.when(second == 0)
        def _():
            pl.when(p + 1 < pairs)(lambda: start(heads_load(p + 1)))
            wait(heads_load(p))
            key_sums[...] = jnp.zeros_like(key_sums)
            value_sums[...] = jnp.zeros_like(value_sums)

        def window(begin, low, end):
            bar = barred(starts_ref[begin:end], begin, low, end)
            q2, k2, v2 = heads[s, 0, begin:end], heads[s, 1, low:end], heads[s, 2, low:end]
            g2, a2 = att_grad[begin:end, lanes0], att[begin:end, lanes0]
            outs, dks, dvs = [], [], []
            for h in range(2):
                lanes = slice(h * HEAD, (h + 1) * HEAD)
                q, k, v, g = q2[:, lanes], k2[:, lanes], v2[:, lanes], g2[:, lanes]
                weights = jnp.exp(nt(q, k) + bar - head_logs[s, begin:end, h : h + 1])
                dvs.append(tn(weights.astype(BF), g))
                inside = jnp.sum(g.astype(F32) * a2[:, lanes].astype(F32), axis=1, keepdims=True)
                grads = (weights * (nt(g, v) - inside)).astype(BF)
                outs.append(jnp.dot(grads, k, preferred_element_type=F32))
                dks.append(tn(grads, q))
            table = (one_ref[begin:end], -ahead_ref[begin:end], -behind_ref[begin:end])
            dq = turned(jnp.concatenate(outs, axis=1) * HEAD ** (-0.5), table).astype(BF)
            joint[begin:end, lanes0] = dq
            bias_sums[0:1, lanes0] = bias_sums[0:1, lanes0] + jnp.sum(dq.astype(F32), axis=0, keepdims=True)
            key_sums[low:end] += jnp.concatenate(dks, axis=1)
            value_sums[low:end] += jnp.concatenate(dvs, axis=1)

        spans = list(windows(length))
        middle = len(spans) // 2

        @pl.when(second == 0)
        def _():
            for one in spans[:middle]:
                window(*one)

        @pl.when(second == 1)
        def _():
            for one in spans[middle:]:
                window(*one)
            table = (one_ref[...], -ahead_ref[...], -behind_ref[...])
            dk = turned(key_sums[...], table).astype(BF)
            dv = value_sums[...].astype(BF)
            for k, v in ((1, dk), (2, dv)):
                joint[:, span(k * units + p * 128, 128)] = v
                bias_sums[k : k + 1, lanes0] = jnp.sum(v.astype(F32), axis=0, keepdims=True)

    def grad_copies(i):
        at = span(i * chunk, chunk)
        n = 2 + 8 * chunks + 2 * i
        return (
            pltpu.make_async_remote_copy(
                src_ref=grad_rows.at[at, hi],
                dst_ref=grad_got.at[at],
                send_sem=gather_sem.at[n],
                recv_sem=gather_sem.at[n + 1],
                device_id=x_peer,
                device_id_type=MESH,
            ),
            local_copy(10 + i, grad_rows.at[at, lo], grad_own.at[at]),
        )

    def norm_one_task(i):
        pl.when(i == 0)(lambda: load_inputs.wait())
        at = span(i * chunk, chunk)
        grads = acc_rows[at]
        grad, terms = norm_rows(own[at].astype(F32), at, grads, params_ref[0:1])
        norm_sums[0:1] = norm_sums[0:1] + jnp.sum(terms, axis=0, keepdims=True)
        norm_sums[1:2] = norm_sums[1:2] + jnp.sum(grads, axis=0, keepdims=True)
        grad_rows[at] = grad_rows[at] + grad
        start(grad_copies(i))

    def small_copy(n, peer, cols=None):
        src, dst = small_src.at[n], small_in.at[n]
        if cols is not None:
            src, dst = src.at[:, cols], dst.at[:, cols]
        return pltpu.make_async_remote_copy(
            src_ref=src,
            dst_ref=dst,
            send_sem=small_sem.at[n],
            recv_sem=small_sem.at[8 + n],
            device_id=peer,
            device_id_type=MESH,
        )

    def small_hop(n, peer, step_peer):
        small_copy(n, peer).wait_recv()
        small_src[n + 1] = small_src[n] + small_in[n]
        small_copy(n + 1, step_peer).start()

    first_cols = pl.ds(0, half + units)

    def small_task(i):
        @pl.when(i == 0)
        def _():
            small_src[0, :, :half] = norm_sums[:, half:]
            small_src[0, :, half : half + units] = bias_sums[...]
            small_copy(0, x_peer, first_cols).start()

        @pl.when(i == 1)
        def _():
            small_copy(0, x_peer, first_cols).wait_recv()
            small_src[1, :, :half] = norm_sums[:, :half] + small_in[0, :, :half]
            small_copy(1, c_peer, lo).start()

        @pl.when(i == 2)
        def _():
            small_copy(1, c_peer, lo).wait_recv()
            small_src[2, :, :half] = small_src[1, :, :half] + small_in[1, :, :half]
            small_src[2, :, half : half + units] = bias_sums[...]
            small_src[2, :, half + units :] = small_in[0, :, half : half + units]
            small_copy(2, y_peer).start()

        @pl.when(i == 3)
        def _():
            small_hop(2, y_peer, e_peer)

        @pl.when(i == 4)
        def _():
            small_copy(3, e_peer).wait_recv()
            small_src[4] = small_src[3] + small_in[3]
            pl.when(mid)(lambda: small_copy(4, m_peer).start())

        @pl.when((i == 5) & mid)
        def _():
            small_hop(4, m_peer, e_peer)

        @pl.when(i == 6)
        def _():
            @pl.when(mid)
            def _():
                small_out[...] = small_src[5]
                small_copy(4, m_peer).wait_send()
                small_copy(5, e_peer).wait_send()

            @pl.when(outer)
            def _():
                small_copy(5, e_peer).wait_recv()
                small_out[...] = small_in[5]

            for n, cols in ((0, first_cols), (1, lo), (2, None), (3, None)):
                small_copy(n, x_peer, cols).wait_send()

    norm_sums[...] = jnp.zeros_like(norm_sums)
    bias_sums[...] = jnp.zeros_like(bias_sums)
    gates = hidden // 128
    at_two = max(gates, pieces + 3)
    at_norm = at_two + pieces + 3
    at_att = at_norm + chunks // 2 + 3
    at_heads = at_att + 2
    at_one = at_heads + 2 * pairs
    at_last = at_one + pieces + 3

    def tasks(t):
        within(t, 0, gates, gate_task)
        summed(t, 0, 0, feed_product, down_columns_load)
        within(t, at_two, 1, result_task)
        pl.when(t == at_two - 1)(lambda: start(gate_load(0)))
        summed(t, at_two, pieces, act_two_product, gate_load)

        def two(task):
            def both(i):
                task(2 * i)
                task(2 * i + 1)

            return both

        within(t, at_norm + 3, chunks // 2, two(gathered_task))
        within(t, at_norm + 2, chunks // 2, two(forward_task))
        within(t, at_norm, chunks // 2, two(norm_two_task))

        @pl.when(t == at_att)
        def _():
            load_wo.wait()
            load_att.wait()
            load_inputs.start()
            start(heads_load(0))

        within(t, at_att, 2, att_grad_task)
        within(t, at_heads, 2 * pairs, attention_task)
        pl.when(t == at_one - 1)(lambda: start(qkv_load(0)))
        summed(t, at_one, 2 * pieces, act_one_product, qkv_load)
        within(t, at_last, chunks // 2, two(norm_one_task))
        within(t, at_last + chunks // 2, 7, small_task)

    def body(step, carry):
        t = step - LEAD

        def free_out(u):
            e_out(u).wait_send()
            g_mid(u).wait_send()
            keep_own(u, full.at[short(u)]).wait()

        def free_far(u):
            g_out(u).wait_send()
            keep_own(u, e_dst.at[slot(u)]).wait()

        def free_got(u):
            f_out(u).wait_send()
            keep_got(u).wait()

        stage(step - 2, lambda u: x_copy(u).wait_send())
        stage(step - 2, lambda u: y_copy(u).wait_send())
        stage(step - 3, lambda u: e_in(u).wait_send(), outer)
        stage(step - 4, lambda u: m_copy(u).wait_send(), mid)
        stage(step - 5, free_out, mid)
        stage(step - 5, free_far, outer)
        stage(step - 5, lambda u: g_mid(u).wait_recv(), mid)
        stage(step - 6, lambda u: g_out(u).wait_recv(), outer)
        stage(t - 3, lambda u: f_in(u).wait_send(), outer)
        stage(t - 4, lambda u: n_copy(u).wait_send(), mid)
        stage(t - 5, lambda u: k_copy(u).wait_send(), mid)
        stage(t - 6, lambda u: w_copy(u).wait_send(), mid)
        stage(t - 7, free_got, mid)
        stage(t - 6, lambda u: f_out(u).wait_recv(), outer)
        stage(t - 4, t2_e, mid)
        stage(t - 3, t2_d, mid)
        stage(t - 2, t2_c, mid)
        stage(t - 1, t2_b, mid)
        stage(t, t2_a)
        stage(step - 4, t1_d, outer)
        stage(step - 3, t1_c, mid)
        stage(step - 2, t1_b, mid)
        stage(step - 1, t1_a)
        stage(step, produce_far)
        stage(step, produce_own)
        tasks(step)
        return carry

    lax.fori_loop(0, max(total + 7 + LEAD, at_last + chunks // 2 + 7), body, 0)
    result_copy().wait()
    store_result.wait()
    for i in range(chunks):
        wait(grad_copies(i))


def back(
    inner,
    cot_own,
    cotangent,
    gate,
    up,
    act_two,
    attended,
    queries,
    keys,
    values,
    logs,
    starts,
    table,
    act_one,
    hidden_state,
    own_inputs,
    params,
    down_own,
    w_down,
    w_gate,
    w_out,
    w_qkv,
):
    length, width = cotangent.shape
    hidden, units = inner.shape[1], attended.shape[1]
    half, part_rows, block = width // 2, length // 2, length // 4
    area, chunks = BR * BC, block // 64
    counts = [hidden * half // area, half * 2 * hidden // area, units * half // area, half * 3 * units // area]
    bases, end = [], 0
    for blocks in counts:
        bases.append(-(-end // blocks) * blocks)
        end = bases[-1] + blocks

    def bf(*shape):
        return jax.ShapeDtypeStruct(shape, BF)

    def f32(*shape):
        return jax.ShapeDtypeStruct(shape, F32)

    outs = [
        bf(2, end, BR, BC),
        bf(block, half),
        bf(block, half),
        f32(block, half),
        f32(block, half),
        f32(8, half + 2 * units),
    ]
    any_spec, vmem_spec = pl.BlockSpec(memory_space=pl.ANY), pl.BlockSpec(memory_space=pltpu.VMEM)
    wide, thin = bf(SLOTS, BR, BC), bf(SLOTS, BR // 2, BC)
    scratch = [
        f32(8, width),
        f32(8, units),
        f32(6, 8, half + 2 * units),
        f32(6, 8, half + 2 * units),
        bf(2, BR, length),
        bf(2, length, BR),
        bf(length, max(hidden, 3 * units)),
        bf(length, width),
        bf(length, 2 * hidden),
        bf(length, units),
        bf(length, units),
        bf(2, 3, length, 128),
        f32(2, length, 2),
        f32(length, 128),
        f32(length, 128),
        bf(2, 128, width),
        bf(2, 2, length, 128),
        bf(2, hidden, BC),
        bf(2, 2, BC, max(hidden, 2 * units)),
        bf(units, width),
        bf(3, part_rows, BC),
        bf(3, part_rows, BC),
        bf(3, part_rows, BC),
        bf(4, block, BC),
        bf(4, block, BC),
        f32(block, width),
        f32(block, width),
        f32(block, width),
        bf(block, width),
        bf(block, width),
        bf(SHORT, BR, BC),
        bf(SHORT, BR, BC),
        bf(FAR_SLOTS, BR, BC),
        thin,
        bf(SHORT, BR // 2, BC),
        thin,
        bf(SHORT, BR // 2, BC),
        thin,
        bf(SHORT, BR // 2, BC),
        wide,
        bf(SHORT, BR, BC),
        thin,
        bf(SHORT, BR // 2, BC),
        thin,
        wide,
    ]
    dma = pltpu.SemaphoreType.DMA
    flops = 2 * length * width * (8 * units + 6 * hidden) + 2 * length * 640 * 5 * units
    outs = pl.pallas_call(
        functools.partial(back_kernel, bases),
        out_shape=outs,
        in_specs=[any_spec] * 11 + [vmem_spec] * 4 + [any_spec] * 3 + [vmem_spec] + [any_spec] * 5,
        out_specs=[any_spec] * 5 + [vmem_spec],
        scratch_shapes=[pltpu.VMEM(v.shape, v.dtype) for v in scratch]
        + [dma((13 + chunks,)), dma((26,)), dma((14,)), dma((2 + 10 * chunks,)), dma((16,))]
        + [dma((SEMAPHORES,))] * 22
        + [dma((SLOTS,))] * 2,
        compiler_params=pltpu.CompilerParams(
            collective_id=1, has_side_effects=True, vmem_limit_bytes=63 * 2**20
        ),
        cost_estimate=pl.CostEstimate(flops=flops, bytes_accessed=200 * 2**20, transcendentals=length * 8192),
    )(
        inner,
        cot_own,
        cotangent,
        gate,
        up,
        act_two,
        attended,
        queries,
        keys,
        values,
        logs,
        starts,
        *table,
        act_one,
        hidden_state,
        own_inputs,
        params,
        down_own,
        w_down,
        w_gate,
        w_out,
        w_qkv,
    )
    return outs[0], bases, *outs[1:]


def spread_kernel(
    bases, sums, res_own, res_got, grad_own, grad_got, gate_up_out, qkv_out, out_out, down_out, res_out, grad_out, *scratch
):
    buffers, (load_sem, store_sem, row_sem) = scratch[:-3], scratch[-3:]
    r = lax.axis_index("row")
    half, hidden = gate_up_out.shape[0], gate_up_out.shape[2] // 2
    units = out_out.shape[0] // 2
    size = BR * BC // half
    rows = BR // 2

    def span(start, count):
        return pl.ds(pl.multiple_of(start, count), count)

    def widen_pair(src, dst, s):
        def some(i, carry):
            at = span(i * 64, 64)
            for j in range(src.shape[1]):
                for first in range(0, BC, 128):
                    unit = j * BC + first
                    dst[s, at, unit // hidden, unit % hidden : unit % hidden + 128] = src[
                        s, j, at, first : first + 128
                    ].astype(F32)
            return carry

        lax.fori_loop(0, rows // 64, some, 0)

    def widen_kinds(src, dst, s):
        per = units // BC
        for j in range(src.shape[1]):
            dst[s, j // per, :, j % per * BC : (j % per + 1) * BC] = src[s, j].astype(F32)

    def widen_rows(src, dst, s):
        def some(k, carry):
            dst[s, span(k * size, size)] = src[s, k].astype(F32)
            return carry

        lax.fori_loop(0, src.shape[1], some, 0)

    block = res_own.shape[0]
    moves, places = [], []
    for n, (src, dst) in enumerate(((res_own, res_out), (grad_own, grad_out), (res_got, res_out), (grad_got, grad_out))):
        held = buffers[8 + n % 2].at[n // 2]
        side = r if n < 2 else 1 - r
        moves.append(pltpu.make_async_copy(src, held, row_sem.at[n]))
        places.append(pltpu.make_async_copy(held, dst.at[span(side * block, block)], row_sem.at[4 + n]))
    tasks = []
    for w in range(2):
        side = r if w == 0 else 1 - r
        for i in range(half // rows):
            block, at = i * rows // BR, pl.ds(i * rows % BR, rows)
            per = 2 * hidden // BC
            tasks.append(
                (
                    0,
                    widen_pair,
                    sums.at[w, pl.ds(bases[1] + block * per, per), at],
                    gate_up_out.at[pl.ds(i * rows, rows), :, span(side * hidden, hidden)],
                )
            )
    for w in range(2):
        side = r if w == 0 else 1 - r
        for q in range(half // BC):
            at = pl.ds(q * size, size)
            for n, base, out, count in ((1, bases[0], down_out, hidden), (3, bases[2], out_out, units)):
                tasks.append(
                    (
                        n,
                        widen_rows,
                        sums.at[w, pl.ds(base, count // size), at],
                        out.at[span(side * count, count), pl.ds(q * BC, BC)],
                    )
                )
        for i in range(half // rows):
            block, at = i * rows // BR, pl.ds(i * rows % BR, rows)
            per = 3 * units // BC
            tasks.append(
                (
                    2,
                    widen_kinds,
                    sums.at[w, pl.ds(bases[3] + block * per, per), at],
                    qkv_out.at[:, pl.ds(i * rows, rows), span(side * units, units)],
                )
            )

    uses, plan = [0] * 4, []
    for n, widen, src, dst in tasks:
        s = uses[n] % 4
        uses[n] += 1
        held, wide = buffers[2 * n], buffers[2 * n + 1]
        load = pltpu.make_async_copy(src, held.at[s], load_sem.at[4 * n + s])
        store = pltpu.make_async_copy(wide.at[s], dst, store_sem.at[4 * n + s])
        plan.append((n, s, widen, held, wide, load, store))
    busy = {}
    ahead = 4
    for step in plan[:ahead]:
        step[5].start()
    for copy in moves:
        copy.start()
    for i, (n, s, widen, held, wide, load, store) in enumerate(plan):
        if i == ahead:
            for copy, placing in zip(moves, places):
                copy.wait()
                placing.start()
        load.wait()
        if (n, s) in busy:
            busy.pop((n, s)).wait()
        widen(held, wide, s)
        store.start()
        busy[n, s] = store
        if i + ahead < len(plan):
            plan[i + ahead][5].start()
    for copy in list(busy.values()) + places:
        copy.wait()


def spread(sums, bases, rows_of, half, units, hidden):
    block = rows_of[0].shape[0]
    size, rows = BR * BC // half, BR // 2
    shapes = [(half, 2, 2 * hidden), (3, half, 2 * units), (2 * units, half), (2 * hidden, half)]
    pair, kinds = 2 * hidden // BC, 3 * units // BC
    buffers = [
        ((4, pair, rows, BC), BF),
        ((4, rows, 2, hidden), F32),
        ((4, hidden // size, size, BC), BF),
        ((4, hidden, BC), F32),
        ((4, kinds, rows, BC), BF),
        ((4, 3, rows, units), F32),
        ((4, units // size, size, BC), BF),
        ((4, units, BC), F32),
        ((2, block, half), BF),
        ((2, block, half), F32),
    ]
    any_spec = pl.BlockSpec(memory_space=pl.ANY)
    return pl.pallas_call(
        functools.partial(spread_kernel, bases),
        out_shape=[jax.ShapeDtypeStruct(v, F32) for v in shapes]
        + [jax.ShapeDtypeStruct((2 * block, half), BF), jax.ShapeDtypeStruct((2 * block, half), F32)],
        in_specs=[any_spec] * 5,
        out_specs=[any_spec] * 6,
        scratch_shapes=[pltpu.VMEM(*v) for v in buffers] + [pltpu.SemaphoreType.DMA((16,))] * 2
        + [pltpu.SemaphoreType.DMA((8,))],
        compiler_params=pltpu.CompilerParams(vmem_limit_bytes=56 * 2**20),
    )(sums, *rows_of)


def front_kernel(
    tokens,
    starts_ref,
    one_ref,
    ahead_ref,
    behind_ref,
    gain1_ref,
    shift1_ref,
    gain2_ref,
    shift2_ref,
    bias_ref,
    qkv_w,
    out_w,
    gate_w,
    down_w,
    cotangent,
    act_one,
    q_out,
    k_out,
    v_out,
    att_out,
    log_out,
    hid_out,
    act_two,
    gate_out,
    up_out,
    inner_out,
    wq_out,
    wo_out,
    wg_out,
    wd_out,
    cot_out,
    own_out,
    params_ref,
    tok,
    act,
    wq,
    wo,
    wg,
    gate_far,
    gate_own,
    qs,
    ks,
    vs,
    att,
    logs,
    core_in,
    row_src,
    row_in,
    own_in,
    hid,
    tile,
    send_sem,
    recv_sem,
    load_sem,
    store_sem,
):
    r, c, d = lax.axis_index("row"), lax.axis_index("col"), lax.axis_index("dp")
    y, zp = lax.rem(d, 2), lax.rem(d // 2, 2)
    length, width = tok.shape
    half = width // 2
    part, block = length // 2, length // 4
    units, hidden = qs.shape[1], wg.shape[2]
    sub = zp * 2 + y
    dy, dz = 1 - 2 * y, 2 - 4 * zp
    row_peer, col_peer = {"row": 1 - r}, {"col": 1 - c}
    near = ({"dp": d + dy}, {"dp": d + dz}, {"dp": d + dy + dz})
    level = lax.rem(d // 2, 4)
    mid = (level == 1) | (level == 2)
    line = level * 2 + y
    next_peer, last_peer = {"dp": d + 2}, {"dp": d - 2}
    mid_peer = {"dp": d + 2 - 4 * (level // 2)}

    for i, ref in enumerate((gain1_ref, shift1_ref, gain2_ref, shift2_ref)):
        params_ref[i : i + 1, :half] = ref[...]
    params_ref[4:, :half] = jnp.zeros((4, half), F32)
    barrier = pltpu.get_barrier_semaphore()
    for peer in (row_peer, col_peer) + near:
        pl.semaphore_signal(barrier, inc=1, device_id=peer, device_id_type=MESH)

    @pl.when(mid)
    def _():
        pl.semaphore_signal(barrier, inc=1, device_id=mid_peer, device_id_type=MESH)

    stores = []

    def span(start, size):
        return pl.ds(pl.multiple_of(start, size), size)

    def load(n, src, dst):
        copy = pltpu.make_async_copy(src, dst, load_sem.at[n])
        copy.start()
        return copy

    def store(src, dst):
        copy = pltpu.make_async_copy(src, dst, store_sem.at[len(stores)])
        copy.start()
        stores.append(copy)
        return copy

    def remote(n, src, dst, peer):
        return pltpu.make_async_remote_copy(
            src_ref=src,
            dst_ref=dst,
            send_sem=send_sem.at[n],
            recv_sem=recv_sem.at[n],
            device_id=peer,
            device_id_type=MESH,
        )

    mine, theirs = span(r * units, units), span((1 - r) * units, units)
    own_rows, far_rows = span(c * part, part), span((1 - c) * part, part)
    lo, hi = pl.ds(0, half), pl.ds(half, half)
    quarter, eighth = half // 4, half // 8
    down_quarter = hidden // 4

    load_tok = load(0, tokens, tok.at[own_rows, lo])
    load_q = load(1, qkv_w.at[:, :, mine], wq.at[:, lo])
    load_o = load(2, out_w.at[mine], wo.at[:, lo])
    gate_cols = span(r * hidden, hidden)

    def load_gate(i):
        return load(3 + i % 2, gate_w.at[pl.ds(i * eighth, eighth), :, gate_cols], gate_own.at[i % 2])

    gates = [load_gate(0), load_gate(1)]

    rows_sub = span(sub * quarter, quarter)
    rows_far = span(half + sub * quarter, quarter)
    q_x = remote(0, qkv_w.at[:, rows_sub, theirs], wq.at[:, rows_far], row_peer)
    q_n = [remote(1 + k, wq.at[:, rows_far], wq.at[:, rows_far], p) for k, p in enumerate(near)]
    tok_x = remote(4, tokens, tok.at[own_rows, hi], row_peer)
    tok_c = remote(5, tokens, tok.at[own_rows, lo], col_peer)
    tok_f = remote(6, tok.at[own_rows, hi], tok.at[own_rows, hi], col_peer)
    out_rows = units // 4
    out_sub = span(sub * out_rows, out_rows)
    o_x = remote(
        7, out_w.at[span((1 - r) * units + sub * out_rows, out_rows)], wo.at[out_sub, hi], row_peer
    )
    o_n = [remote(8 + k, wo.at[out_sub, hi], wo.at[out_sub, hi], p) for k, p in enumerate(near)]
    rows_line = span(line * eighth, eighth)
    g_x = remote(
        11, gate_w.at[rows_line, :, span((1 - r) * hidden, hidden)], gate_far.at[line], row_peer
    )

    def gate_copy(n, at, peer):
        place = gate_far.at[lax.rem(at + 4, 4) * 2 + y]
        return remote(29 + n, place, place, peer)

    def upward(h):
        return gate_copy(h, level - h, next_peer)

    def downward(h):
        return gate_copy(3 + h, level + h, last_peer)

    def across(n, at):
        return gate_copy(6 + n, at, near[0])

    def gate_hop(h):
        if h == 0:
            g_x.wait_recv()
            pl.when(level < 3)(lambda: upward(0).start())
            pl.when(level > 0)(lambda: downward(0).start())
            across(0, level).start()
            return

        @pl.when(level >= h)
        def _():
            upward(h - 1).wait_recv()
            if h < 3:
                pl.when(level < 3)(lambda: upward(h).start())
            across(h, level - h).start()

        @pl.when(level + h <= 3)
        def _():
            downward(h - 1).wait_recv()
            if h < 3:
                pl.when(level > 0)(lambda: downward(h).start())
            across(3 + h, level + h).start()

    def gates_across(act):
        act(across(0, level))
        for h in range(1, 4):
            pl.when(level >= h)(lambda h=h: act(across(h, level - h)))
            pl.when(level + h <= 3)(lambda h=h: act(across(3 + h, level + h)))

    def gates_sent():
        gates_across(lambda copy: copy.wait_send())
        for h in range(3):
            pl.when((level < 3) & (level >= h))(lambda h=h: upward(h).wait_send())
            pl.when((level > 0) & (level + h <= 3))(lambda h=h: downward(h).wait_send())

    def part_level(at, side):
        block_of = at * 2 + side
        part_gate(gate_far.at[block_of], span(half + block_of * eighth, eighth))

    down_sub = span(sub * down_quarter, down_quarter)
    d_x = remote(
        15,
        down_w.at[span((1 - r) * hidden + sub * down_quarter, down_quarter)],
        wd_out.at[down_sub],
        row_peer,
    )
    d_n = [
        remote(16 + k, wd_out.at[down_sub], wd_out.at[down_sub], p)
        for k, p in enumerate(near)
    ]
    c_x = remote(19, cotangent, cot_out.at[own_rows, hi], row_peer)
    c_c = remote(20, cotangent, cot_out.at[own_rows, lo], col_peer)
    c_f = remote(21, cot_out.at[own_rows, hi], cot_out.at[own_rows, hi], col_peer)
    rs_c = remote(22, act.at[far_rows], core_in, col_peer)
    rs_x = remote(23, row_src, row_in, row_peer)
    own_block = span(c * part + r * block, block)
    x_block = span(c * part + (1 - r) * block, block)
    ag_x = [
        remote(24, tok.at[own_block, lo], tok.at[own_block, hi], row_peer),
        remote(25, tok.at[own_block, hi], tok.at[own_block, lo], row_peer),
    ]
    ag_c = remote(26, tok.at[own_block], tok.at[own_block], col_peer)
    ag_f = remote(27, tok.at[x_block], tok.at[x_block], col_peer)

    p_x = remote(28, params_ref.at[:, lo], params_ref.at[:, hi], row_peer)

    def start(copies):
        for copy in copies:
            copy.start()

    def arrived(copies):
        for copy in copies:
            copy.wait_recv()

    def part_gate(ref, at):
        wg[0, at] = ref[:, 0, :]
        wg[1, at] = ref[:, 1, :]

    @pl.when(mid)
    def _():
        pl.semaphore_wait(barrier, 6)

    @pl.when(jnp.logical_not(mid))
    def _():
        pl.semaphore_wait(barrier, 5)

    p_x.start()
    q_x.start()
    tok_c.start()
    c_c.start()
    for i in range(8):
        if i == 4:
            q_x.wait_recv()
            start(q_n)
            tok_x.start()
        gates[i].wait()
        part_gate(gate_own.at[i % 2], pl.ds(i * eighth, eighth))
        if i + 2 < 8:
            gates.append(load_gate(i + 2))
    tok_x.wait_recv()
    tok_f.start()
    o_x.start()
    g_x.start()

    load_tok.wait()
    p_x.wait_recv()
    tok_c.wait_recv()

    def normed(v, at):
        mean = jnp.sum(v, axis=1, keepdims=True) / width
        spread_of = jnp.sum(v * v, axis=1, keepdims=True) / width - mean * mean
        v = (v - mean) * lax.rsqrt(spread_of + EPSILON)
        return (v * params_ref[at : at + 1] + params_ref[at + 1 : at + 2]).astype(BF)

    norm_rows = 64

    def norm_one(base):
        def body(i, carry):
            at = span(base + i * norm_rows, norm_rows)
            act[at] = normed(tok[at].astype(F32), 0)
            return carry

        lax.fori_loop(0, part // norm_rows, body, 0)

    norm_one(c * part)
    own_in[...] = tok[own_block]
    tok_f.wait_recv()
    norm_one((1 - c) * part)
    store(act, act_one)
    store(own_in, own_out)

    load_q.wait()
    arrived(q_n)
    o_x.wait_recv()
    start(o_n)
    store(wq, wq_out)
    chunk = 256

    def project(i, carry):
        at = span(i * chunk, chunk)
        rows = act[at]
        for kind, ref in enumerate((qs, ks, vs)):
            out = jnp.dot(rows, wq[kind], preferred_element_type=F32) + bias_ref[kind : kind + 1]
            if kind == 2:
                ref[at] = out.astype(BF)
                continue
            table = (one_ref[at], ahead_ref[at], behind_ref[at])
            for g in range(units // 128):
                lanes = slice(g * 128, (g + 1) * 128)
                v = turned(out[:, lanes], table).astype(BF)
                if kind == 0:
                    v = (v.astype(F32) * HEAD ** (-0.5)).astype(BF)
                ref[at, lanes] = v
        return carry

    lax.fori_loop(0, length // chunk, project, 0)
    gate_hop(0)
    d_x.start()
    for ref, out in ((qs, q_out), (ks, k_out), (vs, v_out)):
        store(ref, out)

    pairs = units // 128

    def attend(p, carry):
        @pl.when(p == pairs // 2)
        def _():
            gate_hop(1)
            c_x.start()


        lane0 = p * 128
        q2 = qs[:, span(lane0, 128)]
        k2 = ks[:, span(lane0, 128)]
        v2 = vs[:, span(lane0, 128)]
        for begin, low, end in windows(length):
            bar = barred(starts_ref[begin:end], begin, low, end)
            outs = []
            for h in range(2):
                lanes = slice(h * HEAD, (h + 1) * HEAD)
                scores = nt(q2[begin:end, lanes], k2[low:end, lanes]) + bar
                maxima = jnp.max(scores, axis=1, keepdims=True)
                shifted = jnp.exp(scores - maxima)
                totals = jnp.sum(shifted, axis=1, keepdims=True)
                got = jnp.dot(shifted.astype(BF), v2[low:end, lanes], preferred_element_type=F32)
                outs.append(got / totals)
                logs[p, begin:end, h : h + 1] = maxima + jnp.log(totals)
            out = jnp.concatenate(outs, axis=1)
            att[begin:end, span(lane0, 128)] = out.astype(BF)
        return carry

    lax.fori_loop(0, pairs, attend, 0)
    gate_hop(2)
    store(att, att_out)
    store(logs, log_out)

    load_o.wait()
    arrived(o_n)
    store(wo, wo_out)
    stores[0].wait()
    tok_f.wait_send()

    def branch(base):
        def body(i, carry):
            at = span(base + i * chunk, chunk)
            act[at] = jnp.dot(att[at], wo[...], preferred_element_type=F32).astype(BF)
            return carry

        lax.fori_loop(0, part // chunk, body, 0)

    branch((1 - c) * part)
    rs_c.start()
    branch(c * part)
    rs_c.wait_recv()
    row_src[...] = act[x_block] + core_in[span((1 - r) * block, block)]
    rs_x.start()
    gate_hop(3)
    for at in range(4):
        part_level(at, y)
    rs_x.wait_recv()
    hid_rows = 64

    def norm_two(i, carry):
        at = span(i * hid_rows, hid_rows)
        kept = act[span(c * part + r * block + i * hid_rows, hid_rows)].astype(F32)
        kept = kept + core_in[span(r * block + i * hid_rows, hid_rows)].astype(F32)
        got = row_in[at].astype(F32)
        kept = kept + jnp.concatenate([got[:, half:], got[:, :half]], axis=1)
        kept = own_in[at].astype(F32) + kept
        hid[at] = kept
        tok[span(c * part + r * block + i * hid_rows, hid_rows)] = normed(kept, 2)
        return carry

    lax.fori_loop(0, block // hid_rows, norm_two, 0)
    start(ag_x)
    ag_c.start()
    store(hid, hid_out)
    d_x.wait_recv()
    start(d_n)
    c_x.wait_recv()
    c_f.start()
    gates_across(lambda copy: copy.wait_recv())
    for at in range(4):
        part_level(at, 1 - y)
    store(wg, wg_out)

    stores_of = []
    columns = [(at, min(512, hidden - at)) for at in range(0, hidden, 512)]
    for b in range(4):
        cc = c if b % 2 == 0 else 1 - c
        rr = r if b < 2 else 1 - r
        at = span(cc * part + rr * block, block)
        if b == 1:
            ag_c.wait_recv()
        elif b == 2:
            arrived(ag_x)
            ag_f.start()
        elif b == 3:
            ag_f.wait_recv()
        s = b % 2
        for copy in stores_of[3 * (b - 2) : 3 * (b - 1)] if b >= 2 else ():
            copy.wait()
        rows = tok[at]
        for first, size in columns:
            cols = slice(first, first + size)
            gate = jnp.dot(rows, wg[0, :, cols], preferred_element_type=F32)
            up = jnp.dot(rows, wg[1, :, cols], preferred_element_type=F32)
            tile[s, 0, :, cols] = gate.astype(BF)
            tile[s, 1, :, cols] = up.astype(BF)
            tile[s, 2, :, cols] = (gate / (1.0 + jnp.exp(-gate)) * up).astype(BF)
        for k, out in enumerate((gate_out, up_out, inner_out)):
            copy = pltpu.make_async_copy(tile.at[s, k], out.at[at], load_sem.at[7 + 3 * s + k])
            copy.start()
            stores_of.append(copy)
    store(tok, act_two)
    for copy in stores_of[6:] + stores[1:]:
        copy.wait()
    arrived(d_n)
    c_c.wait_recv()
    c_f.wait_recv()
    for copy in [p_x, q_x, tok_x, tok_c, o_x, g_x, d_x, c_x, c_c, c_f, rs_c, rs_x, ag_c, ag_f] + (
        q_n + o_n + d_n + ag_x
    ):
        copy.wait_send()
    gates_sent()


def front(tokens, starts, table, params, bias, qkv_w, out_w, gate_w, down_w, cotangent):
    part, half = tokens.shape
    length, width, block = 2 * part, 2 * half, part // 2
    units, hidden = out_w.shape[0] // 2, down_w.shape[0] // 2
    any_spec, vmem_spec = pl.BlockSpec(memory_space=pl.ANY), pl.BlockSpec(memory_space=pltpu.VMEM)
    pairs = units // 128

    def bf(*shape):
        return jax.ShapeDtypeStruct(shape, BF)

    def f32(*shape):
        return jax.ShapeDtypeStruct(shape, F32)

    outs = [
        bf(length, width),
        bf(length, units),
        bf(length, units),
        bf(length, units),
        bf(length, units),
        f32(pairs, length, 2),
        f32(block, width),
        bf(length, width),
        bf(length, hidden),
        bf(length, hidden),
        bf(length, hidden),
        bf(3, width, units),
        bf(units, width),
        bf(2, width, hidden),
        bf(hidden, half),
        bf(length, width),
        bf(block, width),
        f32(8, width),
    ]
    scratch = [
        bf(length, width),
        bf(length, width),
        bf(3, width, units),
        bf(units, width),
        bf(2, width, hidden),
        bf(8, half // 8, 2, hidden),
        bf(2, half // 8, 2, hidden),
        bf(length, units),
        bf(length, units),
        bf(length, units),
        bf(length, units),
        f32(pairs, length, 2),
        bf(part, width),
        bf(block, width),
        bf(block, width),
        bf(block, width),
        f32(block, width),
        bf(2, 3, block, hidden),
    ]
    dma = pltpu.SemaphoreType.DMA
    return pl.pallas_call(
        front_kernel,
        out_shape=outs,
        in_specs=[any_spec] + [vmem_spec] * 9 + [any_spec] * 5,
        out_specs=[any_spec] * (len(outs) - 1) + [vmem_spec],
        scratch_shapes=[pltpu.VMEM(v.shape, v.dtype) for v in scratch]
        + [dma((42,)), dma((42,)), dma((13,)), dma((16,))],
        compiler_params=pltpu.CompilerParams(
            collective_id=2, has_side_effects=True, vmem_limit_bytes=63 * 2**20
        ),
        cost_estimate=pl.CostEstimate(
            flops=2 * length * width * (4 * units + 2 * hidden),
            bytes_accessed=100 * 2**20,
            transcendentals=length * 2048,
        ),
    )(tokens, starts, *table, *params, bias, qkv_w, out_w, gate_w, down_w, cotangent)


def local(
    tokens,
    segments,
    ln1_gain,
    ln1_bias,
    qkv_weight,
    qkv_bias,
    out_weight,
    ln2_gain,
    ln2_bias,
    gate_up_weight,
    down_weight,
    cotangent,
):
    place = Place()
    r, c = place.r, place.c
    ids = segments[0]
    length = ids.shape[0]
    factor = HEAD ** (-0.5)
    half = qkv_weight.shape[0]
    units = qkv_weight.shape[2] // 2
    heads = units // HEAD
    hidden = gate_up_weight.shape[2] // 2

    params = [v[None] for v in (ln1_gain, ln1_bias, ln2_gain, ln2_bias)]
    starts = first_places(ids)
    table = rotary_table(jnp.arange(length, dtype=jnp.int32)[:, None] - starts)
    bias = piece(qkv_bias, r, 2, 1)
    (
        act_one,
        queries,
        keys,
        values,
        attended,
        logs,
        hidden_state,
        act_two,
        gate,
        up,
        inner,
        w_qkv,
        w_out,
        w_gate,
        w_down,
        cot_all,
        own_inputs,
        params,
    ) = front(
        tokens,
        starts,
        table,
        params,
        bias,
        qkv_weight.transpose(1, 0, 2),
        out_weight,
        gate_up_weight,
        down_weight,
        cotangent,
    )
    if place.count == 8:
        sums, bases, result, result_far, input_grad, input_far, small = back(
            inner,
            cotangent,
            cot_all,
            gate,
            up,
            act_two,
            attended,
            queries,
            keys,
            values,
            logs,
            starts,
            table,
            act_one,
            hidden_state,
            own_inputs,
            params,
            down_weight,
            w_down,
            w_gate,
            w_out,
            w_qkv,
        )
        norms = small[:4, :half]
        bias_grad = ordered(r, small[:3, half : half + units], small[:3, half + units :], 1)
        gate_up_grad, qkv_grad, out_grad, down_grad, result, input_grad = spread(
            sums, bases, (result, result_far, input_grad, input_far), half, units, hidden
        )
        qkv_grad = qkv_grad.transpose(1, 0, 2)
    else:
        block = c * 2 + r
        w_down = jnp.concatenate([piece(down_weight, r, 2), w_down], axis=1)
        cot_all = lax.dynamic_update_slice(cot_all, cotangent, (c * (length // 2), 0))
        own_inputs = own_inputs.astype(F32)
        _, normal_two, inverse_two = norm_forward(hidden_state, params[2], params[3])
        gate, up = gate.astype(F32), up.astype(F32)

        feed = reduce_blocks(dot(inner, w_down).astype(BF), place)
        result = (hidden_state + feed).astype(BF)
        result = ordered(r, result[:, :half], swap(result[:, half:], "row"))

        grad_inner = dot_t(cot_all, w_down)
        rate = 1.0 / (1.0 + jnp.exp(-gate))
        silu = gate * rate
        grad_gate = (grad_inner * up * (rate * (1.0 + gate * (1.0 - rate)))).astype(BF)
        grad_up = (grad_inner * silu).astype(BF)
        grad_two = jnp.stack([grad_gate, grad_up])
        grad_pair = jnp.concatenate([grad_gate, grad_up], axis=1)
        grad_act_two = reduce_blocks(
            jnp.einsum("ksf,kdf->sd", grad_two, w_gate, preferred_element_type=F32).astype(BF), place
        )
        grad_norm, ln2_gain_grad, ln2_bias_grad = norm_backward(
            grad_act_two, normal_two, inverse_two, params[2]
        )
        own_cot = piece(cot_all, block, 4).astype(F32)
        grad_hidden = own_cot + grad_norm
        grad_branch = gather_blocks(grad_hidden.astype(BF), place)
        grad_attended = dot_t(grad_branch, w_out).astype(BF)
        grad_joined = attention_backward(
            queries, keys, values, grad_attended, attended, logs, starts, jnp.stack(table)
        )
        grad_joined = jnp.concatenate(grad_joined, axis=1)
        bias_grad = jnp.sum(grad_joined, axis=0, dtype=F32)
        grad_kinds = grad_joined.reshape(length, 3, units)
        grad_act_one = reduce_blocks(
            jnp.einsum("sku,kdu->sd", grad_kinds, w_qkv, preferred_element_type=F32).astype(BF), place
        )
        _, normal_one, inverse_one = norm_forward(own_inputs, params[0], params[1])
        grad_norm, ln1_gain_grad, ln1_bias_grad = norm_backward(
            grad_act_one, normal_one, inverse_one, params[0]
        )
        input_grad = grad_hidden + grad_norm
        input_grad = ordered(r, input_grad[:, :half], swap(input_grad[:, half:], "row"))

        pairs = (
            ("D", act_two, grad_pair),
            ("D", act_one, grad_joined),
            ("U", attended, grad_branch),
            ("U", inner, cot_all),
        )
        sums = []
        for kind, left, right in pairs:
            both = t_dot(left, right).astype(BF)
            axis = 0 if kind == "D" else 1
            own, sent = jnp.split(both, 2, axis)
            sums.append([lax.psum(v, "dp").astype(F32) for v in (own, swap(sent, "row"))])
        gate_up_grad = ordered(r, *[v.reshape(half, 2, hidden) for v in sums[0]], 2)
        qkv_grad = ordered(r, *[v.reshape(half, 3, units) for v in sums[1]], 2)
        out_grad = ordered(r, *sums[2])
        down_grad = ordered(r, *sums[3])

        small = jnp.stack([ln1_gain_grad, ln1_bias_grad, ln2_gain_grad, ln2_bias_grad])
        small = small[:, :half] + swap(small[:, half:], "row")
        norms = lax.psum(small, ("dp", "col"))
        bias_grad = lax.psum(bias_grad.reshape(3, units), "dp")
        bias_grad = ordered(r, bias_grad, swap(bias_grad, "row"), 1)

    return (
        result,
        input_grad,
        norms[0],
        norms[1],
        qkv_grad,
        bias_grad,
        out_grad,
        norms[2],
        norms[3],
        gate_up_grad,
        down_grad,
    )


def solution(mesh):
    in_specs = (
        P(("dp", "col"), "row"),
        P("dp", None),
        P("row"),
        P("row"),
        P("row", None, "col"),
        P(None, "col"),
        P("col", "row"),
        P("row"),
        P("row"),
        P("row", None, "col"),
        P("col", "row"),
        P(("dp", "col"), "row"),
    )
    out_specs = (
        P(("dp", "col"), "row"),
        P(("dp", "col"), "row"),
        P("row"),
        P("row"),
        P("row", None, "col"),
        P(None, "col"),
        P("col", "row"),
        P("row"),
        P("row"),
        P("row", None, "col"),
        P("col", "row"),
    )
    return jax.shard_map(local, mesh=mesh, in_specs=in_specs, out_specs=out_specs, check_vma=False)
```
